32 devices in a mesh: dp: 16 (over z, y, x), seq: 2 (over core).
Axes of the slice: x: 2, y: 2, z: 4, core: 2. Of those that a mesh axis runs over, the one named last changes fastest.
Arguments:
- layer_input: bfloat16 [16, 1024, 512], P('dp', 'seq'), may hold values from -6 to 6
- source_states: bfloat16 [16, 512, 512], P('dp', 'seq'), may hold values from -6 to 6
- source_lengths: int32 [16, 8], P('dp'), may hold values from 1 to 260, as said below
- cotangent: bfloat16 [16, 1024, 512], P('dp', 'seq'), may hold values from -6 to 6
- norm_gain: bfloat16 [3, 512], replicated, may hold values from 0.5 to 1.5
- norm_bias: bfloat16 [3, 512], replicated, may hold values from -1.25 to 1.25
- self_in: bfloat16 [512, 1536], replicated, may hold values from -0.25 to 0.25
- self_bias: bfloat16 [3, 512], replicated, may hold values from -0.625 to 0.625
- self_out: bfloat16 [512, 512], replicated, may hold values from -1.5 to 1.5
- cross_query: bfloat16 [512, 512], replicated, may hold values from -0.25 to 0.25
- cross_keyval: bfloat16 [512, 1024], replicated, may hold values from -0.25 to 0.25
- cross_bias: bfloat16 [3, 512], replicated, may hold values from -0.625 to 0.625
- cross_out: bfloat16 [512, 512], replicated, may hold values from -1.5 to 1.5
- feed_in: bfloat16 [512, 2048], replicated, may hold values from -0.25 to 0.25
- inner_bias: bfloat16 [2048], replicated, may hold values from -1.75 to 1.75
- feed_out: bfloat16 [2048, 512], replicated, may hold values from -0.125 to 0.125
- outer_bias: bfloat16 [512], replicated, may hold values from -1.75 to 1.75
Outputs:
- block_output: bfloat16 [16, 1024, 512], P('dp', 'seq')
- input_grad: bfloat16 [16, 1024, 512], P('dp', 'seq')
- source_grad: bfloat16 [16, 512, 512], P('dp', 'seq')
- grad_norm_gain: float32 [3, 512], replicated
- grad_norm_bias: float32 [3, 512], replicated
- grad_self_in: float32 [512, 1536], replicated
- grad_self_bias: float32 [3, 512], replicated
- grad_self_out: float32 [512, 512], replicated
- grad_cross_query: float32 [512, 512], replicated
- grad_cross_keyval: float32 [512, 1024], replicated
- grad_cross_bias: float32 [3, 512], replicated
- grad_cross_out: float32 [512, 512], replicated
- grad_feed_in: float32 [512, 2048], replicated
- grad_inner_bias: float32 [2048], replicated
- grad_feed_out: float32 [2048, 512], replicated
- grad_outer_bias: float32 [512], replicated
The draws below stay inside these ranges and needn't reach their ends.
Inputs may be any that keep to these rules, and one draw needn't show every extreme that they name: `source_lengths`: in each group the 8 lengths sum to 512; exactly one sentence, at a place drawn from the seed, has the largest length, 512 - 7 * max(1, 36), and its upsampled positions begin in the first block of 512 positions of its group and end in the last block.
All inputs are finite; a program needn't handle non-finite values.
Results may differ from the reference program's by a relative error of at most 0.03.
Values may be sent and summed in bfloat16 or wider, within the bound.
No kernel may reach another device: no remote copies, remote signals or barrier semaphores. Data moves between devices by JAX's collectives and lax.ppermute only.
A program may use at most 192 MiB of HBM per device.

```python
import math
import jax
import jax.numpy as jnp
from jax import lax

D = 512
HEADS = 8
HD = 64
FF = 2048
NSENT = 8
TOK_DEV = 512
BATCH = 16
POS = 1024
SRC_POS = 512


def draw_source_lengths(key, part):
    key = jax.random.fold_in(key, 7)
    rest = (NSENT - 1) * max(1, (TOK_DEV // 2 - 1) // (NSENT - 1))
    longest_len = SRC_POS - rest

    def one_group(group_key):
        place_key, cut_key = jax.random.split(group_key)
        longest = jax.random.randint(place_key, (), 0, NSENT)
        if NSENT > 2:
            cuts = jnp.sort(jax.random.permutation(cut_key, rest - 1)[:NSENT - 2] + 1)
            bounds = jnp.concatenate([jnp.zeros((1,), jnp.int32), cuts.astype(jnp.int32), jnp.full((1,), rest, jnp.int32)])
        else:
            bounds = jnp.array([0, rest], jnp.int32)
        shorter = bounds[1:] - bounds[:-1]
        order = jnp.arange(NSENT)
        index = jnp.clip(order - (order > longest).astype(order.dtype), 0, NSENT - 2)
        return jnp.where(order == longest, longest_len, shorter[index]).astype(jnp.int32)
    return jax.vmap(one_group)(jax.random.split(key, BATCH))


def block_levels(rng, dims, pieces, smallest, largest):
    def one(dim, blocks):
        heights = jax.random.uniform(jax.random.fold_in(jax.random.fold_in(rng, 6), dim), (blocks,), jnp.float32, smallest / len(pieces), largest / len(pieces))
        return jnp.repeat(jnp.exp(heights), dims[dim] // blocks).reshape((-1,) + (1,) * (len(dims) - dim - 1))

    level = one(*pieces[0])
    for cut in pieces[1:]:
        level = level * one(*cut)
    return level


def bell_draw(key, extent, deviation, reach, cuts=(), kind=jnp.bfloat16):
    values = deviation * jax.random.normal(key, extent, jnp.float32)
    if cuts:
        values = values * block_levels(key, extent, cuts, -0.22, 0.18)
    return jnp.clip(values, -reach, reach).astype(kind)


def setup_inputs(seed: int = 0) -> dict:
    seeds = jax.random.split(jax.random.key(seed), 18)
    return {
        "layer_input": bell_draw(seeds[0], (BATCH, POS, D), 1.0, 6.0, ((0, 16), (1, 2))),
        "source_states": bell_draw(seeds[1], (BATCH, SRC_POS, D), 1.0, 6.0, ((0, 16), (1, 2))),
        "source_lengths": draw_source_lengths(jax.random.fold_in(seeds[17], 71), 0),
        "cotangent": bell_draw(seeds[3], (BATCH, POS, D), 1.0, 6.0, ((0, 16), (1, 2))),
        "norm_gain": jnp.clip(1.0 + 0.1 * jax.random.normal(seeds[4], (3, D), jnp.float32), 0.5, 1.5).astype(jnp.bfloat16),
        "norm_bias": bell_draw(seeds[5], (3, D), 0.2, 1.25),
        "self_in": bell_draw(seeds[6], (D, 3 * D), D ** -0.5, 0.25),
        "self_bias": bell_draw(seeds[7], (3, D), 0.1, 0.625),
        "self_out": bell_draw(seeds[8], (D, D), (D // 32) ** -0.5, 1.5),
        "cross_query": bell_draw(seeds[9], (D, D), D ** -0.5, 0.25),
        "cross_keyval": bell_draw(seeds[10], (D, 2 * D), D ** -0.5, 0.25),
        "cross_bias": bell_draw(seeds[11], (3, D), 0.1, 0.625),
        "cross_out": bell_draw(seeds[12], (D, D), (D // 32) ** -0.5, 1.5),
        "feed_in": bell_draw(seeds[13], (D, FF), D ** -0.5, 0.25),
        "inner_bias": bell_draw(seeds[14], (FF,), 0.3, 1.75),
        "feed_out": bell_draw(seeds[15], (FF, D), FF ** -0.5, 0.125),
        "outer_bias": bell_draw(seeds[16], (D,), 0.3, 1.75),
    }


highest = lax.Precision.HIGHEST
eps = 1e-05
neg_big = -1e+30

@jax.custom_vjp
def low(v):
    return lax.optimization_barrier(v.astype(jnp.bfloat16)).astype(jnp.float32)

@jax.custom_vjp
def low_back(v):
    return v

def low_keep(v):
    return (low(v), None)

def low_pass(kept, grad):
    return (grad,)

def back_keep(v):
    return (v, None)

def back_low(kept, grad):
    return (low(grad),)
low.defvjp(low_keep, low_pass)
low_back.defvjp(back_keep, back_low)

def segment_ids(lengths, count):
    ends = jnp.cumsum(lengths).astype(jnp.int32)
    places = jnp.arange(count, dtype=jnp.int32)
    return lax.optimization_barrier(jnp.sum((places[:, None] >= ends[None, :]).astype(jnp.int32), axis=1)).astype(jnp.int32)

def layer_norm(values, gain, shift):
    center = values - lax.optimization_barrier(jnp.mean(values, axis=-1, keepdims=True))
    spread = lax.optimization_barrier(jnp.mean(center * center, axis=-1, keepdims=True))
    return center * lax.rsqrt(spread + eps) * gain + shift

def matmul(left, right):
    return jnp.dot(left, right, precision=highest)

def attention(queries, keys, values, seg_q, seg_k):
    count = queries.shape[0]
    block = math.gcd(count, 512)
    heads_k = keys.reshape(keys.shape[0], HEADS, HD)
    heads_v = values.reshape(values.shape[0], HEADS, HD)

    def one_block(items):
        block_q, block_seg = items
        raw = jnp.einsum('qhd,khd->qhk', block_q, heads_k, precision=highest) * HD ** (-0.5)
        mask = (block_seg[:, None] == seg_k[None, :])[:, None, :]
        scores = jnp.where(mask, low_back(raw), neg_big)
        shifted = scores - lax.optimization_barrier(jnp.max(scores, axis=-1, keepdims=True))
        expo = jnp.exp(shifted)
        probs = expo / lax.optimization_barrier(jnp.sum(expo, axis=-1, keepdims=True))
        mixed = jnp.einsum('qhk,khd->qhd', low(probs), heads_v, precision=highest)
        return mixed.reshape(block, HEADS * HD)
    blocks_q = queries.reshape(count // block, block, HEADS, HD)
    blocks_seg = seg_q.reshape(count // block, block)
    mixed = lax.map(jax.checkpoint(one_block), (blocks_q, blocks_seg))
    return mixed.reshape(count, HEADS * HD)

def group_layer(inputs, source, seg_target, seg_source, params):
    norm_gain, norm_bias, self_in, self_bias, self_out, cross_query, cross_keyval, cross_bias, cross_out, feed_in, inner_bias, feed_out, outer_bias = params
    width = inputs.shape[1]
    zeros = jnp.zeros((width,), jnp.float32)
    normed_one = low(layer_norm(inputs, norm_gain[0], norm_bias[0]))
    projected = low_back(low(matmul(normed_one, self_in) + jnp.concatenate([self_bias[0], zeros, self_bias[1]])))
    mixed = low_back(low(attention(projected[:, :width], projected[:, width:2 * width], projected[:, 2 * width:], seg_target, seg_target)))
    after_one = inputs + low_back(matmul(mixed, self_out) + self_bias[2])
    normed_two = low(layer_norm(after_one, norm_gain[1], norm_bias[1]))
    queries_two = low_back(low(matmul(normed_two, cross_query) + cross_bias[0]))
    cross_kv = low(matmul(source, cross_keyval) + jnp.concatenate([zeros, cross_bias[1]]))
    mixed_two = low_back(low(attention(queries_two, cross_kv[:, :width], cross_kv[:, width:], seg_target, seg_source)))
    after_two = after_one + low_back(matmul(mixed_two, cross_out) + cross_bias[2])
    normed_three = low(layer_norm(after_two, norm_gain[2], norm_bias[2]))
    hidden = low_back(matmul(normed_three, feed_in) + inner_bias)
    acted = low(jax.nn.gelu(hidden, approximate=True))
    return after_two + low_back(matmul(acted, feed_out) + outer_bias)

def reference(layer_input, source_states, source_lengths, cotangent, norm_gain, norm_bias, self_in, self_bias, self_out, cross_query, cross_keyval, cross_bias, cross_out, feed_in, inner_bias, feed_out, outer_bias):
    params = tuple((item.astype(jnp.float32) for item in (norm_gain, norm_bias, self_in, self_bias, self_out, cross_query, cross_keyval, cross_bias, cross_out, feed_in, inner_bias, feed_out, outer_bias)))
    seg_target = jax.vmap(lambda lengths_row: segment_ids(2 * lengths_row, POS))(source_lengths)
    seg_source = jax.vmap(lambda lengths_row: segment_ids(lengths_row, SRC_POS))(source_lengths)

    def forward(inputs, source, weights):
        return lax.map(lambda group_items: group_layer(group_items[0], group_items[1], group_items[2], group_items[3], weights), (inputs, source, seg_target, seg_source))
    output, pullback = jax.vjp(forward, layer_input.astype(jnp.float32), source_states.astype(jnp.float32), params)
    grad_input, grad_source, grads = pullback(cotangent.astype(jnp.float32))
    return (output.astype(jnp.bfloat16), grad_input.astype(jnp.bfloat16), grad_source.astype(jnp.bfloat16), grads[0], grads[1], grads[2], grads[3], grads[4], grads[5], grads[6], grads[7], grads[8], grads[9], grads[10], grads[11], grads[12])
```

```python
import functools
import jax
import jax.numpy as jnp
from jax import lax
from jax.experimental import pallas as pl
from jax.experimental.pallas import tpu as pltpu
from jax.sharding import PartitionSpec as P

HEADS = 8
HD = 64
PAIR = 2 * HD
eps = 1e-05
far = -1e30
BF = jnp.bfloat16
F32 = jnp.float32


def mm(left, right):
    return lax.dot_general(left, right, (((1,), (0,)), ((), ())), preferred_element_type=F32)


def mm_t(left, right):
    return lax.dot_general(left, right, (((1,), (1,)), ((), ())), preferred_element_type=F32)


def t_mm(left, right):
    return lax.dot_general(left, right, (((0,), (0,)), ((), ())), preferred_element_type=F32)


def norm_parts(values):
    center = values - jnp.mean(values, axis=-1, keepdims=True)
    spread = jnp.mean(center * center, axis=-1, keepdims=True)
    rate = lax.rsqrt(spread + eps)
    return center * rate, rate


def norm_rows(values, gain, shift):
    return norm_parts(values)[0] * gain + shift


def norm_back(values, gain, grad):
    xhat, rate = norm_parts(values)
    e = grad * gain
    back = rate * (
        e - jnp.mean(e, axis=-1, keepdims=True) - xhat * jnp.mean(e * xhat, axis=-1, keepdims=True)
    )
    return back, grad * xhat


def sentence_lanes(lengths, factor, shape):
    lane = lax.broadcasted_iota(jnp.int32, shape, 1) % HD
    begin = jnp.zeros(shape, jnp.int32)
    end = jnp.zeros(shape, jnp.int32)
    total = jnp.int32(0)
    for n in range(lengths.shape[1]):
        after = total + factor * lengths[0, n]
        begin = jnp.where(lane == n, total, begin)
        end = jnp.where(lane == n, after, end)
        total = after
    return begin, end


def sentence_hits(lengths, factor, first, rows):
    begin, end = sentence_lanes(lengths, factor, (1, PAIR))
    place = lax.broadcasted_iota(jnp.int32, (rows, PAIR), 0) + first
    return jnp.where((place >= begin) & (place < end), 1.0, 0.0)


def sentence_far(lengths, hits):
    lane = lax.broadcasted_iota(jnp.int32, hits.shape, 1) % HD
    return jnp.where(lane < lengths.shape[1], (1.0 - hits) * far, 0.0)


def gelu_parts(v):
    c = 0.7978845608028654
    square = v * v
    t = jnp.tanh(c * (v + 0.044715 * (square * v)))
    half = 0.5 * (1.0 + t)
    slope = half + (0.5 * v) * (1.0 - t * t) * (c * (1.0 + 3 * 0.044715 * square))
    return v * half, slope


def attend(lengths, q_ref, k_ref, v_ref, qfar_ref, khit_ref, p_ref, p_out, sem, mixed_ref, recip_ref):
    rows = q_ref.shape[0]
    keys = k_ref.shape[0]
    qlane = lax.broadcasted_iota(jnp.int32, (rows, PAIR), 1) < HD
    klane = lax.broadcasted_iota(jnp.int32, (keys, PAIR), 1) < HD
    vrow = lax.broadcasted_iota(jnp.int32, (PAIR, keys), 0) < HD

    def one(pair, _):
        lanes = pl.ds(pl.multiple_of(pair * PAIR, PAIR), PAIR)
        qp = q_ref[:, lanes]
        kp = k_ref[:, lanes]
        vpt = v_ref[:, lanes].T
        outs = []
        for h in (0, 1):
            qe = jnp.where(qlane if h == 0 else ~qlane, qp, qfar_ref[...])
            ke = jnp.where(klane if h == 0 else ~klane, kp, khit_ref[...])
            st = mm_t(ke, qe)
            top = jnp.max(st, axis=0, keepdims=True)
            p = jnp.exp(st - top).astype(BF)

            copy = pltpu.make_async_copy(p_ref.at[h], p_out.at[2 * pair + h], sem.at[h])

            @pl.when(pair > 0)
            def _():
                copy.wait()

            p_ref[h] = p
            copy.start()
            ve = jnp.where(vrow if h == 0 else ~vrow, vpt, jnp.ones_like(vpt))
            outs.append(mm(ve, p).T)
        value = jnp.where(qlane, outs[0], outs[1])
        total = pltpu.roll(jnp.where(qlane, outs[1], outs[0]), HD, 1)
        recip = 1.0 / total
        mixed_ref[:, lanes] = (value * recip).astype(BF)
        recip_ref[:, lanes] = recip
        return 0

    lax.fori_loop(0, HEADS // 2, one, 0)
    for h in (0, 1):
        pltpu.make_async_copy(p_ref.at[h], p_out.at[0], sem.at[h]).wait()


def forward_kernel(
    ways,
    len_ref, x_ref, xp_ref, src_ref, srcp_ref, ct_ref,
    gain_ref, shift_ref, sbias_ref, cbias_ref, ibias_ref, obias_ref,
    w_in_h, w_so_h, w_cq_h, w_ckv_h, w_co_h, w_f1_h, w_f2_h,
    y_ref, gkeep_out, gsend_out, two_out, n1_out, n2_out, q_out, k_out, v_out, cq_out, ck_out, cv_out,
    p_out, cp_out, recip_out, crecip_out, mixed_out, cmixed_out, one_out, small_out,
    w_in, w_so, w_cq, w_ckv, w_co, w_f1, w_f2,
    n1, q, k, v, qfar, khit, p_buf, mixed, recip, one, n2, cq, ck, cv, shit, cp_buf, cmixed, crecip,
    after, n3, n3t, ctt, acc, dn3, gbuf, small, gib,
    srcb, w_sem, p_sem, o_sem, g_sem, x_sem,
):
    rows, width = x_ref.shape
    me = lax.axis_index("seq")
    weights = [(w_in_h, w_in), (w_so_h, w_so), (w_cq_h, w_cq), (w_ckv_h, w_ckv), (w_co_h, w_co), (w_f1_h, w_f1), (w_f2_h, w_f2)]
    loads = [pltpu.make_async_copy(a, b, w_sem.at[i]) for i, (a, b) in enumerate(weights)]
    src_rows = src_ref.shape[0]

    def peers(b):
        return (
            pltpu.make_async_copy(xp_ref.at[pl.ds((b - 1) * rows, rows)], n3, x_sem.at[0]),
            pltpu.make_async_copy(srcp_ref.at[pl.ds((b - 1) * src_rows, src_rows)], srcb, x_sem.at[1]),
        )

    loads[0].start()
    for load in peers(1):
        load.start()
    for load in loads[1:]:
        load.start()
    gain = gain_ref[...].astype(F32)
    shift = shift_ref[...].astype(F32)
    sbias = sbias_ref[...].astype(F32)
    cbias = cbias_ref[...].astype(F32)
    stores = []

    def store(src, dst):
        copy = pltpu.make_async_copy(src, dst, o_sem.at[len(stores)])
        copy.start()
        stores.append(copy)

    chunk = 128
    for r in range(0, rows, chunk):
        n1[r:r + chunk] = norm_rows(x_ref[r:r + chunk].astype(F32), gain[0:1], shift[0:1]).astype(BF)
    store(n1, n1_out)
    for b in range(ways):
        at = lax.rem(me + b, ways)
        khit[b * rows:(b + 1) * rows] = sentence_hits(len_ref, 2, at * rows, rows).astype(BF)
        shit[b * src_rows:(b + 1) * src_rows] = sentence_hits(len_ref, 1, at * src_rows, src_rows).astype(BF)
    qfar[...] = sentence_far(len_ref, khit[0:rows].astype(F32)).astype(BF)

    loads[0].wait()
    q[...] = ((mm(n1[...], w_in[:, 0:width]) + sbias[0:1]) * HD ** -0.5).astype(BF)
    for b in range(ways):
        at = slice(b * rows, (b + 1) * rows)
        rowed = n1
        if b > 0:
            rowed = n3
            peers(b)[0].wait()
            for r in range(0, rows, chunk):
                block = n3[r:r + chunk].astype(F32)
                n3[r:r + chunk] = norm_rows(block, gain[0:1], shift[0:1]).astype(BF)
        k[at] = mm(rowed[...], w_in[:, width:2 * width]).astype(BF)
        v[at] = (mm(rowed[...], w_in[:, 2 * width:]) + sbias[1:2]).astype(BF)
        if 0 < b < ways - 1:
            peers(b + 1)[0].start()
    store(q, q_out)
    store(k, k_out)
    store(v, v_out)
    attend(len_ref, q, k, v, qfar, khit, p_buf, p_out, p_sem, mixed, recip)
    store(recip, recip_out)
    store(mixed, mixed_out)

    loads[1].wait()
    one[...] = x_ref[...].astype(F32) + mm(mixed[...], w_so[...]) + sbias[2:3]
    for r in range(0, rows, chunk):
        n2[r:r + chunk] = norm_rows(one[r:r + chunk], gain[1:2], shift[1:2]).astype(BF)
    store(one, one_out)
    store(n2, n2_out)
    loads[2].wait()
    cq[...] = ((mm(n2[...], w_cq[...]) + cbias[0:1]) * HD ** -0.5).astype(BF)
    loads[3].wait()
    for b in range(ways):
        if b > 0:
            peers(b)[1].wait()
        source = src_ref[...] if b == 0 else srcb[...]
        at = slice(b * src_rows, (b + 1) * src_rows)
        ck[at] = mm(source, w_ckv[:, 0:width]).astype(BF)
        cv[at] = (mm(source, w_ckv[:, width:]) + cbias[1:2]).astype(BF)
        if 0 < b < ways - 1:
            peers(b + 1)[1].start()
    store(cq, cq_out)
    store(ck, ck_out)
    store(cv, cv_out)
    attend(len_ref, cq, ck, cv, qfar, shit, cp_buf, cp_out, p_sem, cmixed, crecip)
    store(crecip, crecip_out)
    store(cmixed, cmixed_out)

    loads[4].wait()
    after[...] = one[...] + mm(cmixed[...], w_co[...]) + cbias[2:3]
    for r in range(0, rows, chunk):
        n3[r:r + chunk] = norm_rows(after[r:r + chunk], gain[2:3], shift[2:3]).astype(BF)
    n3t[...] = n3[...].T
    acc[...] = after[...] + obias_ref[...].astype(F32)
    dn3[...] = jnp.zeros_like(dn3)
    small[...] = jnp.zeros_like(small)
    loads[5].wait()
    loads[6].wait()
    cols = width
    halves = ((gsend_out, 1 - lax.rem(me, 2)), (gkeep_out, lax.rem(me, 2)))
    steps = w_f1.shape[1] // cols // 2
    for turn, (gout, half) in enumerate(halves):

        def step(jj, _, gout=gout, half=half, turn=turn):
            j = half * steps + jj
            at = pl.ds(pl.multiple_of(j * cols, cols), cols)
            hidden = mm(n3[...], w_f1[:, at]) + ibias_ref[:, at].astype(F32)
            acted, slope = gelu_parts(hidden)
            acted = acted.astype(BF)
            acc[...] += mm(acted, w_f2[at])
            gh = mm_t(ct_ref[...], w_f2[at]) * slope
            gh = gh.astype(BF)
            gib[:, at] = jnp.sum(gh.astype(F32), axis=0, keepdims=True)
            dn3[...] += mm_t(gh, w_f1[:, at])
            copies = [
                pltpu.make_async_copy(gbuf.at[i], gout.at[pl.ds(jj * 2 * width + i * width, width)], g_sem.at[i])
                for i in (0, 1)
            ]

            def clear():
                for copy in copies:
                    copy.wait()

            if turn == 0:
                pl.when(jj > 0)(clear)
            else:
                clear()
            gbuf[0] = mm(n3t[...], gh).astype(BF)
            copies[0].start()
            gbuf[1] = t_mm(acted, ct_ref[...]).astype(BF)
            copies[1].start()
            return 0

        lax.fori_loop(0, steps, step, 0)
    y_ref[...] = acc[...].astype(BF)
    gain_grad = jnp.zeros((1, width), F32)
    shift_grad = jnp.zeros((1, width), F32)
    outer_grad = jnp.zeros((1, width), F32)
    for r in range(0, rows, chunk):
        at = slice(r, r + chunk)
        grad = dn3[at]
        back, rowed = norm_back(after[at], gain[2:3], grad)
        ct = ct_ref[at].astype(F32)
        acc[at] = ct + back
        gain_grad += jnp.sum(rowed, axis=0, keepdims=True)
        shift_grad += jnp.sum(grad, axis=0, keepdims=True)
        outer_grad += jnp.sum(ct, axis=0, keepdims=True)
    store(acc, two_out)
    for j in range(w_f1.shape[1] // width):
        small[j:j + 1] = gib[:, j * width:(j + 1) * width]
    small[8:9] = gain_grad
    small[9:10] = shift_grad
    small[10:11] = outer_grad
    small_out[...] = small[...]
    for i in (0, 1):
        pltpu.make_async_copy(gbuf.at[i], gkeep_out.at[pl.ds(0, width)], g_sem.at[i]).wait()
    for copy in stores:
        copy.wait()


def forward_call(ways, len_, x, xp, src, srcp, ct, gains, shifts, sbias, cbias, ibias, obias, weights):
    rows, width = x.shape
    srows = src.shape[0]
    nk, ns = ways * rows, ways * srows
    ff = weights[5].shape[1]
    any_ = pl.BlockSpec(memory_space=pl.ANY)
    vm = pl.BlockSpec(memory_space=pltpu.VMEM)
    sm = pl.BlockSpec(memory_space=pltpu.SMEM)
    S = jax.ShapeDtypeStruct
    outs = [
        (S((rows, width), BF), vm),
        (S((ff, width), BF), any_), (S((ff, width), BF), any_),
        (S((rows, width), F32), any_),
        (S((rows, width), BF), any_), (S((rows, width), BF), any_),
        (S((rows, width), BF), any_), (S((nk, width), BF), any_), (S((nk, width), BF), any_),
        (S((rows, width), BF), any_), (S((ns, width), BF), any_), (S((ns, width), BF), any_),
        (S((HEADS, nk, rows), BF), any_), (S((HEADS, ns, rows), BF), any_),
        (S((rows, width), F32), any_), (S((rows, width), F32), any_),
        (S((rows, width), BF), any_), (S((rows, width), BF), any_),
        (S((rows, width), F32), any_),
        (S((16, width), F32), vm),
    ]
    V = pltpu.VMEM
    rw = (rows, width)
    scratch = [V(w.shape, BF) for w in weights] + [
        V(rw, BF), V(rw, BF), V((nk, width), BF), V((nk, width), BF),
        V((rows, PAIR), BF), V((nk, PAIR), BF), V((2, nk, rows), BF), V(rw, BF), V(rw, F32),
        V(rw, F32), V(rw, BF), V(rw, BF), V((ns, width), BF), V((ns, width), BF), V((ns, PAIR), BF), V((2, ns, rows), BF),
        V(rw, BF), V(rw, F32),
        V(rw, F32), V(rw, BF), V((width, rows), BF), V((width, rows), BF), V(rw, F32), V(rw, F32),
        V((2, width, width), BF), V((16, width), F32), V((1, ff), F32), V((srows, width), BF),
        pltpu.SemaphoreType.DMA((7,)), pltpu.SemaphoreType.DMA((2,)), pltpu.SemaphoreType.DMA((16,)), pltpu.SemaphoreType.DMA((2,)), pltpu.SemaphoreType.DMA((2,)),
    ]
    return pl.pallas_call(
        functools.partial(forward_kernel, ways),
        out_shape=[o[0] for o in outs],
        in_specs=[sm, vm, any_, vm, any_, vm] + [vm] * 6 + [any_] * 7,
        out_specs=[o[1] for o in outs],
        scratch_shapes=scratch,
        compiler_params=pltpu.CompilerParams(vmem_limit_bytes=60 * 2**20),
        name="forward",
    )(len_, x, xp, src, srcp, ct, gains, shifts, sbias, cbias, ibias, obias, *weights)


def attend_back(q_ref, k_ref, v_ref, gm_ref, recip_ref, mixed_ref, p_hbm, p_ref, sem, dq_ref, dk_ref, dv_ref):
    rows = q_ref.shape[0]
    keys = k_ref.shape[0]
    qlane = lax.broadcasted_iota(jnp.int32, (rows, PAIR), 1)
    klane = lax.broadcasted_iota(jnp.int32, (keys, PAIR), 1)

    def fetch(pair, slot):
        return pltpu.make_async_copy(p_hbm.at[pl.ds(2 * pair, 2)], p_ref.at[slot], sem.at[slot])

    fetch(0, 0).start()

    def one(pair, _):
        slot = lax.rem(pair, 2)

        @pl.when(pair + 1 < HEADS // 2)
        def _():
            fetch(pair + 1, 1 - slot).start()

        lanes = pl.ds(pl.multiple_of(pair * PAIR, PAIR), PAIR)
        qp = q_ref[:, lanes]
        kp = k_ref[:, lanes]
        vp = v_ref[:, lanes]
        kpt = kp.T
        dop = (gm_ref[:, lanes].astype(F32) * recip_ref[:, lanes]).astype(BF)
        prod = dop.astype(F32) * mixed_ref[:, lanes].astype(F32)
        fetch(pair, slot).wait()
        dqs, dks, dvs = [], [], []
        for h in (0, 1):
            inside = (qlane < HD) if h == 0 else (qlane >= HD)
            kinside = (klane < HD) if h == 0 else (klane >= HD)
            spare = HD * (1 - h)
            delta = jnp.sum(jnp.where(inside, prod, 0.0), axis=1, keepdims=True)
            high = delta.astype(BF).astype(F32)
            tail = jnp.where(qlane == spare, -high, jnp.where(qlane == spare + 1, high - delta, 0.0))
            doe = jnp.where(inside, dop, tail.astype(BF))
            ones = jnp.where((klane == spare) | (klane == spare + 1), 1.0, 0.0).astype(BF)
            ve = jnp.where(kinside, vp, ones)
            dpt = mm_t(ve, doe)
            p = p_ref[slot, h]
            dst = (p.astype(F32) * dpt).astype(BF)
            dvs.append(mm(p, dop))
            dks.append(mm(dst, qp))
            dqs.append(mm(kpt, dst).T)
        dq_ref[:, lanes] = (jnp.where(qlane < HD, dqs[0], dqs[1]) * HD ** -0.5).astype(BF)
        dk_ref[:, lanes] = jnp.where(klane < HD, dks[0], dks[1]).astype(BF)
        dv_ref[:, lanes] = jnp.where(klane < HD, dvs[0], dvs[1]).astype(BF)
        return 0

    lax.fori_loop(0, HEADS // 2, one, 0)


def column_sum(block):
    return jnp.sum(block.astype(F32), axis=0, keepdims=True)


def start_all(pairs, sem):
    copies = [pltpu.make_async_copy(a, b, sem.at[i]) for i, (a, b) in enumerate(pairs)]
    for copy in copies:
        copy.start()
    return copies


def halves_of(me):
    return lax.rem(me, 2), 1 - lax.rem(me, 2)


def cross_kernel(
    gain_ref, two_h, n2_h, q_h, k_h, v_h, p_h, recip_h, cmixed_h, mixed_h, one_h, w_cq_h, w_co_h, w_so_h,
    gkeep, gsend, dkv, gm_out, oneg, small_out,
    two, n2, q, k, v, p_buf, recip, cmixed, mixed, one, w_cq, w_co, w_so, gm, dq, g, dn, p_sem, sem,
):
    rows, width = two.shape
    me = lax.axis_index("seq")
    loads = start_all(
        [(two_h, two), (cmixed_h, cmixed), (w_co_h, w_co), (recip_h, recip), (q_h, q), (k_h, k), (v_h, v), (n2_h, n2),
         (w_cq_h, w_cq), (one_h, one), (mixed_h, mixed), (w_so_h, w_so)], sem)
    gain = gain_ref[...].astype(F32)
    half = rows // 2
    keep, send = (pl.ds(pl.multiple_of(at * (width // 2), width // 2), width // 2) for at in halves_of(me))

    def put(i, value):
        g[...] = value.astype(BF)
        gkeep[i * (width // 2):(i + 1) * (width // 2)] = g[keep]
        gsend[i * (width // 2):(i + 1) * (width // 2)] = g[send]

    small_out[...] = jnp.zeros_like(small_out)
    loads[0].wait()
    branch = two[...].astype(BF)
    small_out[0:1] = column_sum(branch)
    loads[1].wait()
    put(0, t_mm(cmixed[...], branch))
    loads[2].wait()
    gm[...] = mm_t(branch, w_co[...]).astype(BF)
    for i in (3, 4, 5, 6):
        loads[i].wait()
    attend_back(q, k, v, gm, recip, cmixed, p_h, p_buf, p_sem, dq, dkv.at[:, 0:width], dkv.at[:, width:])
    small_out[1:2] = column_sum(dq[...])
    loads[7].wait()
    put(1, t_mm(n2[...], dq[...]))
    loads[8].wait()
    dn[...] = mm_t(dq[...], w_cq[...])
    loads[9].wait()
    chunk = 128
    gain_grad = jnp.zeros((1, width), F32)
    shift_grad = jnp.zeros((1, width), F32)
    for r in range(0, rows, chunk):
        at = slice(r, r + chunk)
        grad = dn[at]
        back, rowed = norm_back(one[at], gain[1:2], grad)
        oneg[at] = two[at] + back
        gain_grad += jnp.sum(rowed, axis=0, keepdims=True)
        shift_grad += jnp.sum(grad, axis=0, keepdims=True)
    small_out[2:3] = gain_grad
    small_out[3:4] = shift_grad
    branch = oneg[...].astype(BF)
    small_out[4:5] = column_sum(branch)
    loads[10].wait()
    put(2, t_mm(mixed[...], branch))
    loads[11].wait()
    gm_out[...] = mm_t(branch, w_so[...]).astype(BF)


def self_kernel(
    q_h, k_h, v_h, p_h, recip_h, mixed_h, gm_h,
    dq, dkv,
    q, k, v, p_buf, recip, mixed, gm, p_sem, sem,
):
    width = q.shape[1]
    loads = start_all([(q_h, q), (k_h, k), (v_h, v), (recip_h, recip), (mixed_h, mixed), (gm_h, gm)], sem)
    for load in loads:
        load.wait()
    attend_back(q, k, v, gm, recip, mixed, p_h, p_buf, p_sem, dq, dkv.at[:, 0:width], dkv.at[:, width:])


def source_kernel(src_ref, mine_ref, came_ref, w_ref, gkeep, gsend, sgrad, small_out, g):
    width = src_ref.shape[1]
    me = lax.axis_index("seq")
    keep, send = (pl.ds(pl.multiple_of(at * (width // 2), width // 2), width // 2) for at in halves_of(me))
    half = width // 2
    total = mine_ref[...].astype(F32)
    for b in range(came_ref.shape[0]):
        total = total + came_ref[b].astype(F32)
    small_out[...] = jnp.zeros_like(small_out)
    small_out[0:1] = jnp.sum(total[:, width:], axis=0, keepdims=True)
    total = total.astype(BF)
    sgrad[...] = mm_t(total, w_ref[...]).astype(BF)
    for i in (0, 1):
        g[...] = t_mm(src_ref[...], total[:, i * width:(i + 1) * width]).astype(BF)
        gkeep[i * half:(i + 1) * half] = g[keep]
        gsend[i * half:(i + 1) * half] = g[send]


def last_kernel(
    x_ref, gain_ref, n1_ref, dq_ref, mine_ref, came_ref, oneg_ref, w_ref, small1, small2, small3,
    gkeep, gsend, xgrad, small_out, g, dproj, n1t, dn,
):
    rows, width = x_ref.shape
    me = lax.axis_index("seq")
    half = width // 2
    keep, send = (pl.ds(pl.multiple_of(at * half, half), half) for at in halves_of(me))
    gain = gain_ref[...].astype(F32)
    dproj[:, 0:width] = dq_ref[...]
    total = mine_ref[...].astype(F32)
    for b in range(came_ref.shape[0]):
        total = total + came_ref[b].astype(F32)
    dproj[:, width:] = total.astype(BF)
    n1t[...] = n1_ref[...].T
    for i in range(3):
        g[...] = mm(n1t[...], dproj[:, i * width:(i + 1) * width]).astype(BF)
        gkeep[i * half:(i + 1) * half] = g[keep]
        gsend[i * half:(i + 1) * half] = g[send]
    dn[...] = mm_t(dproj[...], w_ref[...])
    gain_grad = jnp.zeros((1, width), F32)
    shift_grad = jnp.zeros((1, width), F32)
    chunk = 128
    for r in range(0, rows, chunk):
        at = slice(r, r + chunk)
        grad = dn[at]
        back, rowed = norm_back(x_ref[at].astype(F32), gain[0:1], grad)
        xgrad[at] = (oneg_ref[at] + back).astype(BF)
        gain_grad += jnp.sum(rowed, axis=0, keepdims=True)
        shift_grad += jnp.sum(grad, axis=0, keepdims=True)
    small_out[...] = jnp.zeros_like(small_out)
    small_out[0:1] = gain_grad
    small_out[1:2] = shift_grad
    small_out[2:3] = column_sum(dproj[:, 0:width])
    small_out[3:4] = column_sum(dproj[:, 2 * width:])
    small_out[4:5] = small3[0:1]
    small_out[8:16] = small2[...]
    small_out[16:32] = small1[...]
    for side, ref in zip(halves_of(me), (gkeep, gsend)):
        ref[3 * half:] = jnp.zeros((half // 2, width), BF)
        ref[3 * half:3 * half + 16] = small_out[pl.ds(pl.multiple_of(side * 16, 16), 16)].astype(BF)


def call(kernel, name, outs, in_specs, scratch, args):
    return pl.pallas_call(
        kernel,
        out_shape=[jax.ShapeDtypeStruct(*o) for o in outs],
        in_specs=in_specs,
        out_specs=[VM] * len(outs),
        scratch_shapes=scratch,
        compiler_params=pltpu.CompilerParams(vmem_limit_bytes=60 * 2**20),
        name=name,
    )(*args)


ANY = pl.BlockSpec(memory_space=pl.ANY)
VM = pl.BlockSpec(memory_space=pltpu.VMEM)
V = pltpu.VMEM


def cross_call(gains, two, n2, q, k, v, p, recip, cmixed, mixed, one, w_cq, w_co, w_so):
    rows, width = two.shape
    ns = k.shape[0]
    rw, ww = (rows, width), (width, width)
    outs = [((3 * width // 2, width), BF), ((3 * width // 2, width), BF), ((ns, 2 * width), BF), (rw, BF), (rw, F32), ((8, width), F32)]
    scratch = [V(rw, F32), V(rw, BF), V(rw, BF), V((ns, width), BF), V((ns, width), BF), V((2, 2, ns, rows), BF), V(rw, F32), V(rw, BF), V(rw, BF),
               V(rw, F32), V(ww, BF), V(ww, BF), V(ww, BF), V(rw, BF), V(rw, BF), V(ww, BF), V(rw, F32),
               pltpu.SemaphoreType.DMA((2,)), pltpu.SemaphoreType.DMA((12,))]
    return call(cross_kernel, "cross_back", outs, [VM] + [ANY] * 13, scratch,
                (gains, two, n2, q, k, v, p, recip, cmixed, mixed, one, w_cq, w_co, w_so))


def self_call(q, k, v, p, recip, mixed, gm):
    rows, width = q.shape
    nk = k.shape[0]
    rw = (rows, width)
    scratch = [V(rw, BF), V((nk, width), BF), V((nk, width), BF), V((2, 2, nk, rows), BF), V(rw, F32), V(rw, BF), V(rw, BF),
               pltpu.SemaphoreType.DMA((2,)), pltpu.SemaphoreType.DMA((6,))]
    return call(self_kernel, "self_back", [(rw, BF), ((nk, 2 * width), BF)], [ANY] * 7, scratch, (q, k, v, p, recip, mixed, gm))


def source_call(src, mine, came, w):
    width = src.shape[1]
    return call(source_kernel, "source_back", [((width, width), BF), ((width, width), BF), (src.shape, BF), ((8, width), F32)],
                [VM] * 4, [V((width, width), BF)], (src, mine, came, w))


def last_call(x, gains, n1, dq, mine, came, oneg, w, s1, s2, s3):
    rows, width = x.shape
    outs = [((7 * width // 4, width), BF), ((7 * width // 4, width), BF), ((rows, width), BF), ((32, width), F32)]
    scratch = [V((width, width), BF), V((rows, 3 * width), BF), V((width, rows), BF), V((rows, width), F32)]
    return call(last_kernel, "last_back", outs, [VM] * 11, scratch, (x, gains, n1, dq, mine, came, oneg, w, s1, s2, s3))


def flip(value, axis, bit):
    size = lax.axis_size(axis)
    return lax.ppermute(value, axis, [(i, i ^ bit) for i in range(size)])


def ring(value, axis, shift):
    size = lax.axis_size(axis)
    return lax.ppermute(value, axis, [(i, (i + shift) % size) for i in range(size)])


def bits_of(axis):
    size = lax.axis_size(axis)
    return [(axis, 1 << b) for b in range(size.bit_length() - 1)]


def add(left, right):
    return (left.astype(F32) + right.astype(F32)).astype(BF)


def halved(value, axis, bit):
    half = value.shape[0] // 2
    side = lax.axis_index(axis) // bit % 2
    return (
        lax.dynamic_slice_in_dim(value, side * half, half),
        lax.dynamic_slice_in_dim(value, (1 - side) * half, half),
    )


def joined(mine, came, axis, bit):
    side = lax.axis_index(axis) // bit % 2
    return jnp.where(side == 0, jnp.concatenate([mine, came]), jnp.concatenate([came, mine]))


def orders(parts):
    rest = bits_of("seq")[1:]
    dp = bits_of("dp")
    swapped = dp[1::-1] + dp[2:]
    rotated = dp[2:] + dp[:2]
    return [rest + order for order in (dp, swapped, rotated)[:parts]]


def cut(rows, parts):
    unit = lax.axis_size("dp") * lax.axis_size("seq") // 2
    pieces = rows // unit
    if parts == 1:
        sizes = [pieces]
    elif parts == 2:
        sizes = [pieces - pieces // 2, pieces // 2]
    else:
        side = pieces * 3 // 8
        sizes = [side, side, pieces - 2 * side]
    return [size * unit for size in sizes]


def sum_over_chips(value, parts):
    begin = 0
    done = []
    for size, order in zip(cut(value.shape[0], parts), orders(parts)):
        part = value[begin:begin + size]
        begin += size
        for axis, bit in order:
            mine, other = halved(part, axis, bit)
            part = add(mine, flip(other, axis, bit))
        done.append(part)
    full = []
    for part, order in zip(done, orders(parts)):
        for axis, bit in reversed(order):
            part = joined(part, flip(part, axis, bit), axis, bit)
        full.append(part)
    return jnp.concatenate(full) if parts > 1 else full[0]


def sum_everywhere(keeps, sends, parts):
    mine = [add(keep, flip(send, "seq", 1)) for keep, send in zip(keeps, sends)]
    mine = jnp.concatenate(mine) if len(mine) > 1 else mine[0]
    mine = sum_over_chips(mine, parts)
    came = flip(mine, "seq", 1)
    even = lax.axis_index("seq") % 2 == 0
    return jnp.where(even, mine, came), jnp.where(even, came, mine)


def local(
    layer_input, source_states, source_lengths, cotangent, norm_gain, norm_bias, self_in, self_bias, self_out,
    cross_query, cross_keyval, cross_bias, cross_out, feed_in, inner_bias, feed_out, outer_bias,
):
    ways = lax.axis_size("seq")
    x = layer_input[0]
    source = source_states[0]
    rows, width = x.shape
    srows = source.shape[0]
    xp = jnp.concatenate([ring(x, "seq", -b) for b in range(1, ways)])
    srcp = jnp.concatenate([ring(source, "seq", -b) for b in range(1, ways)])
    (y, gkeep, gsend, two, n1, n2, q, k, v, cq, ck, cv, p, cp, recip, crecip, mixed, cmixed, one, small1) = forward_call(
        ways, source_lengths, x, xp, source, srcp, cotangent[0], norm_gain, norm_bias, self_bias, cross_bias,
        inner_bias.reshape(1, -1), outer_bias.reshape(1, -1),
        (self_in, self_out, cross_query, cross_keyval, cross_out, feed_in, feed_out),
    )
    feed = sum_everywhere([gkeep], [gsend], 3)
    ckeep, csend, dckv, gm, oneg, small2 = cross_call(
        norm_gain, two, n2, cq, ck, cv, cp, crecip, cmixed, mixed, one, cross_query, cross_out, self_out)
    cross = sum_everywhere([ckeep], [csend], 2)
    dckv_came = jnp.stack([ring(dckv[b * srows:(b + 1) * srows], "seq", b) for b in range(1, ways)])
    dq, dkv = self_call(q, k, v, p, recip, mixed, gm)
    dkv_came = jnp.stack([ring(dkv[b * rows:(b + 1) * rows], "seq", b) for b in range(1, ways)])
    skeep, ssend, sgrad, small3 = source_call(source, dckv[:srows], dckv_came, cross_keyval)
    lkeep, lsend, xgrad, small = last_call(x, norm_gain, n1, dq, dkv[:rows], dkv_came, oneg, self_in, small1, small2, small3)
    last = sum_everywhere([skeep, lkeep], [ssend, lsend], 2)

    half = width // 2

    def block(pair, i):
        return jnp.concatenate([side[i * half:(i + 1) * half] for side in pair]).astype(F32)

    per = feed_in.shape[1] // width // 2
    firsts = [side[2 * j * width:(2 * j + 1) * width] for side in feed for j in range(per)]
    seconds = [side[(2 * j + 1) * width:(2 * j + 2) * width] for side in feed for j in range(per)]
    g_feed_in = jnp.concatenate(firsts, axis=1).astype(F32)
    g_feed_out = jnp.concatenate(seconds, axis=0).astype(F32)
    g_cross_out, g_cross_query, g_self_out = (block(cross, i) for i in range(3))
    g_keyval = jnp.concatenate([block(last, 0), block(last, 1)], axis=1)
    g_self_in = jnp.concatenate([block(last, i) for i in (2, 3, 4)], axis=1)
    low, high = (side[5 * half:5 * half + 16].astype(F32) for side in last)
    inner = jnp.concatenate([high[j] for j in range(2 * per)])
    return (
        y[None], xgrad[None], sgrad[None],
        jnp.stack([low[0], low[10], high[8]]),
        jnp.stack([low[1], low[11], high[9]]),
        g_self_in,
        jnp.stack([low[2], low[3], low[12]]),
        g_self_out, g_cross_query, g_keyval,
        jnp.stack([low[9], low[4], low[8]]),
        g_cross_out, g_feed_in, inner, g_feed_out, high[10],
    )


def solution(mesh):
    split = P("dp", "seq", None)
    in_specs = (split, split, P("dp", None), split) + (P(),) * 13
    out_specs = (split,) * 3 + (P(),) * 13
    return jax.shard_map(local, mesh=mesh, in_specs=in_specs, out_specs=out_specs, check_vma=False)
```

```python
import functools
import jax
import jax.numpy as jnp
from jax import lax
from jax.experimental import pallas as pl
from jax.experimental.pallas import tpu as pltpu
from jax.sharding import PartitionSpec as P

HEADS = 8
HD = 64
PAIR = 2 * HD
eps = 1e-05
far = -1e30
BF = jnp.bfloat16
F32 = jnp.float32


def mm(left, right):
    return lax.dot_general(left, right, (((1,), (0,)), ((), ())), preferred_element_type=F32)


def mm_t(left, right):
    return lax.dot_general(left, right, (((1,), (1,)), ((), ())), preferred_element_type=F32)


def t_mm(left, right):
    return lax.dot_general(left, right, (((0,), (0,)), ((), ())), preferred_element_type=F32)


def norm_parts(values):
    center = values - jnp.mean(values, axis=-1, keepdims=True)
    spread = jnp.mean(center * center, axis=-1, keepdims=True)
    rate = lax.rsqrt(spread + eps)
    return center * rate, rate


def norm_rows(values, gain, shift):
    return norm_parts(values)[0] * gain + shift


def norm_back(values, gain, grad):
    xhat, rate = norm_parts(values)
    e = grad * gain
    back = rate * (
        e - jnp.mean(e, axis=-1, keepdims=True) - xhat * jnp.mean(e * xhat, axis=-1, keepdims=True)
    )
    return back, grad * xhat


def sentence_lanes(lengths, factor, shape):
    lane = lax.broadcasted_iota(jnp.int32, shape, 1) % HD
    begin = jnp.zeros(shape, jnp.int32)
    end = jnp.zeros(shape, jnp.int32)
    total = jnp.int32(0)
    for n in range(lengths.shape[1]):
        after = total + factor * lengths[0, n]
        begin = jnp.where(lane == n, total, begin)
        end = jnp.where(lane == n, after, end)
        total = after
    return begin, end


def sentence_hits(lengths, factor, first, rows):
    begin, end = sentence_lanes(lengths, factor, (1, PAIR))
    place = lax.broadcasted_iota(jnp.int32, (rows, PAIR), 0) + first
    return jnp.where((place >= begin) & (place < end), 1.0, 0.0)


def sentence_far(lengths, hits):
    lane = lax.broadcasted_iota(jnp.int32, hits.shape, 1) % HD
    return jnp.where(lane < lengths.shape[1], (1.0 - hits) * far, 0.0)


def gelu_parts(v):
    c = 0.7978845608028654
    square = v * v
    t = jnp.tanh(c * (v + 0.044715 * (square * v)))
    half = 0.5 * (1.0 + t)
    slope = half + (0.5 * v) * (1.0 - t * t) * (c * (1.0 + 3 * 0.044715 * square))
    return v * half, slope


def swap_heads(width):
    row = lax.broadcasted_iota(jnp.int32, (width, width), 0) // HD
    column = lax.broadcasted_iota(jnp.int32, (width, width), 1) // HD
    return jnp.where((row != column) & (row // 2 == column // 2), 1.0, 0.0).astype(BF)


def score_bound(q_ref, k_ref, swap_ref, lift_ref):
    most = jnp.max(jnp.abs(k_ref[...]).astype(F32), axis=0, keepdims=True)
    size = (jnp.abs(q_ref[...]).astype(F32) * most).astype(BF)
    lift_ref[...] = (-1.02 * mm(size, swap_ref[...])).astype(BF)


def attend(q_ref, k_ref, v_ref, qfar_ref, khit_ref, lift_ref, p_ref, p_out, sem, mixed_ref, recip_ref):
    rows = q_ref.shape[0]
    keys = k_ref.shape[0]
    slots = p_ref.shape[0]
    qlane = lax.broadcasted_iota(jnp.int32, (rows, PAIR), 1) < HD
    klane = lax.broadcasted_iota(jnp.int32, (keys, PAIR), 1) < HD
    vrow = lax.broadcasted_iota(jnp.int32, (PAIR, keys), 0) < HD

    def copy(n, slot):
        return pltpu.make_async_copy(p_ref.at[slot], p_out.at[n], sem.at[slot])

    def one(pair, exact, reuse):
        lanes = pl.ds(pair * PAIR if isinstance(pair, int) else pl.multiple_of(pair * PAIR, PAIR), PAIR)
        qp = q_ref[:, lanes]
        kp = k_ref[:, lanes]
        vpt = v_ref[:, lanes].T
        rest = qfar_ref[...] if exact else qfar_ref[...] + lift_ref[:, lanes]
        outs = []
        for h in (0, 1):
            qe = jnp.where(qlane if h == 0 else ~qlane, qp, rest)
            ke = jnp.where(klane if h == 0 else ~klane, kp, khit_ref[...])
            st = mm_t(ke, qe)
            if exact:
                st = st - jnp.max(st, axis=0, keepdims=True)
            p = jnp.exp(st).astype(BF)
            n = 2 * pair + h
            slot = n if slots == HEADS else h
            if reuse is not None:
                pl.when(reuse)(lambda n=n, slot=slot: copy(n, slot).wait())
            p_ref[slot] = p
            copy(n, slot).start()
            ve = jnp.where(vrow if h == 0 else ~vrow, vpt, jnp.ones_like(vpt))
            outs.append(mm(ve, p).T)
        value = jnp.where(qlane, outs[0], outs[1])
        total = jnp.where(qlane, outs[1], outs[0])
        recip = 1.0 / pltpu.roll(total, HD, 1)
        mixed_ref[:, lanes] = (value * recip).astype(BF)
        recip_ref[:, lanes] = recip
        return jnp.min(total.reshape(rows // 8, 8, PAIR), axis=0)

    if slots == HEADS:
        least = one(0, False, None)
        for pair in range(1, HEADS // 2):
            least = jnp.minimum(least, one(pair, False, None))
    else:
        least = lax.fori_loop(
            0, HEADS // 2, lambda pair, low: jnp.minimum(low, one(pair, False, pair > 0)), jnp.full((8, PAIR), 1.0, F32))

    @pl.when(jnp.logical_not(jnp.min(least) > 1e-18))
    def _():
        for slot in range(slots):
            copy(slot, slot).wait()

        def again(pair, _):
            one(pair, True, pair > 0 if slots < HEADS else None)
            return 0

        lax.fori_loop(0, HEADS // 2, again, 0)


def drain(p_ref, p_out, sem):
    for slot in range(p_ref.shape[0]):
        pltpu.make_async_copy(p_ref.at[slot], p_out.at[slot], sem.at[slot]).wait()


def feed_half(half, ready, ct_ref, w1, w2, ibias_ref, n3, n3t, acc, dn3, gib, gbuf, gout, g_sem):
    width = n3.shape[1]
    steps = w2.shape[0] // width
    begun = []
    for j in range(steps):
        at = slice(j * width, (j + 1) * width)
        wide = pl.ds(pl.multiple_of((half * steps + j) * width, width), width)
        ready("w1", j)
        hidden = mm(n3[...], w1[:, at]) + ibias_ref[:, wide].astype(F32)
        acted, slope = gelu_parts(hidden)
        acted = acted.astype(BF)
        ready("w2", j)
        gh = (mm_t(ct_ref[...], w2[at]) * slope).astype(BF)
        gib[:, wide] = column_sum(gh)
        ready("n3t", j)
        for i, product in enumerate((lambda: mm(n3t[...], gh), lambda: t_mm(acted, ct_ref[...]))):
            slot = (2 * j + i) % gbuf.shape[0]
            if len(begun) >= gbuf.shape[0]:
                begun[len(begun) - gbuf.shape[0]].wait()
            gbuf[slot] = product().astype(BF)
            copy = pltpu.make_async_copy(gbuf.at[slot], gout.at[pl.ds((2 * j + i) * width, width)], g_sem.at[slot])
            copy.start()
            begun.append(copy)
        ready("acc", j)
        acc[...] += mm(acted, w2[at])
        ready("dn3", j)
        dn3[...] += mm_t(gh, w1[:, at])
    for copy in begun[-gbuf.shape[0]:]:
        copy.wait()


def column_sum(block):
    return jnp.sum(block.astype(F32), axis=0, keepdims=True)


def start_all(pairs, sem):
    copies = [pltpu.make_async_copy(a, b, sem.at[i]) for i, (a, b) in enumerate(pairs)]
    for copy in copies:
        copy.start()
    return copies


def halves_of(me):
    return lax.rem(me, 2), 1 - lax.rem(me, 2)


def columns(ref, half):
    size = ref.shape[1] // 2
    return ref.at[:, pl.ds(pl.multiple_of(half * size, size), size)]


def rows_of(ref, half):
    size = ref.shape[0] // 2
    return ref.at[pl.ds(pl.multiple_of(half * size, size), size)]


def forward_kernel(
    ways,
    len_ref, x_ref, xp_ref, src_ref, srcp_ref, ct_ref,
    gain_ref, shift_ref, sbias_ref, cbias_ref, ibias_ref, obias_ref,
    w_in_h, w_so_h, w_cq_h, w_ckv_h, w_co_h, w_f1_h, w_f2_h,
    gsend_out, acc, dn3, n3, n3t, gib, after, n1_out, n2_out, q_out, k_out, v_out, cq_out, ck_out, cv_out,
    p_out, cp_out, recip_out, crecip_out, mixed_out, cmixed_out, one_out,
    w_in, w_so, w_cq, w_ckv, w_co, w_f1, w_f2,
    n1, q, k, v, qfar, khit, p_buf, mixed, recip, one, n2, cq, ck, cv, shit, cp_buf, cmixed, crecip,
    gbuf, srcb, swap, lift, w_sem, p_sem, cp_sem, o_sem, g_sem, x_sem,
):
    rows, width = x_ref.shape
    me = lax.axis_index("seq")
    other = halves_of(me)[1]
    weights = [
        (w_in_h, w_in), (w_so_h, w_so), (w_cq_h, w_cq), (w_ckv_h, w_ckv), (w_co_h, w_co),
        (columns(w_f1_h, other), w_f1), (rows_of(w_f2_h, other), w_f2),
    ]
    loads = [pltpu.make_async_copy(a, b, w_sem.at[i]) for i, (a, b) in enumerate(weights)]
    src_rows = src_ref.shape[0]

    def peers(b):
        return (
            pltpu.make_async_copy(xp_ref.at[pl.ds((b - 1) * rows, rows)], n3, x_sem.at[0]),
            pltpu.make_async_copy(srcp_ref.at[pl.ds((b - 1) * src_rows, src_rows)], srcb, x_sem.at[1]),
        )

    loads[0].start()
    for load in peers(1):
        load.start()
    for load in loads[1:]:
        load.start()
    gain = gain_ref[...].astype(F32)
    shift = shift_ref[...].astype(F32)
    sbias = sbias_ref[...].astype(F32)
    cbias = cbias_ref[...].astype(F32)
    stores = []

    def store(src, dst):
        copy = pltpu.make_async_copy(src, dst, o_sem.at[len(stores)])
        copy.start()
        stores.append(copy)

    chunk = 128
    for r in range(0, rows, chunk):
        n1[r:r + chunk] = norm_rows(x_ref[r:r + chunk].astype(F32), gain[0:1], shift[0:1]).astype(BF)
    store(n1, n1_out.at[0:rows])
    for b in range(ways):
        at = lax.rem(me + b, ways)
        khit[b * rows:(b + 1) * rows] = sentence_hits(len_ref, 2, at * rows, rows).astype(BF)
        shit[b * src_rows:(b + 1) * src_rows] = sentence_hits(len_ref, 1, at * src_rows, src_rows).astype(BF)
    qfar[...] = sentence_far(len_ref, khit[0:rows].astype(F32)).astype(BF)

    loads[0].wait()
    q[...] = ((mm(n1[...], w_in[:, 0:width]) + sbias[0:1]) * HD ** -0.5).astype(BF)
    for b in range(ways):
        at = slice(b * rows, (b + 1) * rows)
        rowed = n1
        if b > 0:
            rowed = n3
            peers(b)[0].wait()
            for r in range(0, rows, chunk):
                block = n3[r:r + chunk].astype(F32)
                n3[r:r + chunk] = norm_rows(block, gain[0:1], shift[0:1]).astype(BF)
            nsave = pltpu.make_async_copy(n3, n1_out.at[at], x_sem.at[0])
            nsave.start()
        k[at] = mm(rowed[...], w_in[:, width:2 * width]).astype(BF)
        v[at] = (mm(rowed[...], w_in[:, 2 * width:]) + sbias[1:2]).astype(BF)
        if b > 0:
            nsave.wait()
        if 0 < b < ways - 1:
            peers(b + 1)[0].start()
    store(q, q_out)
    store(k, k_out)
    store(v, v_out)
    swap[...] = swap_heads(width)
    score_bound(q, k, swap, lift)
    attend(q, k, v, qfar, khit, lift, p_buf, p_out, p_sem, mixed, recip)
    store(recip, recip_out)
    store(mixed, mixed_out)

    loads[1].wait()
    one[...] = x_ref[...].astype(F32) + mm(mixed[...], w_so[...]) + sbias[2:3]
    for r in range(0, rows, chunk):
        n2[r:r + chunk] = norm_rows(one[r:r + chunk], gain[1:2], shift[1:2]).astype(BF)
    store(one, one_out)
    store(n2, n2_out)
    loads[2].wait()
    cq[...] = ((mm(n2[...], w_cq[...]) + cbias[0:1]) * HD ** -0.5).astype(BF)
    loads[3].wait()
    for b in range(ways):
        if b > 0:
            peers(b)[1].wait()
        source = src_ref[...] if b == 0 else srcb[...]
        at = slice(b * src_rows, (b + 1) * src_rows)
        ck[at] = mm(source, w_ckv[:, 0:width]).astype(BF)
        cv[at] = (mm(source, w_ckv[:, width:]) + cbias[1:2]).astype(BF)
        if 0 < b < ways - 1:
            peers(b + 1)[1].start()
    store(cq, cq_out)
    store(ck, ck_out)
    store(cv, cv_out)
    score_bound(cq, ck, swap, lift)
    attend(cq, ck, cv, qfar, shit, lift, cp_buf, cp_out, cp_sem, cmixed, crecip)
    store(crecip, crecip_out)
    store(cmixed, cmixed_out)

    loads[4].wait()
    after[...] = one[...] + mm(cmixed[...], w_co[...]) + cbias[2:3]
    for r in range(0, rows, chunk):
        n3[r:r + chunk] = norm_rows(after[r:r + chunk], gain[2:3], shift[2:3]).astype(BF)
    n3t[...] = n3[...].T
    acc[...] = after[...] + obias_ref[...].astype(F32)
    dn3[...] = jnp.zeros_like(dn3)
    gib[...] = jnp.zeros_like(gib)
    loads[5].wait()
    loads[6].wait()
    feed_half(other, lambda name, step: None, ct_ref, w_f1, w_f2, ibias_ref, n3, n3t, acc, dn3, gib, gbuf, gsend_out, g_sem)
    drain(p_buf, p_out, p_sem)
    drain(cp_buf, cp_out, cp_sem)
    for copy in stores:
        copy.wait()


class Arrivals:
    def __init__(self, sem, **pairs):
        self.copies = {}
        for i, (name, (source, target)) in enumerate(pairs.items()):
            self.copies[name] = pltpu.make_async_copy(source, target, sem.at[i])
            self.copies[name].start()

    def need(self, *names):
        for name in names:
            if name in self.copies:
                self.copies.pop(name).wait()


class Departures:
    def __init__(self, sem):
        self.sem = sem
        self.copies = []

    def send(self, source, target):
        copy = pltpu.make_async_copy(source, target, self.sem.at[len(self.copies)])
        copy.start()
        self.copies.append(copy)

    def finish(self):
        for copy in self.copies:
            copy.wait()


def feed_kernel(
    gain_ref, ibias_ref, gib_ref, ct_h, n3_h, n3t_h, acc_h, dn3_h, after_h, w_f1_h, w_f2_h,
    y_ref, gkeep_out, two, small_out,
    gib, ct, n3, n3t, acc, dn3, after, w_f1, w_f2, gbuf, sem, g_sem,
):
    rows, width = ct.shape
    mine = halves_of(lax.axis_index("seq"))[0]
    steps = w_f2.shape[0] // width
    pairs = {"n3": (n3_h, n3)}
    w1, w2 = columns(w_f1_h, mine), rows_of(w_f2_h, mine)
    for j in range(steps):
        at = pl.ds(j * width, width)
        pairs["w1%d" % j] = (w1.at[:, at], w_f1.at[:, at])
        if j == 0:
            pairs["ct"] = (ct_h, ct)
        pairs["w2%d" % j] = (w2.at[at], w_f2.at[at])
        if j == 0:
            pairs.update(n3t=(n3t_h, n3t), acc=(acc_h, acc), dn3=(dn3_h, dn3))
    pairs["after"] = (after_h, after)
    arrivals = Arrivals(sem, **pairs)
    gain = gain_ref[...].astype(F32)
    gib[...] = gib_ref[...]

    def ready(name, j):
        if name == "w1":
            arrivals.need("n3", "w1%d" % j)
        elif name == "w2":
            arrivals.need("ct", "w2%d" % j)
        else:
            arrivals.need(name)

    feed_half(mine, ready, ct, w_f1, w_f2, ibias_ref, n3, n3t, acc, dn3, gib, gbuf, gkeep_out, g_sem)
    y_ref[...] = acc[...].astype(BF)
    arrivals.need("after")
    gain_grad = jnp.zeros((1, width), F32)
    shift_grad = jnp.zeros((1, width), F32)
    outer_grad = jnp.zeros((1, width), F32)
    chunk = 128
    for r in range(0, rows, chunk):
        at = slice(r, r + chunk)
        grad = dn3[at]
        back, rowed = norm_back(after[at], gain[2:3], grad)
        grown = ct[at].astype(F32)
        two[at] = grown + back
        gain_grad += jnp.sum(rowed, axis=0, keepdims=True)
        shift_grad += jnp.sum(grad, axis=0, keepdims=True)
        outer_grad += jnp.sum(grown, axis=0, keepdims=True)
    small_out[...] = jnp.zeros_like(small_out)
    for j in range(gib.shape[1] // width):
        small_out[j:j + 1] = gib[:, j * width:(j + 1) * width]
    small_out[8:9] = gain_grad
    small_out[9:10] = shift_grad
    small_out[10:11] = outer_grad


ANY = pl.BlockSpec(memory_space=pl.ANY)
VM = pl.BlockSpec(memory_space=pltpu.VMEM)
SM = pl.BlockSpec(memory_space=pltpu.SMEM)
V = pltpu.VMEM


def sems(count):
    return pltpu.SemaphoreType.DMA((count,))


def call(kernel, name, outs, in_specs, scratch, args, micros, out_specs=None, after=(), room=60):
    if after:
        args = (lax.optimization_barrier((args[0], *after))[0], *args[1:])
    return pl.pallas_call(
        kernel,
        out_shape=[jax.ShapeDtypeStruct(*o) for o in outs],
        in_specs=in_specs,
        out_specs=out_specs or [VM] * len(outs),
        scratch_shapes=scratch,
        compiler_params=pltpu.CompilerParams(vmem_limit_bytes=room * 2**20),
        cost_estimate=pl.CostEstimate(flops=int(micros * 1e9), bytes_accessed=int(micros * 3e6), transcendentals=0),
        name=name,
    )(*args)


def forward_call(ways, len_, x, xp, src, srcp, ct, gains, shifts, sbias, cbias, ibias, obias, weights):
    rows, width = x.shape
    srows = src.shape[0]
    nk, ns = ways * rows, ways * srows
    ff = weights[5].shape[1]
    rw = (rows, width)
    outs = [
        (((ff, width), BF), ANY), ((rw, F32), VM), ((rw, F32), VM), ((rw, BF), VM), (((width, rows), BF), VM),
        (((1, ff), F32), VM), ((rw, F32), VM),
        (((nk, width), BF), ANY), ((rw, BF), ANY), ((rw, BF), ANY), (((nk, width), BF), ANY), (((nk, width), BF), ANY),
        ((rw, BF), ANY), (((ns, width), BF), ANY), (((ns, width), BF), ANY),
        (((HEADS, nk, rows), BF), ANY), (((HEADS, ns, rows), BF), ANY),
        ((rw, F32), ANY), ((rw, F32), ANY), ((rw, BF), ANY), ((rw, BF), ANY), ((rw, F32), ANY),
    ]
    half = ff // 2
    peer = VM if ways == 2 else ANY
    slots = HEADS if ways == 2 else 2
    scratch = [V(w.shape, BF) for w in weights[:5]] + [V((width, half), BF), V((half, width), BF)] + [
        V(rw, BF), V(rw, BF), V((nk, width), BF), V((nk, width), BF),
        V((rows, PAIR), BF), V((nk, PAIR), BF), V((slots, nk, rows), BF), V(rw, BF), V(rw, F32),
        V(rw, F32), V(rw, BF), V(rw, BF), V((ns, width), BF), V((ns, width), BF), V((ns, PAIR), BF), V((slots, ns, rows), BF),
        V(rw, BF), V(rw, F32),
        V((2, width, width), BF), V((srows, width), BF), V((width, width), BF), V(rw, BF),
        sems(7), sems(slots), sems(slots), sems(16), sems(2), sems(2),
    ]
    return call(
        functools.partial(forward_kernel, ways), "forward", [o[0] for o in outs],
        [SM, VM, peer, VM, peer, VM] + [VM] * 6 + [ANY] * 7, scratch,
        (len_, x, xp, src, srcp, ct, gains, shifts, sbias, cbias, ibias, obias, *weights), 31, [o[1] for o in outs], room=60,
    )


def feed_call(ct, gains, ibias, n3, n3t, gib, acc, dn3, after, w_f1, w_f2):
    rw = ct.shape
    width = rw[1]
    ff = w_f1.shape[1]
    steps = ff // 2 // width
    return call(
        feed_kernel, "feed", [(rw, BF), ((ff, width), BF), (rw, F32), ((16, width), F32)],
        [VM] * 3 + [ANY] * 8,
        [V((1, ff), F32), V(rw, BF), V(rw, BF), V(n3t.shape, BF), V(rw, F32), V(rw, F32), V(rw, F32), V((width, ff // 2), BF),
         V((ff // 2, width), BF), V((4, width, width), BF), sems(6 + 2 * steps), sems(4)],
        (gains, ibias, gib, ct, n3, n3t, acc, dn3, after, w_f1, w_f2), 9, [VM, ANY, VM, VM],
    )


def attend_back(first, last, arrive, q_ref, k_ref, v_ref, gm_ref, recip_ref, mixed_ref, p_hbm, p_ref, sem, dq_ref, dk_ref, dv_ref):
    rows = q_ref.shape[0]
    keys = k_ref.shape[0]
    qlane = lax.broadcasted_iota(jnp.int32, (rows, PAIR), 1)
    klane = lax.broadcasted_iota(jnp.int32, (keys, PAIR), 1)

    qrow = lax.broadcasted_iota(jnp.int32, (PAIR, rows), 0)

    def fetch(pair, slot):
        return pltpu.make_async_copy(p_hbm.at[pl.ds(2 * pair, 2)], p_ref.at[slot], sem.at[slot])

    def one(pair, _):
        static = isinstance(pair, int)
        slot = (pair - first) % 2 if static else lax.rem(pair - first, 2)
        if static:
            if pair + 1 < last:
                fetch(pair + 1, 1 - slot).start()
        else:

            @pl.when(pair + 1 < last)
            def _():
                fetch(pair + 1, 1 - slot).start()

        lanes = pl.ds(pair * PAIR if static else pl.multiple_of(pair * PAIR, PAIR), PAIR)
        arrive(pair)
        qp = q_ref[:, lanes]
        kp = k_ref[:, lanes]
        vp = v_ref[:, lanes]
        kpt = kp.T
        dop = (gm_ref[:, lanes].astype(F32) * recip_ref[:, lanes]).astype(BF)
        prod = dop.astype(F32) * mixed_ref[:, lanes].astype(F32)
        fetch(pair, slot).wait()
        dqs, dks, dvs = [], [], []
        for h in (0, 1):
            inside = (qlane < HD) if h == 0 else (qlane >= HD)
            kinside = (klane < HD) if h == 0 else (klane >= HD)
            spare = HD * (1 - h)
            delta = jnp.sum(jnp.where(inside, prod, 0.0), axis=1, keepdims=True)
            high = delta.astype(BF).astype(F32)
            tail = jnp.where(qlane == spare, -high, jnp.where(qlane == spare + 1, high - delta, 0.0))
            doe = jnp.where(inside, dop, tail.astype(BF))
            ones = jnp.where((klane == spare) | (klane == spare + 1), 1.0, 0.0).astype(BF)
            ve = jnp.where(kinside, vp, ones)
            dpt = mm_t(ve, doe)
            p = p_ref[slot, h]
            dst = (p.astype(F32) * dpt).astype(BF)
            dvs.append(mm(p, dop))
            dks.append(mm(dst, qp))
            dqs.append(mm(kpt, dst))
        lanes = pl.ds((pair - first) * PAIR if static else pl.multiple_of((pair - first) * PAIR, PAIR), PAIR)
        dq_ref[:, lanes] = (jnp.where(qrow < HD, dqs[0], dqs[1]) * HD ** -0.5).astype(BF).T
        dk_ref[:, lanes] = jnp.where(klane < HD, dks[0], dks[1]).astype(BF)
        dv_ref[:, lanes] = jnp.where(klane < HD, dvs[0], dvs[1]).astype(BF)
        return 0

    fetch(first, 0).start()
    if keys <= 2 * rows:
        for pair in range(first, last):
            one(pair, 0)
    else:
        lax.fori_loop(first, last, one, 0)


def weight_halves(width, me, g, gkeep, gsend, departures, keep_out, send_out):
    half = width // 2
    keep, send = (pl.ds(pl.multiple_of(at * half, half), half) for at in halves_of(me))

    def put(i, value):
        at = slice(i * half, (i + 1) * half)
        g[...] = value.astype(BF)
        gkeep[at] = g[keep]
        gsend[at] = g[send]
        rows = pl.ds(i * half, half)
        departures.send(gsend.at[rows], send_out.at[rows])
        departures.send(gkeep.at[rows], keep_out.at[rows])

    return put


def cross_kernel(
    gain_ref, two_h, src_h, srcp_h, n2_h, q_h, k_h, v_h, p_h, recip_h, cmixed_h, mixed_h, one_h, w_cq_h, w_co_h, w_so_h, w_ckv_h,
    keep_out, send_out, sgrad_out, gm_out, oneg_out, small_out,
    two, src, n2, q, k, v, p_buf, recip, cmixed, mixed, one, w_cq, w_co, w_so, w_ckv, gm, dq, dk, dv, g, dn, gkeep, gsend, sgrad,
    p_sem, sem, out_sem,
):
    rows, width = two.shape
    srows = src_h.shape[0]
    me = lax.axis_index("seq")
    arrivals = Arrivals(
        sem, two=(two_h, two), w_co=(w_co_h, w_co), q=(q_h, q), k=(k_h, k), v=(v_h, v), recip=(recip_h, recip),
        cmixed=(cmixed_h, cmixed), w_cq=(w_cq_h, w_cq), one=(one_h, one), n2=(n2_h, n2), w_so=(w_so_h, w_so), mixed=(mixed_h, mixed),
        src=(src_h, src.at[pl.ds(0, srows)]), srcp=(srcp_h, src.at[pl.ds(srows, srcp_h.shape[0])]), w_ckv=(w_ckv_h, w_ckv))
    departures = Departures(out_sem)
    gain = gain_ref[...].astype(F32)
    put = weight_halves(width, me, g, gkeep, gsend, departures, keep_out, send_out)
    small_out[...] = jnp.zeros_like(small_out)
    arrivals.need("two", "w_co")
    branch = two[...].astype(BF)
    small_out[0:1] = column_sum(branch)
    gm[...] = mm_t(branch, w_co[...]).astype(BF)
    arrivals.need("q", "k", "v", "recip", "cmixed")
    attend_back(0, HEADS // 2, lambda pair: None, q, k, v, gm, recip, cmixed, p_h, p_buf, p_sem, dq, dk, dv)
    arrivals.need("w_cq", "one")
    dn[...] = mm_t(dq[...], w_cq[...])
    chunk = 128
    gain_grad = jnp.zeros((1, width), F32)
    shift_grad = jnp.zeros((1, width), F32)
    for r in range(0, rows, chunk):
        at = slice(r, r + chunk)
        grad = dn[at]
        back, rowed = norm_back(one[at], gain[1:2], grad)
        one[at] = two[at] + back
        gain_grad += jnp.sum(rowed, axis=0, keepdims=True)
        shift_grad += jnp.sum(grad, axis=0, keepdims=True)
    departures.send(one, oneg_out)
    small_out[2:3] = gain_grad
    small_out[3:4] = shift_grad
    after = one[...].astype(BF)
    small_out[4:5] = column_sum(after)
    arrivals.need("w_so")
    gm[...] = mm_t(after, w_so[...]).astype(BF)
    departures.send(gm, gm_out)
    put(0, t_mm(cmixed[...], two[...].astype(BF)))
    arrivals.need("n2", "mixed")
    put(1, t_mm(n2[...], dq[...]))
    put(2, t_mm(mixed[...], after))
    arrivals.need("src", "srcp", "w_ckv")
    for i, ref in enumerate((dk, dv)):
        put(3 + i, t_mm(src[...], ref[...]))
    sgrad[...] = (mm_t(dk[...], w_ckv[:, 0:width]) + mm_t(dv[...], w_ckv[:, width:])).astype(BF)
    departures.send(sgrad, sgrad_out)
    small_out[1:2] = column_sum(dq[...])
    small_out[5:6] = column_sum(dv[...])
    departures.finish()


def self_kernel(
    gain_ref, small1, small2, q_h, k_h, v_h, p_h, recip_h, mixed_h, gm_h, n1_h, x_h, xp_h, w_h,
    keep_out, send_out, dn_own, dn_peer_out,
    q, k, v, p_buf, recip, mixed, gm, n1, x, w, dq, dk, dv, g, gkeep, gsend, small, dn_peer,
    p_sem, pair_sem, sem, out_sem,
):
    rows, width = q.shape
    nk = k.shape[0]
    half = width // 2
    me = lax.axis_index("seq")
    operands = ((q_h, q), (k_h, k), (v_h, v), (gm_h, gm), (recip_h, recip), (mixed_h, mixed))

    def lanes_of(pair):
        lanes = pl.ds(pair * PAIR if isinstance(pair, int) else pl.multiple_of(pair * PAIR, PAIR), PAIR)
        return [
            pltpu.make_async_copy(source.at[:, lanes], target.at[:, lanes], pair_sem.at[i, pair])
            for i, (source, target) in enumerate(operands)
        ]

    for pair in range(HEADS // 2):
        for copy in lanes_of(pair):
            copy.start()

    def arrive(pair):
        for copy in lanes_of(pair):
            copy.wait()

    if nk > 2 * rows:
        n1, x = v, k
        dn_peer = v.at[pl.ds(0, nk - rows)]

    def rest():
        return Arrivals(sem, n1=(n1_h, n1), w=(w_h, w), x=(x_h, x.at[pl.ds(0, rows)]), xp=(xp_h, x.at[pl.ds(rows, nk - rows)]))

    arrivals = rest() if nk <= 2 * rows else None
    departures = Departures(out_sem)
    gain = gain_ref[...].astype(F32)
    attend_back(0, HEADS // 2, arrive, q, k, v, gm, recip, mixed, p_h, p_buf, p_sem, dq, dk, dv)
    arrivals = arrivals or rest()
    put = weight_halves(width, me, g, gkeep, gsend, departures, keep_out, send_out)
    arrivals.need("n1")
    put(0, t_mm(n1[0:rows], dq[...]))
    put(1, t_mm(n1[...], dk[...]))
    put(2, t_mm(n1[...], dv[...]))
    arrivals.need("w", "x", "xp")
    gain_grad = jnp.zeros((1, width), F32)
    shift_grad = jnp.zeros((1, width), F32)
    chunk = 128
    for b in reversed(range(nk // rows)):
        at = slice(b * rows, (b + 1) * rows)
        grad = mm_t(dk[at], w[:, width:2 * width]) + mm_t(dv[at], w[:, 2 * width:])
        if b == 0:
            grad = grad + mm_t(dq[...], w[:, 0:width])
        dn_own[...] = grad
        for r in range(0, rows, chunk):
            piece = dn_own[r:r + chunk]
            xhat = norm_parts(x[b * rows + r:b * rows + r + chunk].astype(F32))[0]
            gain_grad += jnp.sum(piece * xhat, axis=0, keepdims=True)
            shift_grad += jnp.sum(piece, axis=0, keepdims=True)
        if b > 0:
            dn_peer[(b - 1) * rows:b * rows] = dn_own[...].astype(BF)
    departures.send(dn_peer, dn_peer_out)
    small[...] = jnp.zeros_like(small)
    small[0:1] = gain_grad
    small[1:2] = shift_grad
    small[2:3] = column_sum(dq[...])
    small[3:4] = column_sum(dv[...])
    small[8:16] = small2[...]
    small[16:32] = small1[...]
    for side, ref, out in zip(halves_of(me), (gkeep, gsend), (keep_out, send_out)):
        ref[3 * half:3 * half + 16] = small[pl.ds(pl.multiple_of(side * 16, 16), 16)].astype(BF)
        ref[3 * half + 16:] = jnp.zeros((16, width), BF)
        departures.send(ref.at[pl.ds(3 * half, 32)], out.at[pl.ds(3 * half, 32)])
    departures.finish()


def last_kernel(x_ref, gain_ref, dn_ref, came_ref, oneg_ref, xgrad):
    gain = gain_ref[...].astype(F32)
    chunk = 128
    for r in range(0, x_ref.shape[0], chunk):
        at = slice(r, r + chunk)
        grad = dn_ref[at]
        for b in range(came_ref.shape[0]):
            grad = grad + came_ref[b, at].astype(F32)
        back = norm_back(x_ref[at].astype(F32), gain[0:1], grad)[0]
        xgrad[at] = (oneg_ref[at] + back).astype(BF)


def cross_call(gains, two, src, srcp, n2, q, k, v, p, recip, cmixed, mixed, one, w_cq, w_co, w_so, w_ckv):
    rows, width = two.shape
    ns = k.shape[0]
    rw, ww, nw = (rows, width), (width, width), (ns, width)
    half = (5 * width // 2, width)
    outs = [(half, BF), (half, BF), (nw, BF), (rw, BF), (rw, F32), ((8, width), F32)]
    scratch = [V(rw, F32), V(nw, BF), V(rw, BF), V(rw, BF), V(nw, BF), V(nw, BF), V((2, 2, ns, rows), BF), V(rw, F32), V(rw, BF), V(rw, BF),
               V(rw, F32), V(ww, BF), V(ww, BF), V(ww, BF), V((width, 2 * width), BF), V(rw, BF), V(rw, BF), V(nw, BF), V(nw, BF), V(ww, BF),
               V(rw, F32), V(half, BF), V(half, BF), V(nw, BF), sems(2), sems(15), sems(13)]
    return call(cross_kernel, "cross_back", outs, [VM] + [ANY] * 16, scratch,
                (gains, two, src, srcp, n2, q, k, v, p, recip, cmixed, mixed, one, w_cq, w_co, w_so, w_ckv), 14, [ANY] * 5 + [VM])


def self_call(gains, small1, small2, q, k, v, p, recip, mixed, gm, n1, x, xp, w):
    rows, width = x.shape
    nk = n1.shape[0]
    rw, nw, pw = (rows, width), (nk, width), (nk - rows, width)
    half = (3 * width // 2 + 32, width)
    outs = [(half, BF), (half, BF), (rw, F32), (pw, BF)]
    spare = nw if nk <= 2 * rows else (16, width)
    scratch = [V(rw, BF), V(nw, BF), V(nw, BF), V((2, 2, nk, rows), BF), V(rw, F32), V(rw, BF), V(rw, BF),
               V(spare, BF), V(spare, BF), V(w.shape, BF), V(rw, BF), V(nw, BF), V(nw, BF), V((width, width), BF), V(half, BF), V(half, BF),
               V((32, width), F32), V(pw if nk <= 2 * rows else (16, width), BF), sems(2), pltpu.SemaphoreType.DMA((6, HEADS // 2)), sems(4), sems(9)]
    return call(self_kernel, "self_back", outs, [VM] * 3 + [ANY] * 11, scratch,
                (gains, small1, small2, q, k, v, p, recip, mixed, gm, n1, x, xp, w), 18, [ANY, ANY, VM, ANY])


def last_call(x, gains, dn, came, oneg, after):
    return call(last_kernel, "last_back", [(x.shape, BF)], [VM] * 5, [], (x, gains, dn, came, oneg), 3, after=after, room=12)[0]


def feed_plan(ff, width):
    per = ff // width // 2
    moves = []
    for half in (0, 1):
        for j in range(per):
            moves.append((half, 2 * j * width, width, 0, 0, (half * per + j) * width))
            moves.append((half, (2 * j + 1) * width, width, 1, (half * per + j) * width, 0))
    return [(width, ff), (ff, width)], moves


def cross_plan(width):
    part = width // 2
    moves = []
    for half in (0, 1):
        for i, (out, column) in enumerate(((0, 0), (1, 0), (2, 0), (3, 0), (3, width))):
            moves.append((half, i * part, part, out, half * part, column))
    return [(width, width)] * 3 + [(width, 2 * width)], moves


def last_plan(width):
    part = width // 2
    moves = []
    for half in (0, 1):
        for i in range(3):
            moves.append((half, i * part, part, 0, half * part, i * width))
        moves.append((half, 3 * part, 16, 1, half * 16, 0))
    return [(width, 3 * width), (32, width)], moves


def unpack_kernel(moves, where, *refs):
    parts = refs[:4]
    outs = refs[4:-4]
    full, buf, in_sem, out_sem = refs[-4:]
    size = parts[0].shape[0]
    half = where[0]
    spots = ((half, where[1]), (half, 1 - where[1]), (1 - half, where[2]), (1 - half, 1 - where[2]))
    loads = []
    for i, (part, (row, side)) in enumerate(zip(parts, spots)):
        at = pl.ds(pl.multiple_of(side * size, 16), size)
        loads.append(pltpu.make_async_copy(part, full.at[row, at], in_sem.at[i]))
    for load in loads:
        load.start()
    for load in loads:
        load.wait()
    stores = []
    for i, (row, first, rows, out, to, column) in enumerate(moves):
        slot = i % buf.shape[0]
        if i >= buf.shape[0]:
            stores[i - buf.shape[0]].wait()
        buf[slot, 0:rows] = full[row, first:first + rows].astype(F32)
        copy = pltpu.make_async_copy(
            buf.at[slot, pl.ds(0, rows)], outs[out].at[pl.ds(to, rows), pl.ds(column, buf.shape[2])], out_sem.at[slot])
        copy.start()
        stores.append(copy)
    for copy in stores[-buf.shape[0]:]:
        copy.wait()


def unpack_call(where, parts, name, plan, micros):
    shapes, moves = plan
    size, width = parts[0].shape
    most = max(move[2] for move in moves)
    scratch = [V((2, 2 * size, width), BF), V((4, most, width), F32), sems(4), sems(4)]
    return call(functools.partial(unpack_kernel, moves), name, [(shape, F32) for shape in shapes], [SM] + [ANY] * 4, scratch,
                (where, *parts), micros, [ANY] * len(shapes), room=12)


def ring(value, axis, shift):
    size = lax.axis_size(axis)
    return lax.ppermute(value, axis, [(i, (i + shift) % size) for i in range(size)])


def add(left, right):
    return (left.astype(F32) + right.astype(F32)).astype(BF)


def steps_of():
    rest = [("seq", 1 << b) for b in range(1, lax.axis_size("seq").bit_length() - 1)]
    dp = [("dp", 1 << b) for b in range(lax.axis_size("dp").bit_length() - 1)]
    near, far_off = dp[:2], dp[2:]
    halving = list(zip(near, near[::-1]))
    whole = [(step, step) for step in rest] + list(zip(far_off[::-1], far_off))
    return halving, whole


def flip(value, step):
    ways = lax.axis_size("seq")
    pairs = []
    for i in range(lax.axis_size("dp")):
        for s in range(ways):
            axis, bit = step[s % 2]
            to = (i ^ bit) * ways + s if axis == "dp" else i * ways + (s ^ bit)
            pairs.append((i * ways + s, to))
    return lax.ppermute(value, ("dp", "seq"), pairs)


def flip_core(value):
    return flip(value, (("seq", 1), ("seq", 1)))


def side_of(step):
    sides = [lax.axis_index(axis) // bit % 2 for axis, bit in step]
    return jnp.where(lax.axis_index("seq") % 2 == 0, sides[0], sides[1])


def scatter_step(mine, came, step):
    side = side_of(step)
    half = mine.shape[0] // 2

    def take(value, at):
        return lax.dynamic_slice_in_dim(value, at * half, half)

    send = add(take(mine, 1 - side), take(came, 1 - side))
    return add(take(mine, side), take(came, side)), send, flip(send, step)


def joined(mine, came, step):
    return jnp.where(side_of(step) == 0, jnp.concatenate([mine, came]), jnp.concatenate([came, mine]))


def places(step):
    parity = lax.axis_index("seq") % 2
    sides = [lax.axis_index(axis) // bit % 2 for axis, bit in step]
    own = jnp.where(parity == 0, sides[0], sides[1])
    other = jnp.where(parity == 0, sides[1], sides[0])
    return jnp.stack([parity, own, other]).astype(jnp.int32)


def tie(value, *others):
    return lax.optimization_barrier((value, *others))[0]


def local(
    layer_input, source_states, source_lengths, cotangent, norm_gain, norm_bias, self_in, self_bias, self_out,
    cross_query, cross_keyval, cross_bias, cross_out, feed_in, inner_bias, feed_out, outer_bias,
):
    ways = lax.axis_size("seq")
    x = layer_input[0]
    source = source_states[0]
    ct = cotangent[0]
    rows, width = x.shape
    srows = source.shape[0]
    xp = jnp.concatenate([ring(x, "seq", -b) for b in range(1, ways)])
    srcp = jnp.concatenate([ring(source, "seq", -b) for b in range(1, ways)])
    ibias = inner_bias.reshape(1, -1)
    (gsend, acc, dn3, n3, n3t, gib, after, n1, n2, q, k, v, cq, ck, cv, p, cp, recip, crecip, mixed, cmixed, one) = forward_call(
        ways, source_lengths, x, xp, source, srcp, ct, norm_gain, norm_bias, self_bias, cross_bias,
        ibias, outer_bias.reshape(1, -1),
        (self_in, self_out, cross_query, cross_keyval, cross_out, feed_in, feed_out),
    )
    halving, whole = steps_of()
    first, second = halving
    feed_came = flip_core(gsend)
    y, gkeep, two, small1 = feed_call(ct, norm_gain, ibias, n3, n3t, gib, acc, dn3, after, feed_in, feed_out)
    feed, feed_sent, feed_came = scatter_step(gkeep, tie(feed_came, two), first)
    ckeep, csend, sgrad, gm, oneg, small2 = cross_call(
        norm_gain, tie(two, feed_sent), source, srcp, n2, cq, ck, cv, cp, crecip, cmixed, mixed, one,
        cross_query, cross_out, self_out, cross_keyval)
    cross_came = flip_core(csend)
    feed, feed_sent, feed_came = scatter_step(feed, tie(feed_came, gm), second)
    lkeep, lsend, dn, dn_peer = self_call(
        norm_gain, small1, small2, q, k, v, p, recip, mixed, tie(gm, feed_sent), n1, x, xp, self_in)
    last_came = flip_core(lsend)
    dn_came = jnp.stack([ring(dn_peer[(b - 1) * rows:b * rows], "seq", b) for b in range(1, ways)])
    for b in range(1, ways):
        sgrad_came = ring(sgrad[b * srows:(b + 1) * srows], "seq", b).astype(F32)
        total = sgrad_came if b == 1 else total + sgrad_came
    sgrad = (sgrad[:srows].astype(F32) + total).astype(BF)
    cross, cross_sent, cross_came = scatter_step(ckeep, tie(cross_came, dn), first)
    feed = add(feed, tie(feed_came, cross_sent))
    feed_came = flip(feed, whole[0])
    last, last_sent, last_came = scatter_step(lkeep, tie(last_came, feed), first)
    cross, cross_sent, cross_came = scatter_step(cross, tie(cross_came, last_sent), second)
    feed = add(feed, tie(feed_came, cross_sent))
    for step in whole[1:-1]:
        feed = add(feed, flip(feed, step))
    feed_came = flip(feed, whole[-1])
    last, last_sent, last_came = scatter_step(last, tie(last_came, feed), second)
    xgrad = last_call(x, norm_gain, dn, dn_came, oneg, (last_sent,))
    cross = add(cross, tie(cross_came, xgrad))
    cross_came = flip(cross, whole[0])
    feed = add(feed, tie(feed_came, cross))
    feed_came = flip(feed, second)
    last = add(last, tie(last_came, feed))
    last_came = flip(last, whole[0])
    cross = add(cross, tie(cross_came, last))
    for step in whole[1:-1]:
        cross = add(cross, flip(cross, step))
    cross_came = flip(cross, whole[-1])
    feed = joined(feed, tie(feed_came, cross), second)
    feed_came = flip(feed, first)
    feed_other = flip_core(feed)
    last = add(last, tie(last_came, feed))
    for step in whole[1:-1]:
        last = add(last, flip(last, step))
    last_came = flip(last, whole[-1])
    cross = add(cross, tie(cross_came, last))
    cross_came = flip(cross, second)
    last = add(last, tie(last_came, cross))
    last_came = flip(last, second)
    feed_came = tie(feed_came, last)
    feed_last = flip_core(feed_came)
    where = places(first)
    cross = joined(cross, tie(cross_came, feed_came), second)
    cross_came = flip(cross, first)
    cross_other = flip_core(cross)
    last = joined(last, tie(last_came, cross), second)
    last_came = flip(last, first)
    last_other = flip_core(last)
    g_feed_in, g_feed_out = unpack_call(
        where, (feed, feed_came, feed_other, tie(feed_last, last)), "feed_unpack", feed_plan(feed_in.shape[1], width), 5)
    cross_came = tie(cross_came, g_feed_in)
    cross_last = flip_core(cross_came)
    last_came = tie(last_came, cross_came)
    last_last = flip_core(last_came)
    g_cross_out, g_cross_query, g_self_out, g_keyval = unpack_call(
        where, (cross, cross_came, cross_other, tie(cross_last, last_came)), "cross_unpack", cross_plan(width), 3)
    g_self_in, small = unpack_call(
        where, (last, last_came, last_other, tie(last_last, g_keyval)), "last_unpack", last_plan(width), 3)
    per = feed_in.shape[1] // width
    return (
        y[None], xgrad[None], sgrad[None],
        jnp.stack([small[0], small[10], small[24]]),
        jnp.stack([small[1], small[11], small[25]]),
        g_self_in,
        jnp.stack([small[2], small[3], small[12]]),
        g_self_out, g_cross_query, g_keyval,
        jnp.stack([small[9], small[13], small[8]]),
        g_cross_out, g_feed_in, small[16:16 + per].reshape(-1), g_feed_out, small[26],
    )


def solution(mesh):
    split = P("dp", "seq", None)
    in_specs = (split, split, P("dp", None), split) + (P(),) * 13
    out_specs = (split,) * 3 + (P(),) * 13
    return jax.shard_map(local, mesh=mesh, in_specs=in_specs, out_specs=out_specs, check_vma=False)
```

```python
import functools
import jax
import jax.numpy as jnp
from jax import lax
from jax.experimental import pallas as pl
from jax.experimental.pallas import tpu as pltpu
from jax.sharding import PartitionSpec as P

HEADS = 8
HD = 64
PAIR = 2 * HD
eps = 1e-05
far = -1e30
BF = jnp.bfloat16
F32 = jnp.float32


def mm(left, right):
    return lax.dot_general(left, right, (((1,), (0,)), ((), ())), preferred_element_type=F32)


def mm_t(left, right):
    return lax.dot_general(left, right, (((1,), (1,)), ((), ())), preferred_element_type=F32)


def t_mm(left, right):
    return lax.dot_general(left, right, (((0,), (0,)), ((), ())), preferred_element_type=F32)


def norm_parts(values):
    center = values - jnp.mean(values, axis=-1, keepdims=True)
    spread = jnp.mean(center * center, axis=-1, keepdims=True)
    rate = lax.rsqrt(spread + eps)
    return center * rate, rate


def norm_rows(values, gain, shift):
    return norm_parts(values)[0] * gain + shift


def norm_back(values, gain, grad):
    xhat, rate = norm_parts(values)
    e = grad * gain
    back = rate * (
        e - jnp.mean(e, axis=-1, keepdims=True) - xhat * jnp.mean(e * xhat, axis=-1, keepdims=True)
    )
    return back, grad * xhat


def sentence_lanes(lengths, factor, shape):
    lane = lax.broadcasted_iota(jnp.int32, shape, 1) % HD
    begin = jnp.zeros(shape, jnp.int32)
    end = jnp.zeros(shape, jnp.int32)
    total = jnp.int32(0)
    for n in range(lengths.shape[1]):
        after = total + factor * lengths[0, n]
        begin = jnp.where(lane == n, total, begin)
        end = jnp.where(lane == n, after, end)
        total = after
    return begin, end


def sentence_hits(lengths, factor, first, rows):
    begin, end = sentence_lanes(lengths, factor, (1, PAIR))
    place = lax.broadcasted_iota(jnp.int32, (rows, PAIR), 0) + first
    return jnp.where((place >= begin) & (place < end), 1.0, 0.0)


def sentence_far(lengths, hits):
    lane = lax.broadcasted_iota(jnp.int32, hits.shape, 1) % HD
    return jnp.where(lane < lengths.shape[1], (1.0 - hits) * far, 0.0)


def gelu_parts(v):
    c = 0.7978845608028654
    square = v * v
    t = jnp.tanh(c * (v + 0.044715 * (square * v)))
    half = 0.5 * (1.0 + t)
    slope = half + (0.5 * v) * (1.0 - t * t) * (c * (1.0 + 3 * 0.044715 * square))
    return v * half, slope


def swap_heads(width):
    row = lax.broadcasted_iota(jnp.int32, (width, width), 0) // HD
    column = lax.broadcasted_iota(jnp.int32, (width, width), 1) // HD
    return jnp.where((row != column) & (row // 2 == column // 2), 1.0, 0.0).astype(BF)


def score_bound(q_ref, k_ref, swap_ref, lift_ref):
    most = jnp.max(jnp.abs(k_ref[...]).astype(F32), axis=0, keepdims=True)
    size = (jnp.abs(q_ref[...]).astype(F32) * most).astype(BF)
    lift_ref[...] = (-1.02 * mm(size, swap_ref[...])).astype(BF)


def attend(q_ref, k_ref, v_ref, qfar_ref, khit_ref, lift_ref, p_ref, p_out, sem, mixed_ref, recip_ref):
    rows = q_ref.shape[0]
    keys = k_ref.shape[0]
    slots = p_ref.shape[0]
    qlane = lax.broadcasted_iota(jnp.int32, (rows, PAIR), 1) < HD
    klane = lax.broadcasted_iota(jnp.int32, (keys, PAIR), 1) < HD
    vrow = lax.broadcasted_iota(jnp.int32, (PAIR, keys), 0) < HD

    def copy(n, slot):
        return pltpu.make_async_copy(p_ref.at[slot], p_out.at[n], sem.at[slot])

    def one(pair, exact, reuse):
        lanes = pl.ds(pair * PAIR if isinstance(pair, int) else pl.multiple_of(pair * PAIR, PAIR), PAIR)
        qp = q_ref[:, lanes]
        kp = k_ref[:, lanes]
        vpt = v_ref[:, lanes].T
        rest = qfar_ref[...] if exact else qfar_ref[...] + lift_ref[:, lanes]
        outs = []
        for h in (0, 1):
            qe = jnp.where(qlane if h == 0 else ~qlane, qp, rest)
            ke = jnp.where(klane if h == 0 else ~klane, kp, khit_ref[...])
            st = mm_t(ke, qe)
            if exact:
                st = st - jnp.max(st, axis=0, keepdims=True)
            p = jnp.exp(st).astype(BF)
            n = 2 * pair + h
            slot = n if slots == HEADS else h
            if reuse is not None:
                pl.when(reuse)(lambda n=n, slot=slot: copy(n, slot).wait())
            p_ref[slot] = p
            copy(n, slot).start()
            ve = jnp.where(vrow if h == 0 else ~vrow, vpt, jnp.ones_like(vpt))
            outs.append(mm(ve, p).T)
        value = jnp.where(qlane, outs[0], outs[1])
        total = jnp.where(qlane, outs[1], outs[0])
        recip = 1.0 / pltpu.roll(total, HD, 1)
        mixed_ref[:, lanes] = (value * recip).astype(BF)
        recip_ref[:, lanes] = recip
        return jnp.min(total.reshape(rows // 8, 8, PAIR), axis=0)

    least = lax.fori_loop(
        0, HEADS // 2, lambda pair, low: jnp.minimum(low, one(pair, False, None if slots == HEADS else pair > 0)),
        jnp.full((8, PAIR), 1.0, F32))

    @pl.when(jnp.logical_not(jnp.min(least) > 1e-18))
    def _():
        for slot in range(slots):
            copy(slot, slot).wait()

        def again(pair, _):
            one(pair, True, pair > 0 if slots < HEADS else None)
            return 0

        lax.fori_loop(0, HEADS // 2, again, 0)


def drain(p_ref, p_out, sem):
    for slot in range(p_ref.shape[0]):
        pltpu.make_async_copy(p_ref.at[slot], p_out.at[slot], sem.at[slot]).wait()


def feed_half(half, ready, ct_ref, w1, w2, ibias_ref, n3, n3t, acc, dn3, gib, gbuf, gout, g_sem):
    width = n3.shape[1]
    steps = w2.shape[0] // width
    begun = []
    for j in range(steps):
        at = slice(j * width, (j + 1) * width)
        wide = pl.ds(pl.multiple_of((half * steps + j) * width, width), width)
        ready("w1", j)
        hidden = mm(n3[...], w1[:, at]) + ibias_ref[:, wide]
        acted, slope = gelu_parts(hidden)
        acted = acted.astype(BF)
        ready("w2", j)
        gh = (mm_t(ct_ref[...], w2[at]) * slope).astype(BF)
        gib[:, wide] = column_sum(gh)
        ready("n3t", j)
        for i, product in enumerate((lambda: mm(n3t[...], gh), lambda: t_mm(acted, ct_ref[...]))):
            slot = (2 * j + i) % gbuf.shape[0]
            if len(begun) >= gbuf.shape[0]:
                begun[len(begun) - gbuf.shape[0]].wait()
            gbuf[slot] = product().astype(BF)
            copy = pltpu.make_async_copy(gbuf.at[slot], gout.at[pl.ds((2 * j + i) * width, width)], g_sem.at[slot])
            copy.start()
            begun.append(copy)
        ready("acc", j)
        acc[...] += mm(acted, w2[at])
        ready("dn3", j)
        dn3[...] += mm_t(gh, w1[:, at])
    for copy in begun[-gbuf.shape[0]:]:
        copy.wait()


def column_sum(block):
    return jnp.sum(block.astype(F32), axis=0, keepdims=True)


def start_all(pairs, sem):
    copies = [pltpu.make_async_copy(a, b, sem.at[i]) for i, (a, b) in enumerate(pairs)]
    for copy in copies:
        copy.start()
    return copies


def halves_of(me):
    return lax.rem(me, 2), 1 - lax.rem(me, 2)


def columns(ref, half):
    size = ref.shape[1] // 2
    return ref.at[:, pl.ds(pl.multiple_of(half * size, size), size)]


def rows_of(ref, half):
    size = ref.shape[0] // 2
    return ref.at[pl.ds(pl.multiple_of(half * size, size), size)]


def forward_kernel(
    ways,
    len_ref, x_ref, xp_ref, src_ref, srcp_ref, ct_ref,
    gain_ref, shift_ref, sbias_ref, cbias_ref, ibias_ref, obias_ref,
    w_in_h, w_so_h, w_cq_h, w_ckv_h, w_co_h, w_f1_h, w_f2_h,
    gsend_out, acc, dn3, n3, n3t, gib, after, n1_out, n2_out, q_out, k_out, v_out, cq_out, ck_out, cv_out,
    p_out, cp_out, recip_out, crecip_out, mixed_out, cmixed_out, one_out,
    w_in, w_so, w_cq, w_ckv, w_co, w_f1, w_f2,
    n1, q, k, v, qfar, khit, p_buf, mixed, recip, one, n2, cq, ck, cv, shit, cp_buf, cmixed, crecip,
    gbuf, srcb, swap, lift, ibias, w_sem, p_sem, cp_sem, o_sem, g_sem, x_sem,
):
    rows, width = x_ref.shape
    me = lax.axis_index("seq")
    other = halves_of(me)[1]
    weights = [
        (w_in_h, w_in), (w_so_h, w_so), (w_cq_h, w_cq), (w_ckv_h, w_ckv), (w_co_h, w_co),
        (columns(w_f1_h, other), w_f1), (rows_of(w_f2_h, other), w_f2),
    ]
    loads = [pltpu.make_async_copy(a, b, w_sem.at[i]) for i, (a, b) in enumerate(weights)]
    src_rows = src_ref.shape[0]

    def peers(b):
        return (
            pltpu.make_async_copy(xp_ref.at[pl.ds((b - 1) * rows, rows)], n3, x_sem.at[0]),
            pltpu.make_async_copy(srcp_ref.at[pl.ds((b - 1) * src_rows, src_rows)], srcb, x_sem.at[1]),
        )

    loads[0].start()
    for load in peers(1):
        load.start()
    for load in loads[1:]:
        load.start()
    ibias[...] = ibias_ref[...].astype(F32).reshape(ibias.shape)
    gain = gain_ref[...].astype(F32)
    shift = shift_ref[...].astype(F32)
    sbias = sbias_ref[...].astype(F32)
    cbias = cbias_ref[...].astype(F32)
    stores = []

    def store(src, dst):
        copy = pltpu.make_async_copy(src, dst, o_sem.at[len(stores)])
        copy.start()
        stores.append(copy)

    chunk = 128
    for r in range(0, rows, chunk):
        n1[r:r + chunk] = norm_rows(x_ref[r:r + chunk].astype(F32), gain[0:1], shift[0:1]).astype(BF)
    store(n1, n1_out.at[0:rows])
    for b in range(ways):
        at = lax.rem(me + b, ways)
        khit[b * rows:(b + 1) * rows] = sentence_hits(len_ref, 2, at * rows, rows).astype(BF)
        shit[b * src_rows:(b + 1) * src_rows] = sentence_hits(len_ref, 1, at * src_rows, src_rows).astype(BF)
    qfar[...] = sentence_far(len_ref, khit[0:rows].astype(F32)).astype(BF)

    loads[0].wait()
    q[...] = ((mm(n1[...], w_in[:, 0:width]) + sbias[0:1]) * HD ** -0.5).astype(BF)
    for b in range(ways):
        at = slice(b * rows, (b + 1) * rows)
        rowed = n1
        if b > 0:
            rowed = n3
            peers(b)[0].wait()
            for r in range(0, rows, chunk):
                block = n3[r:r + chunk].astype(F32)
                n3[r:r + chunk] = norm_rows(block, gain[0:1], shift[0:1]).astype(BF)
            nsave = pltpu.make_async_copy(n3, n1_out.at[at], x_sem.at[0])
            nsave.start()
        k[at] = mm(rowed[...], w_in[:, width:2 * width]).astype(BF)
        v[at] = (mm(rowed[...], w_in[:, 2 * width:]) + sbias[1:2]).astype(BF)
        if b > 0:
            nsave.wait()
        if 0 < b < ways - 1:
            peers(b + 1)[0].start()
    store(q, q_out)
    store(k, k_out)
    store(v, v_out)
    swap[...] = swap_heads(width)
    score_bound(q, k, swap, lift)
    attend(q, k, v, qfar, khit, lift, p_buf, p_out, p_sem, mixed, recip)
    store(recip, recip_out)
    store(mixed, mixed_out)

    loads[1].wait()
    one[...] = x_ref[...].astype(F32) + mm(mixed[...], w_so[...]) + sbias[2:3]
    for r in range(0, rows, chunk):
        n2[r:r + chunk] = norm_rows(one[r:r + chunk], gain[1:2], shift[1:2]).astype(BF)
    store(one, one_out)
    store(n2, n2_out)
    loads[2].wait()
    cq[...] = ((mm(n2[...], w_cq[...]) + cbias[0:1]) * HD ** -0.5).astype(BF)
    loads[3].wait()
    for b in range(ways):
        if b > 0:
            peers(b)[1].wait()
        source = src_ref[...] if b == 0 else srcb[...]
        at = slice(b * src_rows, (b + 1) * src_rows)
        ck[at] = mm(source, w_ckv[:, 0:width]).astype(BF)
        cv[at] = (mm(source, w_ckv[:, width:]) + cbias[1:2]).astype(BF)
        if 0 < b < ways - 1:
            peers(b + 1)[1].start()
    store(cq, cq_out)
    store(ck, ck_out)
    store(cv, cv_out)
    score_bound(cq, ck, swap, lift)
    attend(cq, ck, cv, qfar, shit, lift, cp_buf, cp_out, cp_sem, cmixed, crecip)
    store(crecip, crecip_out)
    store(cmixed, cmixed_out)

    loads[4].wait()
    after[...] = one[...] + mm(cmixed[...], w_co[...]) + cbias[2:3]
    for r in range(0, rows, chunk):
        n3[r:r + chunk] = norm_rows(after[r:r + chunk], gain[2:3], shift[2:3]).astype(BF)
    n3t[...] = n3[...].T
    acc[...] = after[...] + obias_ref[...].astype(F32).reshape(1, width)
    dn3[...] = jnp.zeros_like(dn3)
    gib[...] = jnp.zeros_like(gib)
    loads[5].wait()
    loads[6].wait()
    feed_half(other, lambda name, step: None, ct_ref, w_f1, w_f2, ibias, n3, n3t, acc, dn3, gib, gbuf, gsend_out, g_sem)
    drain(p_buf, p_out, p_sem)
    drain(cp_buf, cp_out, cp_sem)
    for copy in stores:
        copy.wait()


class Arrivals:
    def __init__(self, sem, **pairs):
        self.copies = {}
        for i, (name, (source, target)) in enumerate(pairs.items()):
            self.copies[name] = pltpu.make_async_copy(source, target, sem.at[i])
            self.copies[name].start()

    def need(self, *names):
        for name in names:
            if name in self.copies:
                self.copies.pop(name).wait()


class Departures:
    def __init__(self, sem):
        self.sem = sem
        self.copies = []

    def send(self, source, target):
        copy = pltpu.make_async_copy(source, target, self.sem.at[len(self.copies)])
        copy.start()
        self.copies.append(copy)

    def finish(self):
        for copy in self.copies:
            copy.wait()


def feed_kernel(
    gain_ref, ibias_ref, gib_ref, ct_h, n3_h, n3t_h, acc_h, dn3_h, after_h, w_f1_h, w_f2_h,
    y_ref, gkeep_out, two, small_out,
    gib, ibias, ct, n3, n3t, acc, dn3, after, w_f1, w_f2, gbuf, sem, g_sem,
):
    rows, width = ct.shape
    mine = halves_of(lax.axis_index("seq"))[0]
    steps = w_f2.shape[0] // width
    pairs = {"n3": (n3_h, n3)}
    w1, w2 = columns(w_f1_h, mine), rows_of(w_f2_h, mine)
    for j in range(steps):
        at = pl.ds(j * width, width)
        pairs["w1%d" % j] = (w1.at[:, at], w_f1.at[:, at])
        if j == 0:
            pairs["ct"] = (ct_h, ct)
        pairs["w2%d" % j] = (w2.at[at], w_f2.at[at])
        if j == 0:
            pairs.update(n3t=(n3t_h, n3t), acc=(acc_h, acc), dn3=(dn3_h, dn3))
    pairs["after"] = (after_h, after)
    arrivals = Arrivals(sem, **pairs)
    gain = gain_ref[...].astype(F32)
    gib[...] = gib_ref[...]
    ibias[...] = ibias_ref[...].astype(F32).reshape(ibias.shape)

    def ready(name, j):
        if name == "w1":
            arrivals.need("n3", "w1%d" % j)
        elif name == "w2":
            arrivals.need("ct", "w2%d" % j)
        else:
            arrivals.need(name)

    feed_half(mine, ready, ct, w_f1, w_f2, ibias, n3, n3t, acc, dn3, gib, gbuf, gkeep_out, g_sem)
    y_ref[...] = acc[...].astype(BF)
    arrivals.need("after")
    gain_grad = jnp.zeros((1, width), F32)
    shift_grad = jnp.zeros((1, width), F32)
    outer_grad = jnp.zeros((1, width), F32)
    chunk = 128
    for r in range(0, rows, chunk):
        at = slice(r, r + chunk)
        grad = dn3[at]
        back, rowed = norm_back(after[at], gain[2:3], grad)
        grown = ct[at].astype(F32)
        two[at] = grown + back
        gain_grad += jnp.sum(rowed, axis=0, keepdims=True)
        shift_grad += jnp.sum(grad, axis=0, keepdims=True)
        outer_grad += jnp.sum(grown, axis=0, keepdims=True)
    small_out[...] = jnp.zeros_like(small_out)
    for j in range(gib.shape[1] // width):
        small_out[j:j + 1] = gib[:, j * width:(j + 1) * width]
    small_out[8:9] = gain_grad
    small_out[9:10] = shift_grad
    small_out[10:11] = outer_grad


ANY = pl.BlockSpec(memory_space=pl.ANY)
VM = pl.BlockSpec(memory_space=pltpu.VMEM)
SM = pl.BlockSpec(memory_space=pltpu.SMEM)
V = pltpu.VMEM


def sems(count):
    return pltpu.SemaphoreType.DMA((count,))


def call(kernel, name, outs, in_specs, scratch, args, micros, out_specs=None, after=(), room=60):
    if after:
        args = (lax.optimization_barrier((args[0], *after))[0], *args[1:])
    return pl.pallas_call(
        kernel,
        out_shape=[jax.ShapeDtypeStruct(*o) for o in outs],
        in_specs=in_specs,
        out_specs=out_specs or [VM] * len(outs),
        scratch_shapes=scratch,
        compiler_params=pltpu.CompilerParams(vmem_limit_bytes=room * 2**20),
        cost_estimate=pl.CostEstimate(flops=int(micros * 1e9), bytes_accessed=int(micros * 3e6), transcendentals=0),
        name=name,
    )(*args)


def forward_call(ways, len_, x, xp, src, srcp, ct, gains, shifts, sbias, cbias, ibias, obias, weights):
    rows, width = x.shape
    srows = src.shape[0]
    nk, ns = ways * rows, ways * srows
    ff = weights[5].shape[1]
    rw = (rows, width)
    outs = [
        (((ff, width), BF), ANY), ((rw, F32), VM), ((rw, F32), VM), ((rw, BF), VM), (((width, rows), BF), VM),
        (((1, ff), F32), VM), ((rw, F32), VM),
        (((nk, width), BF), ANY), ((rw, BF), ANY), ((rw, BF), ANY), (((nk, width), BF), ANY), (((nk, width), BF), ANY),
        ((rw, BF), ANY), (((ns, width), BF), ANY), (((ns, width), BF), ANY),
        (((HEADS, nk, rows), BF), ANY), (((HEADS, ns, rows), BF), ANY),
        ((rw, F32), ANY), ((rw, F32), ANY), ((rw, BF), ANY), ((rw, BF), ANY), ((rw, F32), ANY),
    ]
    half = ff // 2
    peer = VM if ways == 2 else ANY
    slots = HEADS if ways == 2 else 2
    scratch = [V(w.shape, BF) for w in weights[:5]] + [V((width, half), BF), V((half, width), BF)] + [
        V(rw, BF), V(rw, BF), V((nk, width), BF), V((nk, width), BF),
        V((rows, PAIR), BF), V((nk, PAIR), BF), V((slots, nk, rows), BF), V(rw, BF), V(rw, F32),
        V(rw, F32), V(rw, BF), V(rw, BF), V((ns, width), BF), V((ns, width), BF), V((ns, PAIR), BF), V((slots, ns, rows), BF),
        V(rw, BF), V(rw, F32),
        V((2, width, width), BF), V((srows, width), BF), V((width, width), BF), V(rw, BF), V((1, ff), F32),
        sems(7), sems(slots), sems(slots), sems(16), sems(2), sems(2),
    ]
    return call(
        functools.partial(forward_kernel, ways), "forward", [o[0] for o in outs],
        [SM, VM, peer, VM, peer, VM] + [VM] * 6 + [ANY] * 7, scratch,
        (len_, x, xp, src, srcp, ct, gains, shifts, sbias, cbias, ibias, obias, *weights), 31, [o[1] for o in outs], room=60,
    )


def feed_call(ct, gains, ibias, n3, n3t, gib, acc, dn3, after, w_f1, w_f2):
    rw = ct.shape
    width = rw[1]
    ff = w_f1.shape[1]
    steps = ff // 2 // width
    return call(
        feed_kernel, "feed", [(rw, BF), ((ff, width), BF), (rw, F32), ((16, width), F32)],
        [VM] * 3 + [ANY] * 8,
        [V((1, ff), F32), V((1, ff), F32), V(rw, BF), V(rw, BF), V(n3t.shape, BF), V(rw, F32), V(rw, F32), V(rw, F32), V((width, ff // 2), BF),
         V((ff // 2, width), BF), V((4, width, width), BF), sems(6 + 2 * steps), sems(4)],
        (gains, ibias, gib, ct, n3, n3t, acc, dn3, after, w_f1, w_f2), 9, [VM, ANY, VM, VM],
    )


def attend_back(first, last, arrive, q_ref, k_ref, v_ref, gm_ref, recip_ref, mixed_ref, p_hbm, p_ref, sem, dq_ref, dk_ref, dv_ref):
    rows = q_ref.shape[0]
    keys = k_ref.shape[0]
    qlane = lax.broadcasted_iota(jnp.int32, (rows, PAIR), 1)
    klane = lax.broadcasted_iota(jnp.int32, (keys, PAIR), 1)

    qrow = lax.broadcasted_iota(jnp.int32, (PAIR, rows), 0)

    def fetch(pair, slot):
        return pltpu.make_async_copy(p_hbm.at[pl.ds(2 * pair, 2)], p_ref.at[slot], sem.at[slot])

    def one(pair, _):
        static = isinstance(pair, int)
        slot = (pair - first) % 2 if static else lax.rem(pair - first, 2)
        if static:
            if pair + 1 < last:
                fetch(pair + 1, 1 - slot).start()
        else:

            @pl.when(pair + 1 < last)
            def _():
                fetch(pair + 1, 1 - slot).start()

        lanes = pl.ds(pair * PAIR if static else pl.multiple_of(pair * PAIR, PAIR), PAIR)
        arrive(pair)
        qp = q_ref[:, lanes]
        kp = k_ref[:, lanes]
        vp = v_ref[:, lanes]
        kpt = kp.T
        dop = (gm_ref[:, lanes].astype(F32) * recip_ref[:, lanes]).astype(BF)
        prod = dop.astype(F32) * mixed_ref[:, lanes].astype(F32)
        fetch(pair, slot).wait()
        dqs, dks, dvs = [], [], []
        for h in (0, 1):
            inside = (qlane < HD) if h == 0 else (qlane >= HD)
            kinside = (klane < HD) if h == 0 else (klane >= HD)
            spare = HD * (1 - h)
            delta = jnp.sum(jnp.where(inside, prod, 0.0), axis=1, keepdims=True)
            high = delta.astype(BF).astype(F32)
            tail = jnp.where(qlane == spare, -high, jnp.where(qlane == spare + 1, high - delta, 0.0))
            doe = jnp.where(inside, dop, tail.astype(BF))
            ones = jnp.where((klane == spare) | (klane == spare + 1), 1.0, 0.0).astype(BF)
            ve = jnp.where(kinside, vp, ones)
            dpt = mm_t(ve, doe)
            p = p_ref[slot, h]
            dst = (p.astype(F32) * dpt).astype(BF)
            dvs.append(mm(p, dop))
            dks.append(mm(dst, qp))
            dqs.append(mm(kpt, dst))
        lanes = pl.ds((pair - first) * PAIR if static else pl.multiple_of((pair - first) * PAIR, PAIR), PAIR)
        dq_ref[:, lanes] = (jnp.where(qrow < HD, dqs[0], dqs[1]) * HD ** -0.5).astype(BF).T
        dk_ref[:, lanes] = jnp.where(klane < HD, dks[0], dks[1]).astype(BF)
        dv_ref[:, lanes] = jnp.where(klane < HD, dvs[0], dvs[1]).astype(BF)
        return 0

    fetch(first, 0).start()
    lax.fori_loop(first, last, one, 0)


def weight_halves(width, me, g, gkeep, gsend, departures, keep_out, send_out):
    half = width // 2
    keep, send = (pl.ds(pl.multiple_of(at * half, half), half) for at in halves_of(me))

    def put(i, value):
        at = slice(i * half, (i + 1) * half)
        g[...] = value.astype(BF)
        gkeep[at] = g[keep]
        gsend[at] = g[send]
        route(departures, gsend, i * half, half, send_out)
        route(departures, gkeep, i * half, half, keep_out)

    return put


def route(departures, ref, first, rows, outs):
    begin = 0
    for out in outs:
        end = begin + out.shape[0]
        low, high = max(first, begin), min(first + rows, end)
        if low < high:
            departures.send(ref.at[pl.ds(low, high - low)], out.at[pl.ds(low - begin, high - low)])
        begin = end


def norm_sums(small, begin, gain_grad, shift_grad):
    small[begin:begin + 1] = gain_grad
    small[begin + 1:begin + 2] = shift_grad


def cross_kernel(
    gain_ref, two_h, q_h, k_h, v_h, p_h, recip_h, mixed_h, one_h, w_cq_h, w_co_h, w_so_h,
    dq_out, dk_out, dv_out, btwo_out, bone_out, gm_out, oneg_out, small_out,
    two, q, k, v, p_buf, recip, mixed, one, w_cq, w_co, w_so, gm, dq, dk, dv, dn, btwo, bone, p_sem, sem, out_sem,
):
    rows, width = two.shape
    arrivals = Arrivals(
        sem, two=(two_h, two), w_co=(w_co_h, w_co), q=(q_h, q), k=(k_h, k), v=(v_h, v), recip=(recip_h, recip),
        mixed=(mixed_h, mixed), w_cq=(w_cq_h, w_cq), one=(one_h, one), w_so=(w_so_h, w_so))
    departures = Departures(out_sem)
    gain = gain_ref[...].astype(F32)
    small_out[...] = jnp.zeros_like(small_out)
    arrivals.need("two", "w_co")
    btwo[...] = two[...].astype(BF)
    departures.send(btwo, btwo_out)
    small_out[0:1] = column_sum(btwo[...])
    gm[...] = mm_t(btwo[...], w_co[...]).astype(BF)
    arrivals.need("q", "k", "v", "recip", "mixed")
    attend_back(0, HEADS // 2, lambda pair: None, q, k, v, gm, recip, mixed, p_h, p_buf, p_sem, dq, dk, dv)
    departures.send(dq, dq_out)
    departures.send(dk, dk_out)
    departures.send(dv, dv_out)
    small_out[1:2] = column_sum(dq[...])
    small_out[5:6] = column_sum(dv[...])
    arrivals.need("w_cq", "one")
    dn[...] = mm_t(dq[...], w_cq[...])
    chunk = 128
    gain_grad = jnp.zeros((1, width), F32)
    shift_grad = jnp.zeros((1, width), F32)
    for r in range(0, rows, chunk):
        at = slice(r, r + chunk)
        grad = dn[at]
        back, rowed = norm_back(one[at], gain[1:2], grad)
        total = two[at] + back
        one[at] = total
        bone[at] = total.astype(BF)
        gain_grad += jnp.sum(rowed, axis=0, keepdims=True)
        shift_grad += jnp.sum(grad, axis=0, keepdims=True)
    departures.send(one, oneg_out)
    departures.send(bone, bone_out)
    norm_sums(small_out, 2, gain_grad, shift_grad)
    small_out[4:5] = column_sum(bone[...])
    arrivals.need("w_so")
    gm[...] = mm_t(bone[...], w_so[...]).astype(BF)
    departures.send(gm, gm_out)
    departures.finish()


def cross_weights_kernel(
    dq_h, dk_h, dv_h, btwo_h, bone_h, src_h, srcp_h, n2_h, cmixed_h, mixed_h, w_ckv_h,
    keep_out, send_out, sgrad_out,
    dq, dk, dv, btwo, bone, src, n2, cmixed, mixed, w_ckv, g, gkeep, gsend, sgrad, sem, out_sem,
):
    rows, width = dq.shape
    srows = src_h.shape[0]
    me = lax.axis_index("seq")
    arrivals = Arrivals(
        sem, cmixed=(cmixed_h, cmixed), btwo=(btwo_h, btwo), n2=(n2_h, n2), dq=(dq_h, dq), mixed=(mixed_h, mixed), bone=(bone_h, bone),
        src=(src_h, src.at[pl.ds(0, srows)]), srcp=(srcp_h, src.at[pl.ds(srows, srcp_h.shape[0])]), dk=(dk_h, dk), dv=(dv_h, dv),
        w_ckv=(w_ckv_h, w_ckv))
    departures = Departures(out_sem)
    put = weight_halves(width, me, g, gkeep, gsend, departures, [keep_out], [send_out])
    for i, (left, right) in enumerate((("cmixed", "btwo"), ("n2", "dq"), ("mixed", "bone"))):
        arrivals.need(left, right)
        put(i, t_mm({"cmixed": cmixed, "n2": n2, "mixed": mixed}[left][...], {"btwo": btwo, "dq": dq, "bone": bone}[right][...]))
    arrivals.need("src", "srcp")
    for i, (name, ref) in enumerate((("dk", dk), ("dv", dv))):
        arrivals.need(name)
        put(3 + i, t_mm(src[...], ref[...]))
    arrivals.need("w_ckv")
    sgrad[...] = (mm_t(dk[...], w_ckv[:, 0:width]) + mm_t(dv[...], w_ckv[:, width:])).astype(BF)
    departures.send(sgrad, sgrad_out)
    departures.finish()


def self_kernel(
    first, last,
    q_h, k_h, v_h, p_h, recip_h, mixed_h, gm_h,
    dq, dk, dv,
    q, k, v, p_buf, recip, mixed, gm, p_sem, pair_sem,
):
    operands = ((q_h, q), (k_h, k), (v_h, v), (gm_h, gm), (recip_h, recip), (mixed_h, mixed))

    def lanes_of(pair):
        lanes = pl.ds(pair * PAIR if isinstance(pair, int) else pl.multiple_of(pair * PAIR, PAIR), PAIR)
        return [
            pltpu.make_async_copy(source.at[:, lanes], target.at[:, lanes], pair_sem.at[i, pair - first])
            for i, (source, target) in enumerate(operands)
        ]

    for pair in range(first, last):
        for copy in lanes_of(pair):
            copy.start()

    def arrive(pair):
        for copy in lanes_of(pair):
            copy.wait()

    attend_back(first, last, arrive, q, k, v, gm, recip, mixed, p_h, p_buf, p_sem, dq, dk, dv)


def self_weights_kernel(
    small1, small2, dq_one, dk_one, dv_one, dq_two, dk_two, dv_two, n1_h, x_h, xp_h, w_h,
    keep_one, keep_two, send_one, send_two, dn_out, dn_peer_out,
    dq, dk, dv, n1, x, w, g, gkeep, gsend, small, dn, dn_peer, sem, out_sem,
):
    rows, width = dq.shape
    nk = dk.shape[0]
    half = width // 2
    me = lax.axis_index("seq")
    begin, end = pl.ds(0, half), pl.ds(half, half)
    arrivals = Arrivals(
        sem, n1=(n1_h, n1), dq=(dq_one, dq.at[:, begin]), dq2=(dq_two, dq.at[:, end]), dk=(dk_one, dk.at[:, begin]), dk2=(dk_two, dk.at[:, end]),
        dv=(dv_one, dv.at[:, begin]), dv2=(dv_two, dv.at[:, end]), w=(w_h, w),
        xp=(xp_h, x.at[pl.ds(rows, nk - rows)]), x=(x_h, x.at[pl.ds(0, rows)]))
    departures = Departures(out_sem)
    keep_out, send_out = [keep_one, keep_two], [send_one, send_two]
    put = weight_halves(width, me, g, gkeep, gsend, departures, keep_out, send_out)
    arrivals.need("n1", "dq", "dq2")
    put(0, t_mm(n1[0:rows], dq[...]))
    arrivals.need("dk", "dk2")
    put(1, t_mm(n1[...], dk[...]))
    arrivals.need("dv", "dv2")
    put(2, t_mm(n1[...], dv[...]))
    arrivals.need("w", "x", "xp")
    gain_grad = jnp.zeros((1, width), F32)
    shift_grad = jnp.zeros((1, width), F32)
    chunk = 128
    for b in reversed(range(nk // rows)):
        at = slice(b * rows, (b + 1) * rows)
        grad = mm_t(dk[at], w[:, width:2 * width]) + mm_t(dv[at], w[:, 2 * width:])
        if b == 0:
            grad = grad + mm_t(dq[...], w[:, 0:width])
        dn[...] = grad
        if b == 0:
            departures.send(dn, dn_out)
        for r in range(0, rows, chunk):
            piece = dn[r:r + chunk]
            xhat = norm_parts(x[b * rows + r:b * rows + r + chunk].astype(F32))[0]
            gain_grad += jnp.sum(piece * xhat, axis=0, keepdims=True)
            shift_grad += jnp.sum(piece, axis=0, keepdims=True)
        if b > 0:
            dn_peer[(b - 1) * rows:b * rows] = dn[...].astype(BF)
            there = pl.ds((b - 1) * rows, rows)
            departures.send(dn_peer.at[there], dn_peer_out.at[there])
    small[...] = jnp.zeros_like(small)
    norm_sums(small, 0, gain_grad, shift_grad)
    small[2:3] = column_sum(dq[...])
    small[3:4] = column_sum(dv[...])
    small[8:16] = small2[...]
    small[16:32] = small1[...]
    for side, ref, out in zip(halves_of(me), (gkeep, gsend), (keep_out, send_out)):
        ref[3 * half:3 * half + 16] = small[pl.ds(pl.multiple_of(side * 16, 16), 16)].astype(BF)
        ref[3 * half + 16:] = jnp.zeros((16, width), BF)
        route(departures, ref, 3 * half, 32, out)
    departures.finish()


def last_kernel(x_ref, gain_ref, dn_ref, came_ref, oneg_ref, xgrad):
    gain = gain_ref[...].astype(F32)
    chunk = 128
    for r in range(0, x_ref.shape[0], chunk):
        at = slice(r, r + chunk)
        grad = dn_ref[at]
        for b in range(came_ref.shape[0]):
            grad = grad + came_ref[b, at].astype(F32)
        back = norm_back(x_ref[at].astype(F32), gain[0:1], grad)[0]
        xgrad[at] = (oneg_ref[at] + back).astype(BF)


def cross_call(gains, two, q, k, v, p, recip, mixed, one, w_cq, w_co, w_so):
    rows, width = two.shape
    ns = k.shape[0]
    rw, ww, nw = (rows, width), (width, width), (ns, width)
    outs = [(rw, BF), (nw, BF), (nw, BF), (rw, BF), (rw, BF), (rw, BF), (rw, F32), ((8, width), F32)]
    scratch = [V(rw, F32), V(rw, BF), V(nw, BF), V(nw, BF), V((2, 2, ns, rows), BF), V(rw, F32), V(rw, BF), V(rw, F32),
               V(ww, BF), V(ww, BF), V(ww, BF), V(rw, BF), V(rw, BF), V(nw, BF), V(nw, BF), V(rw, F32), V(rw, BF), V(rw, BF),
               sems(2), sems(10), sems(7)]
    return call(cross_kernel, "cross_back", outs, [VM] + [ANY] * 11, scratch,
                (gains, two, q, k, v, p, recip, mixed, one, w_cq, w_co, w_so), 11, [ANY] * 7 + [VM])


def cross_weights_call(dq, dk, dv, btwo, bone, src, srcp, n2, cmixed, mixed, w_ckv):
    rows, width = dq.shape
    rw, ww, nw = (rows, width), (width, width), dk.shape
    half = (5 * width // 2, width)
    scratch = [V(rw, BF), V(nw, BF), V(nw, BF), V(rw, BF), V(rw, BF), V(nw, BF), V(rw, BF), V(rw, BF), V(rw, BF), V((width, 2 * width), BF),
               V(ww, BF), V(half, BF), V(half, BF), V(nw, BF), sems(11), sems(11)]
    return call(cross_weights_kernel, "cross_weights", [(half, BF), (half, BF), (nw, BF)], [ANY] * 11, scratch,
                (dq, dk, dv, btwo, bone, src, srcp, n2, cmixed, mixed, w_ckv), 6, [ANY] * 3)


def self_call(first, last, name, q, k, v, p, recip, mixed, gm):
    rows, width = q.shape
    nk = k.shape[0]
    rw, nw = (rows, width), (nk, width)
    size = (last - first) * PAIR
    scratch = [V(rw, BF), V(nw, BF), V(nw, BF), V((2, 2, nk, rows), BF), V(rw, F32), V(rw, BF), V(rw, BF),
               sems(2), pltpu.SemaphoreType.DMA((6, last - first))]
    return call(functools.partial(self_kernel, first, last), name, [((rows, size), BF), ((nk, size), BF), ((nk, size), BF)],
                [ANY] * 7, scratch, (q, k, v, p, recip, mixed, gm), 7)


def self_weights_call(small1, small2, grads, n1, x, xp, w):
    rows, width = x.shape
    nk = n1.shape[0]
    rw, nw, pw = (rows, width), (nk, width), (nk - rows, width)
    half = (3 * width // 2 + 32, width)
    part = (half[0] // 2, width)
    scratch = [V(rw, BF), V(nw, BF), V(nw, BF), V(nw, BF), V(nw, BF), V(w.shape, BF), V((width, width), BF), V(half, BF), V(half, BF),
               V((32, width), F32), V(rw, F32), V(pw, BF), sems(10), sems(14 + nk // rows)]
    return call(self_weights_kernel, "self_weights", [(part, BF)] * 4 + [(rw, F32), (pw, BF)], [VM] * 2 + [ANY] * 10, scratch,
                (small1, small2, *grads, n1, x, xp, w), 7, [ANY] * 6)


def last_call(x, gains, dn, came, oneg, after):
    return call(last_kernel, "last_back", [(x.shape, BF)], [VM] * 5, [], (x, gains, dn, came, oneg), 3, after=after, room=12)[0]


def feed_plan(ff, width):
    per = ff // width // 2
    moves = []
    for j in range(per):
        moves.append((2 * j * width, width, 0, (0, 0), (j * width, per * width)))
        moves.append(((2 * j + 1) * width, width, 1, (j * width, per * width), (0, 0)))
    return [(width, ff), (ff, width)], moves


def cross_plan(width):
    part = width // 2
    places = ((0, 0), (1, 0), (2, 0), (3, 0), (3, width))
    return [(width, width)] * 3 + [(width, 2 * width)], [
        (i * part, part, out, (0, part), (column, 0)) for i, (out, column) in enumerate(places)]


def last_plan(width):
    part = width // 2
    return [(width, 3 * width)], [(i * part, part, 0, (0, part), (i * width, 0)) for i in range(3)]


def unpack_kernel(moves, finish, count, where, *refs):
    parts = refs[:4]
    outs = refs[4:4 + count]
    more = refs[4 + count:-4]
    full, buf, in_sem, out_sem = refs[-4:]
    size = parts[0].shape[0]
    slots, _, width = buf.shape
    own = where[0]
    loads = []
    for i, part in enumerate(parts):
        side = where[1 + i // 2]
        at = pl.ds(pl.multiple_of((side if i % 2 == 0 else 1 - side) * size, 16), size)
        loads.append(pltpu.make_async_copy(part, full.at[i // 2, at], in_sem.at[i]))
    for load in loads:
        load.start()
    stores = []
    for turn, half in enumerate((own, 1 - own)):
        loads[2 * turn].wait()
        loads[2 * turn + 1].wait()
        for first, rows, out, (row, down), (column, right) in moves:
            slot = len(stores) % slots
            if len(stores) >= slots:
                stores[len(stores) - slots].wait()
            buf[slot, 0:rows] = full[turn, first:first + rows].astype(F32)
            to_rows = pl.ds(pl.multiple_of(row + half * down, 16), rows)
            to_columns = pl.ds(pl.multiple_of(column + half * right, 128), width)
            copy = pltpu.make_async_copy(buf.at[slot, pl.ds(0, rows)], outs[out].at[to_rows, to_columns], out_sem.at[slot])
            copy.start()
            stores.append(copy)
    if finish is not None:
        finish(full, own, more)
    for copy in stores[-slots:]:
        copy.wait()


def finish_small(begin, full, own, outs):
    gains, shifts, sbias, cbias, inner, outer = outs
    rows = slice(begin, begin + 16)
    low = full[own, rows].astype(F32)
    high = full[1 - own, rows].astype(F32)
    width = low.shape[1]
    for i, (g, s, value) in enumerate(((0, 1, low), (10, 11, low), (8, 9, high))):
        gains[i:i + 1] = value[g:g + 1]
        shifts[i:i + 1] = value[s:s + 1]
    for i, (a, b) in enumerate(((2, 9), (3, 13), (12, 8))):
        sbias[i:i + 1] = low[a:a + 1]
        cbias[i:i + 1] = low[b:b + 1]
    for j in range(inner.shape[0] // width):
        inner[j * width:(j + 1) * width] = high[j]
    outer[...] = high[10]


def unpack_call(where, parts, name, plan, micros, finish=None, more=()):
    shapes, moves = plan
    size, width = parts[0].shape
    most = max(move[1] for move in moves)
    slots = min(6, 2 * len(moves))
    scratch = [V((2, 2 * size, width), BF), V((slots, most, width), F32), sems(4), sems(slots)]
    outs = [(shape, F32) for shape in list(shapes) + list(more)]
    return call(functools.partial(unpack_kernel, moves, finish, len(shapes)), name, outs, [SM] + [ANY] * 4, scratch,
                (where, *parts), micros, [ANY] * len(shapes) + [VM] * len(more), room=24)


def ring(value, axis, shift):
    size = lax.axis_size(axis)
    return lax.ppermute(value, axis, [(i, (i + shift) % size) for i in range(size)])


def add(left, right):
    return (left.astype(F32) + right.astype(F32)).astype(BF)


def steps_of():
    rest = [("seq", 1 << b) for b in range(1, lax.axis_size("seq").bit_length() - 1)]
    dp = [("dp", 1 << b) for b in range(lax.axis_size("dp").bit_length() - 1)]
    near, far_off = dp[:2], dp[2:]
    halving = list(zip(near, near[::-1]))
    whole = [(step, step) for step in rest] + list(zip(far_off[::-1], far_off))
    return halving, whole


def flip(value, step):
    ways = lax.axis_size("seq")
    pairs = []
    for i in range(lax.axis_size("dp")):
        for s in range(ways):
            axis, bit = step[s % 2]
            to = (i ^ bit) * ways + s if axis == "dp" else i * ways + (s ^ bit)
            pairs.append((i * ways + s, to))
    return lax.ppermute(value, ("dp", "seq"), pairs)


def flip_core(value):
    return flip(value, (("seq", 1), ("seq", 1)))


def side_of(step):
    sides = [lax.axis_index(axis) // bit % 2 for axis, bit in step]
    return jnp.where(lax.axis_index("seq") % 2 == 0, sides[0], sides[1])


def scatter_step(mine, came, step):
    side = side_of(step)
    half = mine.shape[0] // 2

    def take(value, at):
        return lax.dynamic_index_in_dim(value.reshape(2, half, value.shape[1]), at, 0, keepdims=False)

    send = add(take(mine, 1 - side), take(came, 1 - side))
    return add(take(mine, side), take(came, side)), send, flip(send, step)


def scatter_pair(mine, came, step):
    side = side_of(step)

    def take(pair, at):
        return jnp.where(at == 0, pair[0], pair[1])

    send = add(take(mine, 1 - side), take(came, 1 - side))
    return add(take(mine, side), take(came, side)), send, flip(send, step)


def joined(mine, came, step):
    return jnp.where(side_of(step) == 0, jnp.concatenate([mine, came]), jnp.concatenate([came, mine]))


def places(step):
    parity = lax.axis_index("seq") % 2
    sides = [lax.axis_index(axis) // bit % 2 for axis, bit in step]
    own = jnp.where(parity == 0, sides[0], sides[1])
    other = jnp.where(parity == 0, sides[1], sides[0])
    return jnp.stack([parity, own, other]).astype(jnp.int32)


def tie(value, *others):
    return lax.optimization_barrier((value, *others))[0]


def local(
    layer_input, source_states, source_lengths, cotangent, norm_gain, norm_bias, self_in, self_bias, self_out,
    cross_query, cross_keyval, cross_bias, cross_out, feed_in, inner_bias, feed_out, outer_bias,
):
    ways = lax.axis_size("seq")
    x = layer_input[0]
    source = source_states[0]
    ct = cotangent[0]
    rows, width = x.shape
    srows = source.shape[0]
    xp = jnp.concatenate([ring(x, "seq", -b) for b in range(1, ways)])
    srcp = jnp.concatenate([ring(source, "seq", -b) for b in range(1, ways)])
    (gsend, acc, dn3, n3, n3t, gib, after, n1, n2, q, k, v, cq, ck, cv, p, cp, recip, crecip, mixed, cmixed, one) = forward_call(
        ways, source_lengths, x, xp, source, srcp, ct, norm_gain, norm_bias, self_bias, cross_bias,
        inner_bias, outer_bias,
        (self_in, self_out, cross_query, cross_keyval, cross_out, feed_in, feed_out),
    )
    halving, whole = steps_of()
    first, second = halving
    feed_came = flip_core(gsend)
    y, gkeep, two, small1 = feed_call(ct, norm_gain, inner_bias, n3, n3t, gib, acc, dn3, after, feed_in, feed_out)
    feed, feed_sent, feed_came = scatter_step(gkeep, tie(feed_came, two), first)
    cdq, cdk, cdv, btwo, bone, gm, oneg, small2 = cross_call(
        norm_gain, tie(two, feed_sent), cq, ck, cv, cp, crecip, cmixed, one, cross_query, cross_out, self_out)
    feed, feed_sent, feed_came = scatter_step(feed, tie(feed_came, gm), second)
    ckeep, csend, sgrad = cross_weights_call(
        tie(cdq, feed_sent), cdk, cdv, btwo, bone, source, srcp, n2, cmixed, mixed, cross_keyval)
    cross_came = flip_core(csend)
    feed = add(feed, tie(feed_came, csend))
    feed_came = flip(feed, whole[0])
    part = HEADS // 4
    grads = self_call(0, part, "self_back_one", q, k, v, p, recip, mixed, tie(gm, feed))
    cross, cross_sent, cross_came = scatter_step(ckeep, tie(cross_came, grads[0]), first)
    more = self_call(part, 2 * part, "self_back_two", q, k, v, p, recip, mixed, tie(gm, cross_sent))
    feed = add(feed, tie(feed_came, more[0]))
    for step in whole[1:-1]:
        feed = add(feed, flip(feed, step))
    feed_came = flip(feed, whole[-1])
    cross, cross_sent, cross_came = scatter_step(cross, tie(cross_came, feed), second)
    *lasts, dn, dn_peer = self_weights_call(
        small1, small2, (*grads, tie(more[0], feed, cross_sent), *more[1:]), n1, x, xp, self_in)
    last_came = [flip_core(half) for half in lasts[2:]]
    dn_came = jnp.stack([ring(dn_peer[(b - 1) * rows:b * rows], "seq", b) for b in range(1, ways)])
    for b in range(1, ways):
        sgrad_came = ring(sgrad[b * srows:(b + 1) * srows], "seq", b).astype(F32)
        total = sgrad_came if b == 1 else total + sgrad_came
    sgrad = (sgrad[:srows].astype(F32) + total).astype(BF)
    cross = add(cross, tie(cross_came, dn))
    cross_came = flip(cross, whole[0])
    feed = add(feed, tie(feed_came, cross))
    feed_came = flip(feed, second)
    last, last_sent, last_came = scatter_pair(lasts[:2], lax.optimization_barrier((*last_came, feed)), first)
    last, last_sent, last_came = scatter_step(last, last_came, second)
    feed = joined(feed, tie(feed_came, last_sent), second)
    feed_came = flip(feed, first)
    feed_other = flip_core(feed)
    xgrad = last_call(x, norm_gain, dn, dn_came, oneg, (feed,))
    last = add(last, tie(last_came, xgrad))
    last_came = flip(last, whole[0])
    cross = add(cross, tie(cross_came, last))
    for step in whole[1:-1]:
        cross = add(cross, flip(cross, step))
    cross_came = flip(cross, whole[-1])
    last = add(last, tie(last_came, cross))
    for step in whole[1:-1]:
        last = add(last, flip(last, step))
    last_came = flip(last, whole[-1])
    cross = add(cross, tie(cross_came, last))
    cross_came = flip(cross, second)
    feed_came = tie(feed_came, cross)
    feed_last = flip_core(feed_came)
    where = places(first)
    last = add(last, tie(last_came, feed_came))
    last_came = flip(last, second)
    cross = joined(cross, tie(cross_came, last), second)
    cross_came = flip(cross, first)
    cross_other = flip_core(cross)
    g_feed_in, g_feed_out = unpack_call(
        where, (feed, feed_came, feed_other, tie(feed_last, cross)), "feed_unpack", feed_plan(feed_in.shape[1], width), 5)
    last = joined(last, tie(last_came, g_feed_in), second)
    last_came = flip(last, first)
    last_other = flip_core(last)
    cross_came = tie(cross_came, last)
    cross_last = flip_core(cross_came)
    g_cross_out, g_cross_query, g_self_out, g_keyval = unpack_call(
        where, (cross, cross_came, cross_other, cross_last), "cross_unpack", cross_plan(width), 3)
    last_last = flip_core(tie(last_came, g_keyval))
    g_self_in, *small = unpack_call(
        where, (last, last_came, last_other, last_last), "last_unpack", last_plan(width), 3,
        functools.partial(finish_small, 3 * width // 2), [(3, width)] * 4 + [inner_bias.shape, outer_bias.shape])
    g_gain, g_shift, g_self_bias, g_cross_bias, g_inner, g_outer = small
    return (
        y[None], xgrad[None], sgrad[None], g_gain, g_shift, g_self_in, g_self_bias, g_self_out, g_cross_query, g_keyval, g_cross_bias,
        g_cross_out, g_feed_in, g_inner, g_feed_out, g_outer,
    )


def solution(mesh):
    split = P("dp", "seq", None)
    in_specs = (split, split, P("dp", None), split) + (P(),) * 13
    out_specs = (split,) * 3 + (P(),) * 13
    return jax.shard_map(local, mesh=mesh, in_specs=in_specs, out_specs=out_specs, check_vma=False)
```

```python
import functools
import jax
import jax.numpy as jnp
from jax import lax
from jax.experimental import pallas as pl
from jax.experimental.pallas import tpu as pltpu
from jax.sharding import PartitionSpec as P

HEADS = 8
HD = 64
PAIR = 2 * HD
eps = 1e-05
far = -1e30
BF = jnp.bfloat16
F32 = jnp.float32


def mm(left, right):
    return lax.dot_general(left, right, (((1,), (0,)), ((), ())), preferred_element_type=F32)


def mm_t(left, right):
    return lax.dot_general(left, right, (((1,), (1,)), ((), ())), preferred_element_type=F32)


def t_mm(left, right):
    return lax.dot_general(left, right, (((0,), (0,)), ((), ())), preferred_element_type=F32)


def norm_parts(values):
    center = values - jnp.mean(values, axis=-1, keepdims=True)
    spread = jnp.mean(center * center, axis=-1, keepdims=True)
    rate = lax.rsqrt(spread + eps)
    return center * rate, rate


def norm_rows(values, gain, shift):
    return norm_parts(values)[0] * gain + shift


def norm_back(values, gain, grad):
    xhat, rate = norm_parts(values)
    e = grad * gain
    back = rate * (
        e - jnp.mean(e, axis=-1, keepdims=True) - xhat * jnp.mean(e * xhat, axis=-1, keepdims=True)
    )
    return back, grad * xhat


def sentence_lanes(lengths, factor, shape):
    lane = lax.broadcasted_iota(jnp.int32, shape, 1) % HD
    begin = jnp.zeros(shape, jnp.int32)
    end = jnp.zeros(shape, jnp.int32)
    total = jnp.int32(0)
    for n in range(lengths.shape[1]):
        after = total + factor * lengths[0, n]
        begin = jnp.where(lane == n, total, begin)
        end = jnp.where(lane == n, after, end)
        total = after
    return begin, end


def sentence_hits(lengths, factor, first, rows):
    begin, end = sentence_lanes(lengths, factor, (1, PAIR))
    place = lax.broadcasted_iota(jnp.int32, (rows, PAIR), 0) + first
    return jnp.where((place >= begin) & (place < end), 1.0, 0.0)


def sentence_far(lengths, hits):
    lane = lax.broadcasted_iota(jnp.int32, hits.shape, 1) % HD
    return jnp.where(lane < lengths.shape[1], (1.0 - hits) * far, 0.0)


def gelu_parts(v):
    c = 0.7978845608028654
    square = v * v
    t = jnp.tanh(c * (v + 0.044715 * (square * v)))
    half = 0.5 * (1.0 + t)
    slope = half + (0.5 * v) * (1.0 - t * t) * (c * (1.0 + 3 * 0.044715 * square))
    return v * half, slope


def swap_heads(width):
    row = lax.broadcasted_iota(jnp.int32, (width, width), 0) // HD
    column = lax.broadcasted_iota(jnp.int32, (width, width), 1) // HD
    return jnp.where((row != column) & (row // 2 == column // 2), 1.0, 0.0).astype(BF)


def score_bound(q_ref, k_ref, swap_ref, lift_ref):
    most = jnp.max(jnp.abs(k_ref[...]).astype(F32), axis=0, keepdims=True)
    size = (jnp.abs(q_ref[...]).astype(F32) * most).astype(BF)
    lift_ref[...] = (-1.02 * mm(size, swap_ref[...])).astype(BF)


def attend(q_ref, k_ref, v_ref, qfar_ref, khit_ref, lift_ref, p_ref, p_out, sem, mixed_ref, recip_ref):
    rows = q_ref.shape[0]
    keys = k_ref.shape[0]
    slots = p_ref.shape[0]
    qlane = lax.broadcasted_iota(jnp.int32, (rows, PAIR), 1) < HD
    klane = lax.broadcasted_iota(jnp.int32, (keys, PAIR), 1) < HD
    vrow = lax.broadcasted_iota(jnp.int32, (PAIR, keys), 0) < HD

    def copy(n, slot):
        return pltpu.make_async_copy(p_ref.at[slot], p_out.at[n], sem.at[slot])

    def one(pair, exact, reuse):
        lanes = pl.ds(pair * PAIR if isinstance(pair, int) else pl.multiple_of(pair * PAIR, PAIR), PAIR)
        qp = q_ref[:, lanes]
        kp = k_ref[:, lanes]
        vpt = v_ref[:, lanes].T
        rest = qfar_ref[...] if exact else qfar_ref[...] + lift_ref[:, lanes]
        outs = []
        for h in (0, 1):
            qe = jnp.where(qlane if h == 0 else ~qlane, qp, rest)
            ke = jnp.where(klane if h == 0 else ~klane, kp, khit_ref[...])
            st = mm_t(ke, qe)
            if exact:
                st = st - jnp.max(st, axis=0, keepdims=True)
            p = jnp.exp(st).astype(BF)
            n = 2 * pair + h
            slot = n if slots == HEADS else h
            if reuse is not None:
                pl.when(reuse)(lambda n=n, slot=slot: copy(n, slot).wait())
            p_ref[slot] = p
            copy(n, slot).start()
            ve = jnp.where(vrow if h == 0 else ~vrow, vpt, jnp.ones_like(vpt))
            outs.append(mm(ve, p).T)
        value = jnp.where(qlane, outs[0], outs[1])
        total = jnp.where(qlane, outs[1], outs[0])
        recip = 1.0 / pltpu.roll(total, HD, 1)
        mixed_ref[:, lanes] = (value * recip).astype(BF)
        recip_ref[:, lanes] = recip
        return jnp.min(total.reshape(rows // 8, 8, PAIR), axis=0)

    least = lax.fori_loop(
        0, HEADS // 2, lambda pair, low: jnp.minimum(low, one(pair, False, None if slots == HEADS else pair > 0)),
        jnp.full((8, PAIR), 1.0, F32))

    @pl.when(jnp.logical_not(jnp.min(least) > 1e-18))
    def _():
        for slot in range(slots):
            copy(slot, slot).wait()

        def again(pair, _):
            one(pair, True, pair > 0 if slots < HEADS else None)
            return 0

        lax.fori_loop(0, HEADS // 2, again, 0)


def drain(p_ref, p_out, sem):
    for slot in range(p_ref.shape[0]):
        pltpu.make_async_copy(p_ref.at[slot], p_out.at[slot], sem.at[slot]).wait()


def feed_half(half, ready, ct_ref, w1, w2, ibias_ref, n3, n3t, acc, dn3, gib, gbuf, gout, g_sem):
    width = n3.shape[1]
    steps = w2.shape[0] // width
    begun = []
    for j in range(steps):
        at = slice(j * width, (j + 1) * width)
        wide = pl.ds(pl.multiple_of((half * steps + j) * width, width), width)
        ready("w1", j)
        hidden = mm(n3[...], w1[:, at]) + ibias_ref[:, wide]
        acted, slope = gelu_parts(hidden)
        acted = acted.astype(BF)
        ready("w2", j)
        gh = (mm_t(ct_ref[...], w2[at]) * slope).astype(BF)
        gib[:, wide] = column_sum(gh)
        ready("n3t", j)
        for i, product in enumerate((lambda: mm(n3t[...], gh), lambda: t_mm(acted, ct_ref[...]))):
            slot = (2 * j + i) % gbuf.shape[0]
            if len(begun) >= gbuf.shape[0]:
                begun[len(begun) - gbuf.shape[0]].wait()
            gbuf[slot] = product().astype(BF)
            copy = pltpu.make_async_copy(gbuf.at[slot], gout.at[pl.ds((2 * j + i) * width, width)], g_sem.at[slot])
            copy.start()
            begun.append(copy)
        ready("acc", j)
        acc[...] += mm(acted, w2[at])
        ready("dn3", j)
        dn3[...] += mm_t(gh, w1[:, at])
    for copy in begun[-gbuf.shape[0]:]:
        copy.wait()


def column_sum(block):
    return jnp.sum(block.astype(F32), axis=0, keepdims=True)


def start_all(pairs, sem):
    copies = [pltpu.make_async_copy(a, b, sem.at[i]) for i, (a, b) in enumerate(pairs)]
    for copy in copies:
        copy.start()
    return copies


def halves_of(me):
    return lax.rem(me, 2), 1 - lax.rem(me, 2)


def columns(ref, half):
    size = ref.shape[1] // 2
    return ref.at[:, pl.ds(pl.multiple_of(half * size, size), size)]


def rows_of(ref, half):
    size = ref.shape[0] // 2
    return ref.at[pl.ds(pl.multiple_of(half * size, size), size)]


def forward_kernel(
    ways,
    len_ref, x_ref, xp_ref, src_ref, srcp_ref, ct_ref,
    gain_ref, shift_ref, sbias_ref, cbias_ref, ibias_ref, obias_ref,
    w_in_h, w_so_h, w_cq_h, w_ckv_h, w_co_h, w_f1_h, w_f2_h,
    gsend_out, acc, dn3, n3, n3t, gib, after, n1_out, n2_out, q_out, k_out, v_out, cq_out, ck_out, cv_out,
    p_out, cp_out, recip_out, crecip_out, mixed_out, cmixed_out, one_out,
    w_in, w_so, w_cq, w_ckv, w_co, w_f1, w_f2,
    n1, q, k, v, qfar, khit, p_buf, mixed, recip, one, n2, cq, ck, cv, shit, cp_buf, cmixed, crecip,
    gbuf, srcb, swap, lift, ibias, w_sem, p_sem, cp_sem, o_sem, g_sem, x_sem,
):
    rows, width = x_ref.shape
    me = lax.axis_index("seq")
    other = halves_of(me)[1]
    weights = [
        (w_in_h, w_in), (w_so_h, w_so), (w_cq_h, w_cq), (w_ckv_h, w_ckv), (w_co_h, w_co),
        (columns(w_f1_h, other), w_f1), (rows_of(w_f2_h, other), w_f2),
    ]
    loads = [pltpu.make_async_copy(a, b, w_sem.at[i]) for i, (a, b) in enumerate(weights)]
    src_rows = src_ref.shape[0]

    def peers(b):
        return (
            pltpu.make_async_copy(xp_ref.at[pl.ds((b - 1) * rows, rows)], n3, x_sem.at[0]),
            pltpu.make_async_copy(srcp_ref.at[pl.ds((b - 1) * src_rows, src_rows)], srcb, x_sem.at[1]),
        )

    loads[0].start()
    for load in peers(1):
        load.start()
    for load in loads[1:]:
        load.start()
    ibias[...] = ibias_ref[...].astype(F32).reshape(ibias.shape)
    gain = gain_ref[...].astype(F32)
    shift = shift_ref[...].astype(F32)
    sbias = sbias_ref[...].astype(F32)
    cbias = cbias_ref[...].astype(F32)
    stores = []

    def store(src, dst):
        copy = pltpu.make_async_copy(src, dst, o_sem.at[len(stores)])
        copy.start()
        stores.append(copy)

    chunk = 128
    for r in range(0, rows, chunk):
        n1[r:r + chunk] = norm_rows(x_ref[r:r + chunk].astype(F32), gain[0:1], shift[0:1]).astype(BF)
    store(n1, n1_out.at[0:rows])
    for b in range(ways):
        at = lax.rem(me + b, ways)
        khit[b * rows:(b + 1) * rows] = sentence_hits(len_ref, 2, at * rows, rows).astype(BF)
        shit[b * src_rows:(b + 1) * src_rows] = sentence_hits(len_ref, 1, at * src_rows, src_rows).astype(BF)
    qfar[...] = sentence_far(len_ref, khit[0:rows].astype(F32)).astype(BF)

    loads[0].wait()
    q[...] = ((mm(n1[...], w_in[:, 0:width]) + sbias[0:1]) * HD ** -0.5).astype(BF)
    for b in range(ways):
        at = slice(b * rows, (b + 1) * rows)
        rowed = n1
        if b > 0:
            rowed = n3
            peers(b)[0].wait()
            for r in range(0, rows, chunk):
                block = n3[r:r + chunk].astype(F32)
                n3[r:r + chunk] = norm_rows(block, gain[0:1], shift[0:1]).astype(BF)
            nsave = pltpu.make_async_copy(n3, n1_out.at[at], x_sem.at[0])
            nsave.start()
        k[at] = mm(rowed[...], w_in[:, width:2 * width]).astype(BF)
        v[at] = (mm(rowed[...], w_in[:, 2 * width:]) + sbias[1:2]).astype(BF)
        if b > 0:
            nsave.wait()
        if 0 < b < ways - 1:
            peers(b + 1)[0].start()
    store(q, q_out)
    store(k, k_out)
    store(v, v_out)
    swap[...] = swap_heads(width)
    score_bound(q, k, swap, lift)
    attend(q, k, v, qfar, khit, lift, p_buf, p_out, p_sem, mixed, recip)
    store(recip, recip_out)
    store(mixed, mixed_out)

    loads[1].wait()
    one[...] = x_ref[...].astype(F32) + mm(mixed[...], w_so[...]) + sbias[2:3]
    for r in range(0, rows, chunk):
        n2[r:r + chunk] = norm_rows(one[r:r + chunk], gain[1:2], shift[1:2]).astype(BF)
    store(one, one_out)
    store(n2, n2_out)
    loads[2].wait()
    cq[...] = ((mm(n2[...], w_cq[...]) + cbias[0:1]) * HD ** -0.5).astype(BF)
    loads[3].wait()
    for b in range(ways):
        if b > 0:
            peers(b)[1].wait()
        source = src_ref[...] if b == 0 else srcb[...]
        at = slice(b * src_rows, (b + 1) * src_rows)
        ck[at] = mm(source, w_ckv[:, 0:width]).astype(BF)
        cv[at] = (mm(source, w_ckv[:, width:]) + cbias[1:2]).astype(BF)
        if 0 < b < ways - 1:
            peers(b + 1)[1].start()
    store(cq, cq_out)
    store(ck, ck_out)
    store(cv, cv_out)
    score_bound(cq, ck, swap, lift)
    attend(cq, ck, cv, qfar, shit, lift, cp_buf, cp_out, cp_sem, cmixed, crecip)
    store(crecip, crecip_out)
    store(cmixed, cmixed_out)

    loads[4].wait()
    after[...] = one[...] + mm(cmixed[...], w_co[...]) + cbias[2:3]
    for r in range(0, rows, chunk):
        n3[r:r + chunk] = norm_rows(after[r:r + chunk], gain[2:3], shift[2:3]).astype(BF)
    n3t[...] = n3[...].T
    acc[...] = after[...] + obias_ref[...].astype(F32).reshape(1, width)
    dn3[...] = jnp.zeros_like(dn3)
    gib[...] = jnp.zeros_like(gib)
    loads[5].wait()
    loads[6].wait()
    feed_half(other, lambda name, step: None, ct_ref, w_f1, w_f2, ibias, n3, n3t, acc, dn3, gib, gbuf, gsend_out, g_sem)
    drain(p_buf, p_out, p_sem)
    drain(cp_buf, cp_out, cp_sem)
    for copy in stores:
        copy.wait()


class Arrivals:
    def __init__(self, sem, **pairs):
        self.copies = {}
        for i, (name, (source, target)) in enumerate(pairs.items()):
            self.copies[name] = pltpu.make_async_copy(source, target, sem.at[i])
            self.copies[name].start()

    def need(self, *names):
        for name in names:
            if name in self.copies:
                self.copies.pop(name).wait()


class Departures:
    def __init__(self, sem):
        self.sem = sem
        self.copies = []

    def send(self, source, target):
        copy = pltpu.make_async_copy(source, target, self.sem.at[len(self.copies)])
        copy.start()
        self.copies.append(copy)

    def finish(self):
        for copy in self.copies:
            copy.wait()


def feed_kernel(
    gain_ref, ibias_ref, gib_ref, ct_h, n3_h, n3t_h, acc_h, dn3_h, after_h, w_f1_h, w_f2_h,
    y_ref, gkeep_out, two, small_out,
    gib, ibias, ct, n3, n3t, acc, dn3, after, w_f1, w_f2, gbuf, sem, g_sem,
):
    rows, width = ct.shape
    mine = halves_of(lax.axis_index("seq"))[0]
    steps = w_f2.shape[0] // width
    pairs = {"n3": (n3_h, n3)}
    w1, w2 = columns(w_f1_h, mine), rows_of(w_f2_h, mine)
    for j in range(steps):
        at = pl.ds(j * width, width)
        pairs["w1%d" % j] = (w1.at[:, at], w_f1.at[:, at])
        if j == 0:
            pairs["ct"] = (ct_h, ct)
        pairs["w2%d" % j] = (w2.at[at], w_f2.at[at])
        if j == 0:
            pairs.update(n3t=(n3t_h, n3t), acc=(acc_h, acc), dn3=(dn3_h, dn3))
    pairs["after"] = (after_h, after)
    arrivals = Arrivals(sem, **pairs)
    gain = gain_ref[...].astype(F32)
    gib[...] = gib_ref[...]
    ibias[...] = ibias_ref[...].astype(F32).reshape(ibias.shape)

    def ready(name, j):
        if name == "w1":
            arrivals.need("n3", "w1%d" % j)
        elif name == "w2":
            arrivals.need("ct", "w2%d" % j)
        else:
            arrivals.need(name)

    feed_half(mine, ready, ct, w_f1, w_f2, ibias, n3, n3t, acc, dn3, gib, gbuf, gkeep_out, g_sem)
    y_ref[...] = acc[...].astype(BF)
    arrivals.need("after")
    gain_grad = jnp.zeros((1, width), F32)
    shift_grad = jnp.zeros((1, width), F32)
    outer_grad = jnp.zeros((1, width), F32)
    chunk = 128
    for r in range(0, rows, chunk):
        at = slice(r, r + chunk)
        grad = dn3[at]
        back, rowed = norm_back(after[at], gain[2:3], grad)
        grown = ct[at].astype(F32)
        two[at] = grown + back
        gain_grad += jnp.sum(rowed, axis=0, keepdims=True)
        shift_grad += jnp.sum(grad, axis=0, keepdims=True)
        outer_grad += jnp.sum(grown, axis=0, keepdims=True)
    small_out[...] = jnp.zeros_like(small_out)
    for j in range(gib.shape[1] // width):
        small_out[j:j + 1] = gib[:, j * width:(j + 1) * width]
    small_out[8:9] = gain_grad
    small_out[9:10] = shift_grad
    small_out[10:11] = outer_grad


ANY = pl.BlockSpec(memory_space=pl.ANY)
VM = pl.BlockSpec(memory_space=pltpu.VMEM)
SM = pl.BlockSpec(memory_space=pltpu.SMEM)
V = pltpu.VMEM


def sems(count):
    return pltpu.SemaphoreType.DMA((count,))


def call(kernel, name, outs, in_specs, scratch, args, micros, out_specs=None, after=(), room=60):
    if after:
        args = (lax.optimization_barrier((args[0], *after))[0], *args[1:])
    return pl.pallas_call(
        kernel,
        out_shape=[jax.ShapeDtypeStruct(*o) for o in outs],
        in_specs=in_specs,
        out_specs=out_specs or [VM] * len(outs),
        scratch_shapes=scratch,
        compiler_params=pltpu.CompilerParams(vmem_limit_bytes=room * 2**20),
        cost_estimate=pl.CostEstimate(flops=int(micros * 1e9), bytes_accessed=int(micros * 3e6), transcendentals=0),
        name=name,
    )(*args)


def forward_call(ways, len_, x, xp, src, srcp, ct, gains, shifts, sbias, cbias, ibias, obias, weights):
    rows, width = x.shape
    srows = src.shape[0]
    nk, ns = ways * rows, ways * srows
    ff = weights[5].shape[1]
    rw = (rows, width)
    outs = [
        (((ff, width), BF), ANY), ((rw, F32), VM), ((rw, F32), VM), ((rw, BF), VM), (((width, rows), BF), VM),
        (((1, ff), F32), VM), ((rw, F32), VM),
        (((nk, width), BF), ANY), ((rw, BF), ANY), ((rw, BF), ANY), (((nk, width), BF), ANY), (((nk, width), BF), ANY),
        ((rw, BF), ANY), (((ns, width), BF), ANY), (((ns, width), BF), ANY),
        (((HEADS, nk, rows), BF), ANY), (((HEADS, ns, rows), BF), ANY),
        ((rw, F32), ANY), ((rw, F32), ANY), ((rw, BF), ANY), ((rw, BF), ANY), ((rw, F32), ANY),
    ]
    half = ff // 2
    peer = VM if ways == 2 else ANY
    slots = HEADS if ways == 2 else 2
    scratch = [V(w.shape, BF) for w in weights[:5]] + [V((width, half), BF), V((half, width), BF)] + [
        V(rw, BF), V(rw, BF), V((nk, width), BF), V((nk, width), BF),
        V((rows, PAIR), BF), V((nk, PAIR), BF), V((slots, nk, rows), BF), V(rw, BF), V(rw, F32),
        V(rw, F32), V(rw, BF), V(rw, BF), V((ns, width), BF), V((ns, width), BF), V((ns, PAIR), BF), V((slots, ns, rows), BF),
        V(rw, BF), V(rw, F32),
        V((2, width, width), BF), V((srows, width), BF), V((width, width), BF), V(rw, BF), V((1, ff), F32),
        sems(7), sems(slots), sems(slots), sems(16), sems(2), sems(2),
    ]
    return call(
        functools.partial(forward_kernel, ways), "forward", [o[0] for o in outs],
        [SM, VM, peer, VM, peer, VM] + [VM] * 6 + [ANY] * 7, scratch,
        (len_, x, xp, src, srcp, ct, gains, shifts, sbias, cbias, ibias, obias, *weights), 31, [o[1] for o in outs], room=60,
    )


def feed_call(ct, gains, ibias, n3, n3t, gib, acc, dn3, after, w_f1, w_f2):
    rw = ct.shape
    width = rw[1]
    ff = w_f1.shape[1]
    steps = ff // 2 // width
    return call(
        feed_kernel, "feed", [(rw, BF), ((ff, width), BF), (rw, F32), ((16, width), F32)],
        [VM] * 3 + [ANY] * 8,
        [V((1, ff), F32), V((1, ff), F32), V(rw, BF), V(rw, BF), V(n3t.shape, BF), V(rw, F32), V(rw, F32), V(rw, F32), V((width, ff // 2), BF),
         V((ff // 2, width), BF), V((4, width, width), BF), sems(6 + 2 * steps), sems(4)],
        (gains, ibias, gib, ct, n3, n3t, acc, dn3, after, w_f1, w_f2), 9, [VM, ANY, VM, VM],
    )


def attend_back(first, last, arrive, q_ref, k_ref, v_ref, gm_ref, recip_ref, mixed_ref, p_hbm, p_ref, sem, dq_ref, dk_ref, dv_ref):
    rows = q_ref.shape[0]
    keys = k_ref.shape[0]
    qlane = lax.broadcasted_iota(jnp.int32, (rows, PAIR), 1)
    klane = lax.broadcasted_iota(jnp.int32, (keys, PAIR), 1)

    qrow = lax.broadcasted_iota(jnp.int32, (PAIR, rows), 0)

    def fetch(pair, slot):
        return pltpu.make_async_copy(p_hbm.at[pl.ds(2 * pair, 2)], p_ref.at[slot], sem.at[slot])

    def one(pair, _):
        static = isinstance(pair, int)
        slot = (pair - first) % 2 if static else lax.rem(pair - first, 2)
        if static:
            if pair + 1 < last:
                fetch(pair + 1, 1 - slot).start()
        else:

            @pl.when(pair + 1 < last)
            def _():
                fetch(pair + 1, 1 - slot).start()

        lanes = pl.ds(pair * PAIR if static else pl.multiple_of(pair * PAIR, PAIR), PAIR)
        arrive(pair)
        qp = q_ref[:, lanes]
        kp = k_ref[:, lanes]
        vp = v_ref[:, lanes]
        kpt = kp.T
        dop = (gm_ref[:, lanes].astype(F32) * recip_ref[:, lanes]).astype(BF)
        prod = dop.astype(F32) * mixed_ref[:, lanes].astype(F32)
        fetch(pair, slot).wait()
        dqs, dks, dvs = [], [], []
        for h in (0, 1):
            inside = (qlane < HD) if h == 0 else (qlane >= HD)
            kinside = (klane < HD) if h == 0 else (klane >= HD)
            spare = HD * (1 - h)
            delta = jnp.sum(jnp.where(inside, prod, 0.0), axis=1, keepdims=True)
            high = delta.astype(BF).astype(F32)
            tail = jnp.where(qlane == spare, -high, jnp.where(qlane == spare + 1, high - delta, 0.0))
            doe = jnp.where(inside, dop, tail.astype(BF))
            ones = jnp.where((klane == spare) | (klane == spare + 1), 1.0, 0.0).astype(BF)
            ve = jnp.where(kinside, vp, ones)
            dpt = mm_t(ve, doe)
            p = p_ref[slot, h]
            dst = (p.astype(F32) * dpt).astype(BF)
            dvs.append(mm(p, dop))
            dks.append(mm(dst, qp))
            dqs.append(mm(kpt, dst))
        lanes = pl.ds((pair - first) * PAIR if static else pl.multiple_of((pair - first) * PAIR, PAIR), PAIR)
        dq_ref[:, lanes] = (jnp.where(qrow < HD, dqs[0], dqs[1]) * HD ** -0.5).astype(BF).T
        dk_ref[:, lanes] = jnp.where(klane < HD, dks[0], dks[1]).astype(BF)
        dv_ref[:, lanes] = jnp.where(klane < HD, dvs[0], dvs[1]).astype(BF)
        return 0

    fetch(first, 0).start()
    lax.fori_loop(first, last, one, 0)


def weight_halves(width, me, g, gkeep, gsend, departures, keep_out, send_out):
    half = width // 2
    keep, send = (pl.ds(pl.multiple_of(at * half, half), half) for at in halves_of(me))

    def put(i, value):
        at = slice(i * half, (i + 1) * half)
        g[...] = value.astype(BF)
        gkeep[at] = g[keep]
        gsend[at] = g[send]
        route(departures, gsend, i * half, half, send_out)
        route(departures, gkeep, i * half, half, keep_out)

    return put


def route(departures, ref, first, rows, outs):
    begin = 0
    for out in outs:
        end = begin + out.shape[0]
        low, high = max(first, begin), min(first + rows, end)
        if low < high:
            departures.send(ref.at[pl.ds(low, high - low)], out.at[pl.ds(low - begin, high - low)])
        begin = end


def norm_sums(small, begin, gain_grad, shift_grad):
    small[begin:begin + 1] = gain_grad
    small[begin + 1:begin + 2] = shift_grad


def cross_kernel(
    gain_ref, two_h, q_h, k_h, v_h, p_h, recip_h, mixed_h, one_h, w_cq_h, w_co_h, w_so_h,
    dq_out, dk_out, dv_out, btwo_out, bone_out, gm_out, oneg_out, small_out,
    two, q, k, v, p_buf, recip, mixed, one, w_cq, w_co, w_so, gm, dq, dk, dv, dn, btwo, bone, p_sem, sem, out_sem,
):
    rows, width = two.shape
    arrivals = Arrivals(
        sem, two=(two_h, two), w_co=(w_co_h, w_co), q=(q_h, q), k=(k_h, k), v=(v_h, v), recip=(recip_h, recip),
        mixed=(mixed_h, mixed), w_cq=(w_cq_h, w_cq), one=(one_h, one), w_so=(w_so_h, w_so))
    departures = Departures(out_sem)
    gain = gain_ref[...].astype(F32)
    small_out[...] = jnp.zeros_like(small_out)
    arrivals.need("two", "w_co")
    btwo[...] = two[...].astype(BF)
    departures.send(btwo, btwo_out)
    small_out[0:1] = column_sum(btwo[...])
    gm[...] = mm_t(btwo[...], w_co[...]).astype(BF)
    arrivals.need("q", "k", "v", "recip", "mixed")
    attend_back(0, HEADS // 2, lambda pair: None, q, k, v, gm, recip, mixed, p_h, p_buf, p_sem, dq, dk, dv)
    departures.send(dq, dq_out)
    departures.send(dk, dk_out)
    departures.send(dv, dv_out)
    small_out[1:2] = column_sum(dq[...])
    small_out[5:6] = column_sum(dv[...])
    arrivals.need("w_cq", "one")
    dn[...] = mm_t(dq[...], w_cq[...])
    chunk = 128
    gain_grad = jnp.zeros((1, width), F32)
    shift_grad = jnp.zeros((1, width), F32)
    for r in range(0, rows, chunk):
        at = slice(r, r + chunk)
        grad = dn[at]
        back, rowed = norm_back(one[at], gain[1:2], grad)
        total = two[at] + back
        one[at] = total
        bone[at] = total.astype(BF)
        gain_grad += jnp.sum(rowed, axis=0, keepdims=True)
        shift_grad += jnp.sum(grad, axis=0, keepdims=True)
    departures.send(one, oneg_out)
    departures.send(bone, bone_out)
    norm_sums(small_out, 2, gain_grad, shift_grad)
    small_out[4:5] = column_sum(bone[...])
    arrivals.need("w_so")
    gm[...] = mm_t(bone[...], w_so[...]).astype(BF)
    departures.send(gm, gm_out)
    departures.finish()


def cross_weights_kernel(
    dq_h, dk_h, dv_h, btwo_h, bone_h, src_h, srcp_h, n2_h, cmixed_h, mixed_h, w_ckv_h,
    keep_out, send_one, send_two, send_three, send_four, sgrad_out,
    dq, dk, dv, btwo, bone, src, n2, cmixed, mixed, w_ckv, g, gkeep, gsend, sgrad, sem, out_sem,
):
    rows, width = dq.shape
    srows = src_h.shape[0]
    me = lax.axis_index("seq")
    arrivals = Arrivals(
        sem, cmixed=(cmixed_h, cmixed), btwo=(btwo_h, btwo), n2=(n2_h, n2), dq=(dq_h, dq), mixed=(mixed_h, mixed), bone=(bone_h, bone),
        src=(src_h, src.at[pl.ds(0, srows)]), srcp=(srcp_h, src.at[pl.ds(srows, srcp_h.shape[0])]), dk=(dk_h, dk), dv=(dv_h, dv),
        w_ckv=(w_ckv_h, w_ckv))
    departures = Departures(out_sem)
    put = weight_halves(width, me, g, gkeep, gsend, departures, [keep_out], [send_one, send_two, send_three, send_four])
    for i, (left, right) in enumerate((("cmixed", "btwo"), ("n2", "dq"), ("mixed", "bone"))):
        arrivals.need(left, right)
        put(i, t_mm({"cmixed": cmixed, "n2": n2, "mixed": mixed}[left][...], {"btwo": btwo, "dq": dq, "bone": bone}[right][...]))
    arrivals.need("src", "srcp")
    for i, (name, ref) in enumerate((("dk", dk), ("dv", dv))):
        arrivals.need(name)
        put(3 + i, t_mm(src[...], ref[...]))
    arrivals.need("w_ckv")
    sgrad[...] = (mm_t(dk[...], w_ckv[:, 0:width]) + mm_t(dv[...], w_ckv[:, width:])).astype(BF)
    departures.send(sgrad, sgrad_out)
    departures.finish()


def self_kernel(
    first, last,
    q_h, k_h, v_h, p_h, recip_h, mixed_h, gm_h,
    dq, dk, dv,
    q, k, v, p_buf, recip, mixed, gm, p_sem, pair_sem,
):
    operands = ((q_h, q), (k_h, k), (v_h, v), (gm_h, gm), (recip_h, recip), (mixed_h, mixed))

    def lanes_of(pair):
        lanes = pl.ds(pair * PAIR if isinstance(pair, int) else pl.multiple_of(pair * PAIR, PAIR), PAIR)
        return [
            pltpu.make_async_copy(source.at[:, lanes], target.at[:, lanes], pair_sem.at[i, pair - first])
            for i, (source, target) in enumerate(operands)
        ]

    for pair in range(first, last):
        for copy in lanes_of(pair):
            copy.start()

    def arrive(pair):
        for copy in lanes_of(pair):
            copy.wait()

    attend_back(first, last, arrive, q, k, v, gm, recip, mixed, p_h, p_buf, p_sem, dq, dk, dv)


def self_weights_kernel(
    small1, small2, dq_one, dk_one, dv_one, dq_two, dk_two, dv_two, n1_h, x_h, xp_h, w_h,
    keep_one, keep_two, send_one, send_two, dn_out, dn_peer_out,
    dq, dk, dv, n1, x, w, g, gkeep, gsend, small, dn, dn_peer, sem, out_sem,
):
    rows, width = dq.shape
    nk = dk.shape[0]
    half = width // 2
    me = lax.axis_index("seq")
    begin, end = pl.ds(0, dq_one.shape[1]), pl.ds(dq_one.shape[1], dq_two.shape[1])
    arrivals = Arrivals(
        sem, n1=(n1_h, n1), dq=(dq_one, dq.at[:, begin]), dq2=(dq_two, dq.at[:, end]), dk=(dk_one, dk.at[:, begin]), dk2=(dk_two, dk.at[:, end]),
        dv=(dv_one, dv.at[:, begin]), dv2=(dv_two, dv.at[:, end]), w=(w_h, w),
        xp=(xp_h, x.at[pl.ds(rows, nk - rows)]), x=(x_h, x.at[pl.ds(0, rows)]))
    departures = Departures(out_sem)
    keep_out, send_out = [keep_one, keep_two], [send_one, send_two]
    put = weight_halves(width, me, g, gkeep, gsend, departures, keep_out, send_out)
    arrivals.need("n1", "dq", "dq2")
    put(0, t_mm(n1[0:rows], dq[...]))
    arrivals.need("dk", "dk2")
    put(1, t_mm(n1[...], dk[...]))
    arrivals.need("dv", "dv2")
    put(2, t_mm(n1[...], dv[...]))
    arrivals.need("w", "x", "xp")
    gain_grad = jnp.zeros((1, width), F32)
    shift_grad = jnp.zeros((1, width), F32)
    chunk = 128
    for b in reversed(range(nk // rows)):
        at = slice(b * rows, (b + 1) * rows)
        grad = mm_t(dk[at], w[:, width:2 * width]) + mm_t(dv[at], w[:, 2 * width:])
        if b == 0:
            grad = grad + mm_t(dq[...], w[:, 0:width])
        dn[...] = grad
        if b == 0:
            departures.send(dn, dn_out)
        for r in range(0, rows, chunk):
            piece = dn[r:r + chunk]
            xhat = norm_parts(x[b * rows + r:b * rows + r + chunk].astype(F32))[0]
            gain_grad += jnp.sum(piece * xhat, axis=0, keepdims=True)
            shift_grad += jnp.sum(piece, axis=0, keepdims=True)
        if b > 0:
            dn_peer[(b - 1) * rows:b * rows] = dn[...].astype(BF)
            there = pl.ds((b - 1) * rows, rows)
            departures.send(dn_peer.at[there], dn_peer_out.at[there])
    small[...] = jnp.zeros_like(small)
    norm_sums(small, 0, gain_grad, shift_grad)
    small[2:3] = column_sum(dq[...])
    small[3:4] = column_sum(dv[...])
    small[8:16] = small2[...]
    small[16:32] = small1[...]
    for side, ref, out in zip(halves_of(me), (gkeep, gsend), (keep_out, send_out)):
        ref[3 * half:3 * half + 16] = small[pl.ds(pl.multiple_of(side * 16, 16), 16)].astype(BF)
        ref[3 * half + 16:] = jnp.zeros((16, width), BF)
        route(departures, ref, 3 * half, 32, out)
    departures.finish()


def last_kernel(x_ref, gain_ref, dn_ref, came_ref, oneg_ref, xgrad):
    gain = gain_ref[...].astype(F32)
    chunk = 128
    for r in range(0, x_ref.shape[0], chunk):
        at = slice(r, r + chunk)
        grad = dn_ref[at]
        for b in range(came_ref.shape[0]):
            grad = grad + came_ref[b, at].astype(F32)
        back = norm_back(x_ref[at].astype(F32), gain[0:1], grad)[0]
        xgrad[at] = (oneg_ref[at] + back).astype(BF)


def cross_call(gains, two, q, k, v, p, recip, mixed, one, w_cq, w_co, w_so):
    rows, width = two.shape
    ns = k.shape[0]
    rw, ww, nw = (rows, width), (width, width), (ns, width)
    outs = [(rw, BF), (nw, BF), (nw, BF), (rw, BF), (rw, BF), (rw, BF), (rw, F32), ((8, width), F32)]
    scratch = [V(rw, F32), V(rw, BF), V(nw, BF), V(nw, BF), V((2, 2, ns, rows), BF), V(rw, F32), V(rw, BF), V(rw, F32),
               V(ww, BF), V(ww, BF), V(ww, BF), V(rw, BF), V(rw, BF), V(nw, BF), V(nw, BF), V(rw, F32), V(rw, BF), V(rw, BF),
               sems(2), sems(10), sems(7)]
    return call(cross_kernel, "cross_back", outs, [VM] + [ANY] * 11, scratch,
                (gains, two, q, k, v, p, recip, mixed, one, w_cq, w_co, w_so), 11, [ANY] * 7 + [VM])


def cross_weights_call(dq, dk, dv, btwo, bone, src, srcp, n2, cmixed, mixed, w_ckv):
    rows, width = dq.shape
    rw, ww, nw = (rows, width), (width, width), dk.shape
    half = (5 * width // 2, width)
    scratch = [V(rw, BF), V(nw, BF), V(nw, BF), V(rw, BF), V(rw, BF), V(nw, BF), V(rw, BF), V(rw, BF), V(rw, BF), V((width, 2 * width), BF),
               V(ww, BF), V(half, BF), V(half, BF), V(nw, BF), sems(11), sems(16)]
    part = (half[0] // 4, width)
    return call(cross_weights_kernel, "cross_weights", [(half, BF)] + [(part, BF)] * 4 + [(nw, BF)], [ANY] * 11, scratch,
                (dq, dk, dv, btwo, bone, src, srcp, n2, cmixed, mixed, w_ckv), 6, [ANY] * 6)


def self_call(first, last, name, q, k, v, p, recip, mixed, gm):
    rows, width = q.shape
    nk = k.shape[0]
    rw, nw = (rows, width), (nk, width)
    size = (last - first) * PAIR
    scratch = [V(rw, BF), V(nw, BF), V(nw, BF), V((2, 2, nk, rows), BF), V(rw, F32), V(rw, BF), V(rw, BF),
               sems(2), pltpu.SemaphoreType.DMA((6, last - first))]
    return call(functools.partial(self_kernel, first, last), name, [((rows, size), BF), ((nk, size), BF), ((nk, size), BF)],
                [ANY] * 7, scratch, (q, k, v, p, recip, mixed, gm), 3 * (last - first))


def self_weights_call(small1, small2, grads, n1, x, xp, w):
    rows, width = x.shape
    nk = n1.shape[0]
    rw, nw, pw = (rows, width), (nk, width), (nk - rows, width)
    half = (3 * width // 2 + 32, width)
    part = (half[0] // 2, width)
    scratch = [V(rw, BF), V(nw, BF), V(nw, BF), V(nw, BF), V(nw, BF), V(w.shape, BF), V((width, width), BF), V(half, BF), V(half, BF),
               V((32, width), F32), V(rw, F32), V(pw, BF), sems(10), sems(14 + nk // rows)]
    return call(self_weights_kernel, "self_weights", [(part, BF)] * 4 + [(rw, F32), (pw, BF)], [VM] * 2 + [ANY] * 10, scratch,
                (small1, small2, *grads, n1, x, xp, w), 7, [ANY] * 6)


def last_call(x, gains, dn, came, oneg, after):
    return call(last_kernel, "last_back", [(x.shape, BF)], [VM] * 5, [], (x, gains, dn, came, oneg), 0.2, after=after, room=12)[0]


def feed_plan(ff, width):
    per = ff // width // 2
    moves = []
    for j in range(per):
        moves.append((2 * j * width, width, 0, (0, 0), (j * width, per * width)))
        moves.append(((2 * j + 1) * width, width, 1, (j * width, per * width), (0, 0)))
    return [(width, ff), (ff, width)], moves


def cross_plan(width):
    part = width // 2
    places = ((0, 0), (1, 0), (2, 0), (3, 0), (3, width))
    return [(width, width)] * 3 + [(width, 2 * width)], [
        (i * part, part, out, (0, part), (column, 0)) for i, (out, column) in enumerate(places)]


def last_plan(width):
    part = width // 2
    return [(width, 3 * width)], [(i * part, part, 0, (0, part), (i * width, 0)) for i in range(3)]


def unpack_kernel(moves, finish, count, where, *refs):
    parts = refs[:4]
    outs = refs[4:4 + count]
    more = refs[4 + count:-4]
    full, buf, in_sem, out_sem = refs[-4:]
    size = parts[0].shape[0]
    slots, _, width = buf.shape
    own = where[0]
    loads = []
    for i, part in enumerate(parts):
        side = where[1 + i // 2]
        at = pl.ds(pl.multiple_of((side if i % 2 == 0 else 1 - side) * size, 16), size)
        loads.append(pltpu.make_async_copy(part, full.at[i // 2, at], in_sem.at[i]))
    for load in loads:
        load.start()
    stores = []
    for turn, half in enumerate((own, 1 - own)):
        loads[2 * turn].wait()
        loads[2 * turn + 1].wait()
        for first, rows, out, (row, down), (column, right) in moves:
            slot = len(stores) % slots
            if len(stores) >= slots:
                stores[len(stores) - slots].wait()
            buf[slot, 0:rows] = full[turn, first:first + rows].astype(F32)
            to_rows = pl.ds(pl.multiple_of(row + half * down, 16), rows)
            to_columns = pl.ds(pl.multiple_of(column + half * right, 128), width)
            copy = pltpu.make_async_copy(buf.at[slot, pl.ds(0, rows)], outs[out].at[to_rows, to_columns], out_sem.at[slot])
            copy.start()
            stores.append(copy)
    if finish is not None:
        finish(full, own, more)
    for copy in stores[-slots:]:
        copy.wait()


def finish_small(begin, full, own, outs):
    gains, shifts, sbias, cbias, inner, outer = outs
    rows = slice(begin, begin + 16)
    low = full[own, rows].astype(F32)
    high = full[1 - own, rows].astype(F32)
    width = low.shape[1]
    for i, (g, s, value) in enumerate(((0, 1, low), (10, 11, low), (8, 9, high))):
        gains[i:i + 1] = value[g:g + 1]
        shifts[i:i + 1] = value[s:s + 1]
    for i, (a, b) in enumerate(((2, 9), (3, 13), (12, 8))):
        sbias[i:i + 1] = low[a:a + 1]
        cbias[i:i + 1] = low[b:b + 1]
    for j in range(inner.shape[0] // width):
        inner[j * width:(j + 1) * width] = high[j]
    outer[...] = high[10]


def unpack_call(where, parts, name, plan, micros, finish=None, more=()):
    shapes, moves = plan
    size, width = parts[0].shape
    most = max(move[1] for move in moves)
    slots = min(6, 2 * len(moves))
    scratch = [V((2, 2 * size, width), BF), V((slots, most, width), F32), sems(4), sems(slots)]
    outs = [(shape, F32) for shape in list(shapes) + list(more)]
    return call(functools.partial(unpack_kernel, moves, finish, len(shapes)), name, outs, [SM] + [ANY] * 4, scratch,
                (where, *parts), micros, [ANY] * len(shapes) + [VM] * len(more), room=24)


def ring(value, axis, shift):
    size = lax.axis_size(axis)
    return lax.ppermute(value, axis, [(i, (i + shift) % size) for i in range(size)])


def add(left, right):
    return (left.astype(F32) + right.astype(F32)).astype(BF)


def steps_of():
    rest = [("seq", 1 << b) for b in range(1, lax.axis_size("seq").bit_length() - 1)]
    dp = [("dp", 1 << b) for b in range(lax.axis_size("dp").bit_length() - 1)]
    near, far_off = dp[:2], dp[2:]
    halving = list(zip(near, near[::-1]))
    whole = [(step, step) for step in rest] + list(zip(far_off[::-1], far_off))
    return halving, whole


def flip(value, step):
    ways = lax.axis_size("seq")
    pairs = []
    for i in range(lax.axis_size("dp")):
        for s in range(ways):
            axis, bit = step[s % 2]
            to = (i ^ bit) * ways + s if axis == "dp" else i * ways + (s ^ bit)
            pairs.append((i * ways + s, to))
    return lax.ppermute(value, ("dp", "seq"), pairs)


def flip_core(value):
    return flip(value, (("seq", 1), ("seq", 1)))


def side_of(step):
    sides = [lax.axis_index(axis) // bit % 2 for axis, bit in step]
    return jnp.where(lax.axis_index("seq") % 2 == 0, sides[0], sides[1])


def scatter_step(mine, came, step):
    side = side_of(step)
    half = mine.shape[0] // 2

    def take(value, at):
        return lax.dynamic_index_in_dim(value.reshape(2, half, value.shape[1]), at, 0, keepdims=False)

    send = add(take(mine, 1 - side), take(came, 1 - side))
    return add(take(mine, side), take(came, side)), send, flip(send, step)


def scatter_quarters(mine, came, step):
    side = side_of(step)
    half = mine.shape[0] // 2

    def take(at):
        kept = lax.dynamic_index_in_dim(mine.reshape(2, half, mine.shape[1]), at, 0, keepdims=False)
        return add(kept, jnp.where(at == 0, jnp.concatenate(came[:2]), jnp.concatenate(came[2:4])))

    send = take(1 - side)
    return take(side), send, flip(send, step)


def scatter_pair(mine, came, step):
    side = side_of(step)

    def take(pair, at):
        return jnp.where(at == 0, pair[0], pair[1])

    send = add(take(mine, 1 - side), take(came, 1 - side))
    return add(take(mine, side), take(came, side)), send, flip(send, step)


def joined(mine, came, step):
    return jnp.where(side_of(step) == 0, jnp.concatenate([mine, came]), jnp.concatenate([came, mine]))


def places(step):
    parity = lax.axis_index("seq") % 2
    sides = [lax.axis_index(axis) // bit % 2 for axis, bit in step]
    own = jnp.where(parity == 0, sides[0], sides[1])
    other = jnp.where(parity == 0, sides[1], sides[0])
    return jnp.stack([parity, own, other]).astype(jnp.int32)


def tie(value, *others):
    return lax.optimization_barrier((value, *others))[0]


def local(
    layer_input, source_states, source_lengths, cotangent, norm_gain, norm_bias, self_in, self_bias, self_out,
    cross_query, cross_keyval, cross_bias, cross_out, feed_in, inner_bias, feed_out, outer_bias,
):
    ways = lax.axis_size("seq")
    x = layer_input[0]
    source = source_states[0]
    ct = cotangent[0]
    rows, width = x.shape
    srows = source.shape[0]
    xp = jnp.concatenate([ring(x, "seq", -b) for b in range(1, ways)])
    srcp = jnp.concatenate([ring(source, "seq", -b) for b in range(1, ways)])
    (gsend, acc, dn3, n3, n3t, gib, after, n1, n2, q, k, v, cq, ck, cv, p, cp, recip, crecip, mixed, cmixed, one) = forward_call(
        ways, source_lengths, x, xp, source, srcp, ct, norm_gain, norm_bias, self_bias, cross_bias,
        inner_bias, outer_bias,
        (self_in, self_out, cross_query, cross_keyval, cross_out, feed_in, feed_out),
    )
    halving, whole = steps_of()
    first, second = halving
    feed_came = flip_core(gsend)
    y, gkeep, two, small1 = feed_call(ct, norm_gain, inner_bias, n3, n3t, gib, acc, dn3, after, feed_in, feed_out)
    feed, feed_sent, feed_came = scatter_step(gkeep, tie(feed_came, two), first)
    cdq, cdk, cdv, btwo, bone, gm, oneg, small2 = cross_call(
        norm_gain, tie(two, feed_sent), cq, ck, cv, cp, crecip, cmixed, one, cross_query, cross_out, self_out)
    feed, feed_sent, feed_came = scatter_step(feed, tie(feed_came, gm), second)
    ckeep, *csend, sgrad = cross_weights_call(
        tie(cdq, feed_sent), cdk, cdv, btwo, bone, source, srcp, n2, cmixed, mixed, cross_keyval)
    cross_came = [flip_core(quarter) for quarter in csend]
    feed = add(feed, tie(feed_came, ckeep))
    feed_came = flip(feed, whole[0])
    cross, cross_sent, cross_came = scatter_quarters(ckeep, lax.optimization_barrier((*cross_came, feed)), first)
    part = 3 * HEADS // 8
    grads = self_call(0, part, "self_back_one", q, k, v, p, recip, mixed, tie(gm, feed, cross_sent))
    feed = add(feed, tie(feed_came, grads[0]))
    for step in whole[1:-1]:
        feed = add(feed, flip(feed, step))
    feed_came = flip(feed, whole[-1])
    cross, cross_sent, cross_came = scatter_step(cross, tie(cross_came, feed), second)
    more = self_call(part, HEADS // 2, "self_back_two", q, k, v, p, recip, mixed, tie(gm, feed, cross_sent))
    cross = add(cross, tie(cross_came, more[0]))
    cross_came = flip(cross, whole[0])
    *lasts, dn, dn_peer = self_weights_call(
        small1, small2, (*grads, tie(more[0], cross), *more[1:]), n1, x, xp, self_in)
    last_came = [flip_core(half) for half in lasts[2:]]
    dn_came = jnp.stack([ring(dn_peer[(b - 1) * rows:b * rows], "seq", b) for b in range(1, ways)])
    for b in range(1, ways):
        sgrad_came = ring(sgrad[b * srows:(b + 1) * srows], "seq", b).astype(F32)
        total = sgrad_came if b == 1 else total + sgrad_came
    sgrad = (sgrad[:srows].astype(F32) + total).astype(BF)
    feed = add(feed, tie(feed_came, dn))
    feed_came = flip(feed, second)
    cross = add(cross, tie(cross_came, feed))
    for step in whole[1:-1]:
        cross = add(cross, flip(cross, step))
    cross_came = flip(cross, whole[-1])
    last, last_sent, last_came = scatter_pair(lasts[:2], lax.optimization_barrier((*last_came, cross)), first)
    last, last_sent, last_came = scatter_step(last, last_came, second)
    feed = joined(feed, tie(feed_came, last_sent), second)
    feed_came = flip(feed, first)
    feed_other = flip_core(feed)
    last = add(last, tie(last_came, feed))
    last_came = flip(last, whole[0])
    cross = add(cross, tie(cross_came, last))
    cross_came = flip(cross, second)
    last = add(last, tie(last_came, cross))
    for step in whole[1:-1]:
        last = add(last, flip(last, step))
    last_came = flip(last, whole[-1])
    cross = joined(cross, tie(cross_came, last), second)
    cross_came = flip(cross, first)
    cross_other = flip_core(cross)
    last = add(last, tie(last_came, cross))
    last_came = flip(last, second)
    feed_came = tie(feed_came, last)
    feed_last = flip_core(feed_came)
    where = places(first)
    xgrad = last_call(x, norm_gain, dn, dn_came, oneg, (feed_came,))
    g_feed_in, g_feed_out = unpack_call(
        where, (feed, feed_came, feed_other, tie(feed_last, xgrad)), "feed_unpack", feed_plan(feed_in.shape[1], width), 5)
    last = joined(last, tie(last_came, g_feed_in), second)
    last_came = flip(last, first)
    last_other = flip_core(last)
    cross_came = tie(cross_came, last)
    cross_last = flip_core(cross_came)
    g_cross_out, g_cross_query, g_self_out, g_keyval = unpack_call(
        where, (cross, cross_came, cross_other, cross_last), "cross_unpack", cross_plan(width), 0.2)
    last_last = flip_core(tie(last_came, g_keyval))
    g_self_in, *small = unpack_call(
        where, (last, last_came, last_other, last_last), "last_unpack", last_plan(width), 0.2,
        functools.partial(finish_small, 3 * width // 2), [(3, width)] * 4 + [inner_bias.shape, outer_bias.shape])
    g_gain, g_shift, g_self_bias, g_cross_bias, g_inner, g_outer = small
    return (
        y[None], xgrad[None], sgrad[None], g_gain, g_shift, g_self_in, g_self_bias, g_self_out, g_cross_query, g_keyval, g_cross_bias,
        g_cross_out, g_feed_in, g_inner, g_feed_out, g_outer,
    )


def solution(mesh):
    split = P("dp", "seq", None)
    in_specs = (split, split, P("dp", None), split) + (P(),) * 13
    out_specs = (split,) * 3 + (P(),) * 13
    return jax.shard_map(local, mesh=mesh, in_specs=in_specs, out_specs=out_specs, check_vma=False)
```

```python
import functools
import jax
import jax.numpy as jnp
from jax import lax
from jax.experimental import pallas as pl
from jax.experimental.pallas import tpu as pltpu
from jax.sharding import PartitionSpec as P

HEADS = 8
HD = 64
PAIR = 2 * HD
eps = 1e-05
far = -1e30
BF = jnp.bfloat16
F32 = jnp.float32


def mm(left, right):
    return lax.dot_general(left, right, (((1,), (0,)), ((), ())), preferred_element_type=F32)


def mm_t(left, right):
    return lax.dot_general(left, right, (((1,), (1,)), ((), ())), preferred_element_type=F32)


def t_mm(left, right):
    return lax.dot_general(left, right, (((0,), (0,)), ((), ())), preferred_element_type=F32)


def norm_parts(values):
    center = values - jnp.mean(values, axis=-1, keepdims=True)
    spread = jnp.mean(center * center, axis=-1, keepdims=True)
    rate = lax.rsqrt(spread + eps)
    return center * rate, rate


def norm_rows(values, gain, shift):
    return norm_parts(values)[0] * gain + shift


def norm_back(values, gain, grad):
    xhat, rate = norm_parts(values)
    e = grad * gain
    back = rate * (
        e - jnp.mean(e, axis=-1, keepdims=True) - xhat * jnp.mean(e * xhat, axis=-1, keepdims=True)
    )
    return back, grad * xhat


def sentence_lanes(lengths, factor, shape):
    lane = lax.broadcasted_iota(jnp.int32, shape, 1) % HD
    begin = jnp.zeros(shape, jnp.int32)
    end = jnp.zeros(shape, jnp.int32)
    total = jnp.int32(0)
    for n in range(lengths.shape[1]):
        after = total + factor * lengths[0, n]
        begin = jnp.where(lane == n, total, begin)
        end = jnp.where(lane == n, after, end)
        total = after
    return begin, end


def sentence_hits(lengths, factor, first, rows):
    begin, end = sentence_lanes(lengths, factor, (1, PAIR))
    place = lax.broadcasted_iota(jnp.int32, (rows, PAIR), 0) + first
    return jnp.where((place >= begin) & (place < end), 1.0, 0.0)


def sentence_far(lengths, hits):
    lane = lax.broadcasted_iota(jnp.int32, hits.shape, 1) % HD
    return jnp.where(lane < lengths.shape[1], (1.0 - hits) * far, 0.0)


def gelu_parts(v):
    c = 0.7978845608028654
    square = v * v
    t = jnp.tanh(c * (v + 0.044715 * (square * v)))
    half = 0.5 * (1.0 + t)
    slope = half + (0.5 * v) * (1.0 - t * t) * (c * (1.0 + 3 * 0.044715 * square))
    return v * half, slope


def swap_heads(width):
    row = lax.broadcasted_iota(jnp.int32, (width, width), 0) // HD
    column = lax.broadcasted_iota(jnp.int32, (width, width), 1) // HD
    return jnp.where((row != column) & (row // 2 == column // 2), 1.0, 0.0).astype(BF)


def score_bound(q_ref, k_ref, swap_ref, lift_ref):
    most = jnp.max(jnp.abs(k_ref[...]).astype(F32), axis=0, keepdims=True)
    size = (jnp.abs(q_ref[...]).astype(F32) * most).astype(BF)
    lift_ref[...] = (-1.02 * mm(size, swap_ref[...])).astype(BF)


def attend(q_ref, k_ref, v_ref, qfar_ref, khit_ref, lift_ref, p_ref, p_out, sem, mixed_ref, recip_ref):
    rows = q_ref.shape[0]
    keys = k_ref.shape[0]
    slots = p_ref.shape[0]
    qlane = lax.broadcasted_iota(jnp.int32, (rows, PAIR), 1) < HD
    klane = lax.broadcasted_iota(jnp.int32, (keys, PAIR), 1) < HD
    vrow = lax.broadcasted_iota(jnp.int32, (PAIR, keys), 0) < HD
    orow = lax.broadcasted_iota(jnp.int32, (PAIR, rows), 0) < HD

    def copy(n, slot):
        return pltpu.make_async_copy(p_ref.at[slot], p_out.at[n], sem.at[slot])

    def one(pair, exact, reuse):
        lanes = pl.ds(pair * PAIR if isinstance(pair, int) else pl.multiple_of(pair * PAIR, PAIR), PAIR)
        qp = q_ref[:, lanes]
        kp = k_ref[:, lanes]
        vpt = v_ref[:, lanes].T
        rest = qfar_ref[...] if exact else qfar_ref[...] + lift_ref[:, lanes]
        outs = []
        for h in (0, 1):
            qe = jnp.where(qlane if h == 0 else ~qlane, qp, rest)
            ke = jnp.where(klane if h == 0 else ~klane, kp, khit_ref[...])
            st = mm_t(ke, qe)
            if exact:
                st = st - jnp.max(st, axis=0, keepdims=True)
            p = jnp.exp(st).astype(BF)
            n = 2 * pair + h
            slot = n if slots == HEADS else h
            if reuse is not None:
                pl.when(reuse)(lambda n=n, slot=slot: copy(n, slot).wait())
            p_ref[slot] = p
            copy(n, slot).start()
            ve = jnp.where(vrow if h == 0 else ~vrow, vpt, jnp.ones_like(vpt))
            outs.append(mm(ve, p))
        value = jnp.where(orow, outs[0], outs[1])
        total = jnp.where(orow, outs[1], outs[0])
        recip = 1.0 / pltpu.roll(total, HD, 0)
        mixed_ref[:, lanes] = (value * recip).astype(BF).T
        recip_ref[:, lanes] = recip.T
        return jnp.min(total.reshape(PAIR // 8, 8, rows), axis=0)

    least = lax.fori_loop(
        0, HEADS // 2, lambda pair, low: jnp.minimum(low, one(pair, False, None if slots == HEADS else pair > 0)),
        jnp.full((8, rows), 1.0, F32))

    @pl.when(jnp.logical_not(jnp.min(least) > 1e-18))
    def _():
        for slot in range(slots):
            copy(slot, slot).wait()

        def again(pair, _):
            one(pair, True, pair > 0 if slots < HEADS else None)
            return 0

        lax.fori_loop(0, HEADS // 2, again, 0)


def drain(p_ref, p_out, sem):
    for slot in range(p_ref.shape[0]):
        pltpu.make_async_copy(p_ref.at[slot], p_out.at[slot], sem.at[slot]).wait()


def feed_half(half, ready, ct_ref, w1, w2, ibias_ref, n3, n3t, acc, dn3, gib, gbuf, gout, g_sem):
    width = n3.shape[1]
    steps = w2.shape[0] // width
    begun = []
    for j in range(steps):
        at = slice(j * width, (j + 1) * width)
        wide = pl.ds(pl.multiple_of((half * steps + j) * width, width), width)
        ready("w1", j)
        hidden = mm(n3[...], w1[:, at]) + ibias_ref[:, wide]
        acted, slope = gelu_parts(hidden)
        acted = acted.astype(BF)
        ready("w2", j)
        gh = (mm_t(ct_ref[...], w2[at]) * slope).astype(BF)
        gib[:, wide] = column_sum(gh)
        ready("n3t", j)
        for i, product in enumerate((lambda: mm(n3t[...], gh), lambda: t_mm(acted, ct_ref[...]))):
            slot = (2 * j + i) % gbuf.shape[0]
            if len(begun) >= gbuf.shape[0]:
                begun[len(begun) - gbuf.shape[0]].wait()
            gbuf[slot] = product().astype(BF)
            copy = pltpu.make_async_copy(gbuf.at[slot], gout.at[pl.ds((2 * j + i) * width, width)], g_sem.at[slot])
            copy.start()
            begun.append(copy)
        ready("acc", j)
        acc[...] += mm(acted, w2[at])
        ready("dn3", j)
        dn3[...] += mm_t(gh, w1[:, at])
    for copy in begun[-gbuf.shape[0]:]:
        copy.wait()


def column_sum(block):
    return jnp.sum(block.astype(F32), axis=0, keepdims=True)


def start_all(pairs, sem):
    copies = [pltpu.make_async_copy(a, b, sem.at[i]) for i, (a, b) in enumerate(pairs)]
    for copy in copies:
        copy.start()
    return copies


def halves_of(me):
    return lax.rem(me, 2), 1 - lax.rem(me, 2)


def columns(ref, half):
    size = ref.shape[1] // 2
    return ref.at[:, pl.ds(pl.multiple_of(half * size, size), size)]


def rows_of(ref, half):
    size = ref.shape[0] // 2
    return ref.at[pl.ds(pl.multiple_of(half * size, size), size)]


def forward_kernel(
    ways,
    len_ref, x_ref, xp_ref, src_ref, srcp_ref, ct_ref,
    gain_ref, shift_ref, sbias_ref, cbias_ref, ibias_ref, obias_ref,
    w_in_h, w_so_h, w_cq_h, w_ckv_h, w_co_h, w_f1_h, w_f2_h,
    gsend_out, acc, dn3, n3, n3t, gib, after, n1_out, n2_out, q_out, k_out, v_out, cq_out, ck_out, cv_out,
    p_out, cp_out, recip_out, crecip_out, mixed_out, cmixed_out, one_out,
    w_in, w_so, w_cq, w_ckv, w_co, w_f1, w_f2,
    n1, q, k, v, qfar, khit, p_buf, mixed, recip, one, n2, cq, ck, cv, shit, cp_buf, cmixed, crecip,
    gbuf, srcb, swap, lift, ibias, w_sem, p_sem, cp_sem, o_sem, g_sem, x_sem,
):
    rows, width = x_ref.shape
    me = lax.axis_index("seq")
    other = halves_of(me)[1]
    weights = [
        (w_in_h, w_in), (w_so_h, w_so), (w_cq_h, w_cq), (w_ckv_h, w_ckv), (w_co_h, w_co),
        (columns(w_f1_h, other), w_f1), (rows_of(w_f2_h, other), w_f2),
    ]
    loads = [pltpu.make_async_copy(a, b, w_sem.at[i]) for i, (a, b) in enumerate(weights)]
    src_rows = src_ref.shape[0]

    def peers(b):
        return (
            pltpu.make_async_copy(xp_ref.at[pl.ds((b - 1) * rows, rows)], n3, x_sem.at[0]),
            pltpu.make_async_copy(srcp_ref.at[pl.ds((b - 1) * src_rows, src_rows)], srcb, x_sem.at[1]),
        )

    loads[0].start()
    for load in peers(1):
        load.start()
    for load in loads[1:]:
        load.start()
    ibias[...] = ibias_ref[...].astype(F32).reshape(ibias.shape)
    gain = gain_ref[...].astype(F32)
    shift = shift_ref[...].astype(F32)
    sbias = sbias_ref[...].astype(F32)
    cbias = cbias_ref[...].astype(F32)
    stores = []

    def store(src, dst):
        copy = pltpu.make_async_copy(src, dst, o_sem.at[len(stores)])
        copy.start()
        stores.append(copy)

    chunk = 128
    for r in range(0, rows, chunk):
        n1[r:r + chunk] = norm_rows(x_ref[r:r + chunk].astype(F32), gain[0:1], shift[0:1]).astype(BF)
    store(n1, n1_out.at[0:rows])
    for b in range(ways):
        at = lax.rem(me + b, ways)
        khit[b * rows:(b + 1) * rows] = sentence_hits(len_ref, 2, at * rows, rows).astype(BF)
        shit[b * src_rows:(b + 1) * src_rows] = sentence_hits(len_ref, 1, at * src_rows, src_rows).astype(BF)
    qfar[...] = sentence_far(len_ref, khit[0:rows].astype(F32)).astype(BF)

    loads[0].wait()
    q[...] = ((mm(n1[...], w_in[:, 0:width]) + sbias[0:1]) * HD ** -0.5).astype(BF)
    for b in range(ways):
        at = slice(b * rows, (b + 1) * rows)
        rowed = n1
        if b > 0:
            rowed = n3
            peers(b)[0].wait()
            for r in range(0, rows, chunk):
                block = n3[r:r + chunk].astype(F32)
                n3[r:r + chunk] = norm_rows(block, gain[0:1], shift[0:1]).astype(BF)
            nsave = pltpu.make_async_copy(n3, n1_out.at[at], x_sem.at[0])
            nsave.start()
        k[at] = mm(rowed[...], w_in[:, width:2 * width]).astype(BF)
        v[at] = (mm(rowed[...], w_in[:, 2 * width:]) + sbias[1:2]).astype(BF)
        if b > 0:
            nsave.wait()
        if 0 < b < ways - 1:
            peers(b + 1)[0].start()
    store(q, q_out)
    store(k, k_out)
    store(v, v_out)
    swap[...] = swap_heads(width)
    score_bound(q, k, swap, lift)
    attend(q, k, v, qfar, khit, lift, p_buf, p_out, p_sem, mixed, recip)
    store(recip, recip_out)
    store(mixed, mixed_out)

    loads[1].wait()
    one[...] = x_ref[...].astype(F32) + mm(mixed[...], w_so[...]) + sbias[2:3]
    for r in range(0, rows, chunk):
        n2[r:r + chunk] = norm_rows(one[r:r + chunk], gain[1:2], shift[1:2]).astype(BF)
    store(one, one_out)
    store(n2, n2_out)
    loads[2].wait()
    cq[...] = ((mm(n2[...], w_cq[...]) + cbias[0:1]) * HD ** -0.5).astype(BF)
    loads[3].wait()
    for b in range(ways):
        if b > 0:
            peers(b)[1].wait()
        source = src_ref[...] if b == 0 else srcb[...]
        at = slice(b * src_rows, (b + 1) * src_rows)
        ck[at] = mm(source, w_ckv[:, 0:width]).astype(BF)
        cv[at] = (mm(source, w_ckv[:, width:]) + cbias[1:2]).astype(BF)
        if 0 < b < ways - 1:
            peers(b + 1)[1].start()
    store(cq, cq_out)
    store(ck, ck_out)
    store(cv, cv_out)
    score_bound(cq, ck, swap, lift)
    attend(cq, ck, cv, qfar, shit, lift, cp_buf, cp_out, cp_sem, cmixed, crecip)
    store(crecip, crecip_out)
    store(cmixed, cmixed_out)

    loads[4].wait()
    after[...] = one[...] + mm(cmixed[...], w_co[...]) + cbias[2:3]
    for r in range(0, rows, chunk):
        n3[r:r + chunk] = norm_rows(after[r:r + chunk], gain[2:3], shift[2:3]).astype(BF)
    n3t[...] = n3[...].T
    acc[...] = after[...] + obias_ref[...].astype(F32).reshape(1, width)
    dn3[...] = jnp.zeros_like(dn3)
    gib[...] = jnp.zeros_like(gib)
    loads[5].wait()
    loads[6].wait()
    feed_half(other, lambda name, step: None, ct_ref, w_f1, w_f2, ibias, n3, n3t, acc, dn3, gib, gbuf, gsend_out, g_sem)
    drain(p_buf, p_out, p_sem)
    drain(cp_buf, cp_out, cp_sem)
    for copy in stores:
        copy.wait()


class Arrivals:
    def __init__(self, sem, **pairs):
        self.copies = {}
        for i, (name, (source, target)) in enumerate(pairs.items()):
            self.copies[name] = pltpu.make_async_copy(source, target, sem.at[i])
            self.copies[name].start()

    def need(self, *names):
        for name in names:
            if name in self.copies:
                self.copies.pop(name).wait()


class Departures:
    def __init__(self, sem):
        self.sem = sem
        self.copies = []

    def send(self, source, target):
        copy = pltpu.make_async_copy(source, target, self.sem.at[len(self.copies)])
        copy.start()
        self.copies.append(copy)

    def finish(self):
        for copy in self.copies:
            copy.wait()


def feed_kernel(
    gain_ref, ibias_ref, gib_ref, ct_h, n3_h, n3t_h, acc_h, dn3_h, after_h, w_f1_h, w_f2_h,
    y_ref, gkeep_out, two, small_out,
    gib, ibias, ct, n3, n3t, acc, dn3, after, w_f1, w_f2, gbuf, sem, g_sem,
):
    rows, width = ct.shape
    mine = halves_of(lax.axis_index("seq"))[0]
    steps = w_f2.shape[0] // width
    pairs = {"n3": (n3_h, n3)}
    w1, w2 = columns(w_f1_h, mine), rows_of(w_f2_h, mine)
    for j in range(steps):
        at = pl.ds(j * width, width)
        pairs["w1%d" % j] = (w1.at[:, at], w_f1.at[:, at])
        if j == 0:
            pairs["ct"] = (ct_h, ct)
        pairs["w2%d" % j] = (w2.at[at], w_f2.at[at])
        if j == 0:
            pairs.update(n3t=(n3t_h, n3t), acc=(acc_h, acc), dn3=(dn3_h, dn3))
    pairs["after"] = (after_h, after)
    arrivals = Arrivals(sem, **pairs)
    gain = gain_ref[...].astype(F32)
    gib[...] = gib_ref[...]
    ibias[...] = ibias_ref[...].astype(F32).reshape(ibias.shape)

    def ready(name, j):
        if name == "w1":
            arrivals.need("n3", "w1%d" % j)
        elif name == "w2":
            arrivals.need("ct", "w2%d" % j)
        else:
            arrivals.need(name)

    feed_half(mine, ready, ct, w_f1, w_f2, ibias, n3, n3t, acc, dn3, gib, gbuf, gkeep_out, g_sem)
    y_ref[...] = acc[...].astype(BF)
    arrivals.need("after")
    gain_grad = jnp.zeros((1, width), F32)
    shift_grad = jnp.zeros((1, width), F32)
    outer_grad = jnp.zeros((1, width), F32)
    chunk = 128
    for r in range(0, rows, chunk):
        at = slice(r, r + chunk)
        grad = dn3[at]
        back, rowed = norm_back(after[at], gain[2:3], grad)
        grown = ct[at].astype(F32)
        two[at] = grown + back
        gain_grad += jnp.sum(rowed, axis=0, keepdims=True)
        shift_grad += jnp.sum(grad, axis=0, keepdims=True)
        outer_grad += jnp.sum(grown, axis=0, keepdims=True)
    small_out[...] = jnp.zeros_like(small_out)
    for j in range(gib.shape[1] // width):
        small_out[j:j + 1] = gib[:, j * width:(j + 1) * width]
    small_out[8:9] = gain_grad
    small_out[9:10] = shift_grad
    small_out[10:11] = outer_grad


ANY = pl.BlockSpec(memory_space=pl.ANY)
VM = pl.BlockSpec(memory_space=pltpu.VMEM)
SM = pl.BlockSpec(memory_space=pltpu.SMEM)
V = pltpu.VMEM


def sems(count):
    return pltpu.SemaphoreType.DMA((count,))


def call(kernel, name, outs, in_specs, scratch, args, micros, out_specs=None, after=(), room=60):
    if after:
        args = (lax.optimization_barrier((args[0], *after))[0], *args[1:])
    return pl.pallas_call(
        kernel,
        out_shape=[jax.ShapeDtypeStruct(*o) for o in outs],
        in_specs=in_specs,
        out_specs=out_specs or [VM] * len(outs),
        scratch_shapes=scratch,
        compiler_params=pltpu.CompilerParams(vmem_limit_bytes=room * 2**20),
        cost_estimate=pl.CostEstimate(flops=int(micros * 1e9), bytes_accessed=int(micros * 3e6), transcendentals=0),
        name=name,
    )(*args)


def forward_call(ways, len_, x, xp, src, srcp, ct, gains, shifts, sbias, cbias, ibias, obias, weights):
    rows, width = x.shape
    srows = src.shape[0]
    nk, ns = ways * rows, ways * srows
    ff = weights[5].shape[1]
    rw = (rows, width)
    outs = [
        (((ff, width), BF), ANY), ((rw, F32), VM), ((rw, F32), VM), ((rw, BF), VM), (((width, rows), BF), VM),
        (((1, ff), F32), VM), ((rw, F32), VM),
        (((nk, width), BF), ANY), ((rw, BF), ANY), ((rw, BF), ANY), (((nk, width), BF), ANY), (((nk, width), BF), ANY),
        ((rw, BF), ANY), (((ns, width), BF), ANY), (((ns, width), BF), ANY),
        (((HEADS, nk, rows), BF), ANY), (((HEADS, ns, rows), BF), ANY),
        ((rw, F32), ANY), ((rw, F32), ANY), ((rw, BF), ANY), ((rw, BF), ANY), ((rw, F32), ANY),
    ]
    half = ff // 2
    peer = VM if ways == 2 else ANY
    slots = HEADS if ways == 2 else 2
    scratch = [V(w.shape, BF) for w in weights[:5]] + [V((width, half), BF), V((half, width), BF)] + [
        V(rw, BF), V(rw, BF), V((nk, width), BF), V((nk, width), BF),
        V((rows, PAIR), BF), V((nk, PAIR), BF), V((slots, nk, rows), BF), V(rw, BF), V(rw, F32),
        V(rw, F32), V(rw, BF), V(rw, BF), V((ns, width), BF), V((ns, width), BF), V((ns, PAIR), BF), V((slots, ns, rows), BF),
        V(rw, BF), V(rw, F32),
        V((2, width, width), BF), V((srows, width), BF), V((width, width), BF), V(rw, BF), V((1, ff), F32),
        sems(7), sems(slots), sems(slots), sems(16), sems(2), sems(2),
    ]
    return call(
        functools.partial(forward_kernel, ways), "forward", [o[0] for o in outs],
        [SM, VM, peer, VM, peer, VM] + [VM] * 6 + [ANY] * 7, scratch,
        (len_, x, xp, src, srcp, ct, gains, shifts, sbias, cbias, ibias, obias, *weights), 31, [o[1] for o in outs], room=60,
    )


def feed_call(ct, gains, ibias, n3, n3t, gib, acc, dn3, after, w_f1, w_f2):
    rw = ct.shape
    width = rw[1]
    ff = w_f1.shape[1]
    steps = ff // 2 // width
    return call(
        feed_kernel, "feed", [(rw, BF), ((ff, width), BF), (rw, F32), ((16, width), F32)],
        [VM] * 3 + [ANY] * 8,
        [V((1, ff), F32), V((1, ff), F32), V(rw, BF), V(rw, BF), V(n3t.shape, BF), V(rw, F32), V(rw, F32), V(rw, F32), V((width, ff // 2), BF),
         V((ff // 2, width), BF), V((4, width, width), BF), sems(6 + 2 * steps), sems(4)],
        (gains, ibias, gib, ct, n3, n3t, acc, dn3, after, w_f1, w_f2), 9, [VM, ANY, VM, VM],
    )


def attend_back(first, last, arrive, q_ref, k_ref, v_ref, gm_ref, recip_ref, mixed_ref, p_hbm, p_ref, sem, dq_ref, dk_ref, dv_ref):
    rows = q_ref.shape[0]
    keys = k_ref.shape[0]
    qlane = lax.broadcasted_iota(jnp.int32, (rows, PAIR), 1)
    klane = lax.broadcasted_iota(jnp.int32, (keys, PAIR), 1)

    qrow = lax.broadcasted_iota(jnp.int32, (PAIR, rows), 0)

    def fetch(pair, slot):
        return pltpu.make_async_copy(p_hbm.at[pl.ds(2 * pair, 2)], p_ref.at[slot], sem.at[slot])

    def one(pair, _):
        static = isinstance(pair, int)
        slot = (pair - first) % 2 if static else lax.rem(pair - first, 2)
        if static:
            if pair + 1 < last:
                fetch(pair + 1, 1 - slot).start()
        else:

            @pl.when(pair + 1 < last)
            def _():
                fetch(pair + 1, 1 - slot).start()

        lanes = pl.ds(pair * PAIR if static else pl.multiple_of(pair * PAIR, PAIR), PAIR)
        arrive(pair)
        qp = q_ref[:, lanes]
        kp = k_ref[:, lanes]
        vp = v_ref[:, lanes]
        kpt = kp.T
        dop = (gm_ref[:, lanes].astype(F32) * recip_ref[:, lanes]).astype(BF)
        prod = dop.astype(F32) * mixed_ref[:, lanes].astype(F32)
        fetch(pair, slot).wait()
        dqs, dks, dvs = [], [], []
        for h in (0, 1):
            inside = (qlane < HD) if h == 0 else (qlane >= HD)
            kinside = (klane < HD) if h == 0 else (klane >= HD)
            spare = HD * (1 - h)
            delta = jnp.sum(jnp.where(inside, prod, 0.0), axis=1, keepdims=True)
            high = delta.astype(BF).astype(F32)
            tail = jnp.where(qlane == spare, -high, jnp.where(qlane == spare + 1, high - delta, 0.0))
            doe = jnp.where(inside, dop, tail.astype(BF))
            ones = jnp.where((klane == spare) | (klane == spare + 1), 1.0, 0.0).astype(BF)
            ve = jnp.where(kinside, vp, ones)
            dpt = mm_t(ve, doe)
            p = p_ref[slot, h]
            dst = (p.astype(F32) * dpt).astype(BF)
            dvs.append(mm(p, dop))
            dks.append(mm(dst, qp))
            dqs.append(mm(kpt, dst))
        lanes = pl.ds((pair - first) * PAIR if static else pl.multiple_of((pair - first) * PAIR, PAIR), PAIR)
        dq_ref[:, lanes] = (jnp.where(qrow < HD, dqs[0], dqs[1]) * HD ** -0.5).astype(BF).T
        dk_ref[:, lanes] = jnp.where(klane < HD, dks[0], dks[1]).astype(BF)
        dv_ref[:, lanes] = jnp.where(klane < HD, dvs[0], dvs[1]).astype(BF)
        return 0

    fetch(first, 0).start()
    lax.fori_loop(first, last, one, 0)


def weight_halves(width, me, g, gkeep, gsend, departures, keep_out, send_out):
    half = width // 2
    keep, send = (pl.ds(pl.multiple_of(at * half, half), half) for at in halves_of(me))

    def put(i, value):
        at = slice(i * half, (i + 1) * half)
        g[...] = value.astype(BF)
        gkeep[at] = g[keep]
        gsend[at] = g[send]
        route(departures, gsend, i * half, half, send_out)
        route(departures, gkeep, i * half, half, keep_out)

    return put


def route(departures, ref, first, rows, outs):
    begin = 0
    for out in outs:
        end = begin + out.shape[0]
        low, high = max(first, begin), min(first + rows, end)
        if low < high:
            departures.send(ref.at[pl.ds(low, high - low)], out.at[pl.ds(low - begin, high - low)])
        begin = end


def norm_sums(small, begin, gain_grad, shift_grad):
    small[begin:begin + 1] = gain_grad
    small[begin + 1:begin + 2] = shift_grad


def cross_kernel(
    gain_ref, two_h, q_h, k_h, v_h, p_h, recip_h, mixed_h, one_h, w_cq_h, w_co_h, w_so_h,
    dq_out, dk_out, dv_out, btwo_out, bone_out, gm_out, oneg_out, small_out,
    two, q, k, v, p_buf, recip, mixed, one, w_cq, w_co, w_so, gm, dq, dk, dv, dn, btwo, bone, p_sem, sem, out_sem,
):
    rows, width = two.shape
    arrivals = Arrivals(
        sem, two=(two_h, two), w_co=(w_co_h, w_co), q=(q_h, q), k=(k_h, k), v=(v_h, v), recip=(recip_h, recip),
        mixed=(mixed_h, mixed), w_cq=(w_cq_h, w_cq), one=(one_h, one), w_so=(w_so_h, w_so))
    departures = Departures(out_sem)
    gain = gain_ref[...].astype(F32)
    small_out[...] = jnp.zeros_like(small_out)
    arrivals.need("two", "w_co")
    btwo[...] = two[...].astype(BF)
    departures.send(btwo, btwo_out)
    small_out[0:1] = column_sum(btwo[...])
    gm[...] = mm_t(btwo[...], w_co[...]).astype(BF)
    arrivals.need("q", "k", "v", "recip", "mixed")
    attend_back(0, HEADS // 2, lambda pair: None, q, k, v, gm, recip, mixed, p_h, p_buf, p_sem, dq, dk, dv)
    departures.send(dq, dq_out)
    departures.send(dk, dk_out)
    departures.send(dv, dv_out)
    small_out[1:2] = column_sum(dq[...])
    small_out[5:6] = column_sum(dv[...])
    arrivals.need("w_cq", "one")
    dn[...] = mm_t(dq[...], w_cq[...])
    chunk = 128
    gain_grad = jnp.zeros((1, width), F32)
    shift_grad = jnp.zeros((1, width), F32)
    for r in range(0, rows, chunk):
        at = slice(r, r + chunk)
        grad = dn[at]
        back, rowed = norm_back(one[at], gain[1:2], grad)
        total = two[at] + back
        one[at] = total
        bone[at] = total.astype(BF)
        gain_grad += jnp.sum(rowed, axis=0, keepdims=True)
        shift_grad += jnp.sum(grad, axis=0, keepdims=True)
    departures.send(one, oneg_out)
    departures.send(bone, bone_out)
    norm_sums(small_out, 2, gain_grad, shift_grad)
    small_out[4:5] = column_sum(bone[...])
    arrivals.need("w_so")
    gm[...] = mm_t(bone[...], w_so[...]).astype(BF)
    departures.send(gm, gm_out)
    departures.finish()


def cross_weights_kernel(
    dq_h, dk_h, dv_h, btwo_h, bone_h, src_h, srcp_h, n2_h, cmixed_h, mixed_h, w_ckv_h,
    keep_out, send_one, send_two, send_three, send_four, sgrad_out,
    dq, dk, dv, btwo, bone, src, n2, cmixed, mixed, w_ckv, g, gkeep, gsend, sgrad, sem, out_sem,
):
    rows, width = dq.shape
    srows = src_h.shape[0]
    me = lax.axis_index("seq")
    arrivals = Arrivals(
        sem, cmixed=(cmixed_h, cmixed), btwo=(btwo_h, btwo), n2=(n2_h, n2), dq=(dq_h, dq), mixed=(mixed_h, mixed), bone=(bone_h, bone),
        src=(src_h, src.at[pl.ds(0, srows)]), srcp=(srcp_h, src.at[pl.ds(srows, srcp_h.shape[0])]), dk=(dk_h, dk), dv=(dv_h, dv),
        w_ckv=(w_ckv_h, w_ckv))
    departures = Departures(out_sem)
    put = weight_halves(width, me, g, gkeep, gsend, departures, [keep_out], [send_one, send_two, send_three, send_four])
    for i, (left, right) in enumerate((("cmixed", "btwo"), ("n2", "dq"), ("mixed", "bone"))):
        arrivals.need(left, right)
        put(i, t_mm({"cmixed": cmixed, "n2": n2, "mixed": mixed}[left][...], {"btwo": btwo, "dq": dq, "bone": bone}[right][...]))
    arrivals.need("src", "srcp")
    for i, (name, ref) in enumerate((("dk", dk), ("dv", dv))):
        arrivals.need(name)
        put(3 + i, t_mm(src[...], ref[...]))
    arrivals.need("w_ckv")
    sgrad[...] = (mm_t(dk[...], w_ckv[:, 0:width]) + mm_t(dv[...], w_ckv[:, width:])).astype(BF)
    departures.send(sgrad, sgrad_out)
    departures.finish()


def self_kernel(
    first, last,
    q_h, k_h, v_h, p_h, recip_h, mixed_h, gm_h,
    dq, dk, dv,
    q, k, v, p_buf, recip, mixed, gm, p_sem, pair_sem,
):
    operands = ((q_h, q), (k_h, k), (v_h, v), (gm_h, gm), (recip_h, recip), (mixed_h, mixed))

    def lanes_of(pair):
        lanes = pl.ds(pair * PAIR if isinstance(pair, int) else pl.multiple_of(pair * PAIR, PAIR), PAIR)
        return [
            pltpu.make_async_copy(source.at[:, lanes], target.at[:, lanes], pair_sem.at[i, pair - first])
            for i, (source, target) in enumerate(operands)
        ]

    for pair in range(first, last):
        for copy in lanes_of(pair):
            copy.start()

    def arrive(pair):
        for copy in lanes_of(pair):
            copy.wait()

    attend_back(first, last, arrive, q, k, v, gm, recip, mixed, p_h, p_buf, p_sem, dq, dk, dv)


def self_weights_kernel(
    small1, small2, dq_one, dk_one, dv_one, dq_two, dk_two, dv_two, n1_h, x_h, xp_h, w_h,
    keep_one, keep_two, send_one, send_two, dn_out, dn_peer_out,
    dq, dk, dv, n1, x, w, g, gkeep, gsend, small, dn, dn_peer, sem, out_sem,
):
    rows, width = dq.shape
    nk = dk.shape[0]
    half = width // 2
    me = lax.axis_index("seq")
    begin, end = pl.ds(0, dq_one.shape[1]), pl.ds(dq_one.shape[1], dq_two.shape[1])
    arrivals = Arrivals(
        sem, n1=(n1_h, n1), dq=(dq_one, dq.at[:, begin]), dq2=(dq_two, dq.at[:, end]), dk=(dk_one, dk.at[:, begin]), dk2=(dk_two, dk.at[:, end]),
        dv=(dv_one, dv.at[:, begin]), dv2=(dv_two, dv.at[:, end]), w=(w_h, w),
        xp=(xp_h, x.at[pl.ds(rows, nk - rows)]), x=(x_h, x.at[pl.ds(0, rows)]))
    departures = Departures(out_sem)
    keep_out, send_out = [keep_one, keep_two], [send_one, send_two]
    put = weight_halves(width, me, g, gkeep, gsend, departures, keep_out, send_out)
    arrivals.need("n1", "dq", "dq2")
    put(0, t_mm(n1[0:rows], dq[...]))
    arrivals.need("dk", "dk2")
    put(1, t_mm(n1[...], dk[...]))
    arrivals.need("dv", "dv2")
    put(2, t_mm(n1[...], dv[...]))
    arrivals.need("w", "x", "xp")
    gain_grad = jnp.zeros((1, width), F32)
    shift_grad = jnp.zeros((1, width), F32)
    chunk = 128
    for b in reversed(range(nk // rows)):
        at = slice(b * rows, (b + 1) * rows)
        grad = mm_t(dk[at], w[:, width:2 * width]) + mm_t(dv[at], w[:, 2 * width:])
        if b == 0:
            grad = grad + mm_t(dq[...], w[:, 0:width])
        dn[...] = grad
        if b == 0:
            departures.send(dn, dn_out)
        for r in range(0, rows, chunk):
            piece = dn[r:r + chunk]
            xhat = norm_parts(x[b * rows + r:b * rows + r + chunk].astype(F32))[0]
            gain_grad += jnp.sum(piece * xhat, axis=0, keepdims=True)
            shift_grad += jnp.sum(piece, axis=0, keepdims=True)
        if b > 0:
            dn_peer[(b - 1) * rows:b * rows] = dn[...].astype(BF)
            there = pl.ds((b - 1) * rows, rows)
            departures.send(dn_peer.at[there], dn_peer_out.at[there])
    small[...] = jnp.zeros_like(small)
    norm_sums(small, 0, gain_grad, shift_grad)
    small[2:3] = column_sum(dq[...])
    small[3:4] = column_sum(dv[...])
    small[8:16] = small2[...]
    small[16:32] = small1[...]
    for side, ref, out in zip(halves_of(me), (gkeep, gsend), (keep_out, send_out)):
        ref[3 * half:3 * half + 16] = small[pl.ds(pl.multiple_of(side * 16, 16), 16)].astype(BF)
        ref[3 * half + 16:] = jnp.zeros((16, width), BF)
        route(departures, ref, 3 * half, 32, out)
    departures.finish()


def last_kernel(x_ref, gain_ref, dn_ref, came_ref, oneg_ref, xgrad):
    gain = gain_ref[...].astype(F32)
    chunk = 128
    for r in range(0, x_ref.shape[0], chunk):
        at = slice(r, r + chunk)
        grad = dn_ref[at]
        for b in range(came_ref.shape[0]):
            grad = grad + came_ref[b, at].astype(F32)
        back = norm_back(x_ref[at].astype(F32), gain[0:1], grad)[0]
        xgrad[at] = (oneg_ref[at] + back).astype(BF)


def cross_call(gains, two, q, k, v, p, recip, mixed, one, w_cq, w_co, w_so):
    rows, width = two.shape
    ns = k.shape[0]
    rw, ww, nw = (rows, width), (width, width), (ns, width)
    outs = [(rw, BF), (nw, BF), (nw, BF), (rw, BF), (rw, BF), (rw, BF), (rw, F32), ((8, width), F32)]
    scratch = [V(rw, F32), V(rw, BF), V(nw, BF), V(nw, BF), V((2, 2, ns, rows), BF), V(rw, F32), V(rw, BF), V(rw, F32),
               V(ww, BF), V(ww, BF), V(ww, BF), V(rw, BF), V(rw, BF), V(nw, BF), V(nw, BF), V(rw, F32), V(rw, BF), V(rw, BF),
               sems(2), sems(10), sems(7)]
    return call(cross_kernel, "cross_back", outs, [VM] + [ANY] * 11, scratch,
                (gains, two, q, k, v, p, recip, mixed, one, w_cq, w_co, w_so), 11, [ANY] * 7 + [VM])


def cross_weights_call(dq, dk, dv, btwo, bone, src, srcp, n2, cmixed, mixed, w_ckv):
    rows, width = dq.shape
    rw, ww, nw = (rows, width), (width, width), dk.shape
    half = (5 * width // 2, width)
    scratch = [V(rw, BF), V(nw, BF), V(nw, BF), V(rw, BF), V(rw, BF), V(nw, BF), V(rw, BF), V(rw, BF), V(rw, BF), V((width, 2 * width), BF),
               V(ww, BF), V(half, BF), V(half, BF), V(nw, BF), sems(11), sems(16)]
    part = (half[0] // 4, width)
    return call(cross_weights_kernel, "cross_weights", [(half, BF)] + [(part, BF)] * 4 + [(nw, BF)], [ANY] * 11, scratch,
                (dq, dk, dv, btwo, bone, src, srcp, n2, cmixed, mixed, w_ckv), 6, [ANY] * 6)


def self_call(first, last, name, q, k, v, p, recip, mixed, gm):
    rows, width = q.shape
    nk = k.shape[0]
    rw, nw = (rows, width), (nk, width)
    size = (last - first) * PAIR
    scratch = [V(rw, BF), V(nw, BF), V(nw, BF), V((2, 2, nk, rows), BF), V(rw, F32), V(rw, BF), V(rw, BF),
               sems(2), pltpu.SemaphoreType.DMA((6, last - first))]
    return call(functools.partial(self_kernel, first, last), name, [((rows, size), BF), ((nk, size), BF), ((nk, size), BF)],
                [ANY] * 7, scratch, (q, k, v, p, recip, mixed, gm), 3 * (last - first))


def self_weights_call(small1, small2, grads, n1, x, xp, w):
    rows, width = x.shape
    nk = n1.shape[0]
    rw, nw, pw = (rows, width), (nk, width), (nk - rows, width)
    half = (3 * width // 2 + 32, width)
    part = (half[0] // 2, width)
    scratch = [V(rw, BF), V(nw, BF), V(nw, BF), V(nw, BF), V(nw, BF), V(w.shape, BF), V((width, width), BF), V(half, BF), V(half, BF),
               V((32, width), F32), V(rw, F32), V(pw, BF), sems(10), sems(14 + nk // rows)]
    return call(self_weights_kernel, "self_weights", [(part, BF)] * 4 + [(rw, F32), (pw, BF)], [VM] * 2 + [ANY] * 10, scratch,
                (small1, small2, *grads, n1, x, xp, w), 7, [ANY] * 6)


def last_call(x, gains, dn, came, oneg, after):
    return call(last_kernel, "last_back", [(x.shape, BF)], [VM] * 5, [], (x, gains, dn, came, oneg), 0.2, after=after, room=12)[0]


def feed_plan(ff, width):
    per = ff // width // 2
    moves = []
    for j in range(per):
        moves.append((2 * j * width, width, 0, (0, 0), (j * width, per * width)))
        moves.append(((2 * j + 1) * width, width, 1, (j * width, per * width), (0, 0)))
    return [(width, ff), (ff, width)], moves


def cross_plan(width):
    part = width // 2
    places = ((0, 0), (1, 0), (2, 0), (3, 0), (3, width))
    return [(width, width)] * 3 + [(width, 2 * width)], [
        (i * part, part, out, (0, part), (column, 0)) for i, (out, column) in enumerate(places)]


def last_plan(width):
    part = width // 2
    return [(width, 3 * width)], [(i * part, part, 0, (0, part), (i * width, 0)) for i in range(3)]


def unpack_kernel(moves, finish, count, where, *refs):
    parts = refs[:4]
    outs = refs[4:4 + count]
    more = refs[4 + count:-4]
    full, buf, in_sem, out_sem = refs[-4:]
    size = parts[0].shape[0]
    slots, _, width = buf.shape
    own = where[0]
    loads = []
    for i, part in enumerate(parts):
        side = where[1 + i // 2]
        at = pl.ds(pl.multiple_of((side if i % 2 == 0 else 1 - side) * size, 16), size)
        loads.append(pltpu.make_async_copy(part, full.at[i // 2, at], in_sem.at[i]))
    for load in loads:
        load.start()
    stores = []
    for turn, half in enumerate((own, 1 - own)):
        loads[2 * turn].wait()
        loads[2 * turn + 1].wait()
        for first, rows, out, (row, down), (column, right) in moves:
            slot = len(stores) % slots
            if len(stores) >= slots:
                stores[len(stores) - slots].wait()
            buf[slot, 0:rows] = full[turn, first:first + rows].astype(F32)
            to_rows = pl.ds(pl.multiple_of(row + half * down, 16), rows)
            to_columns = pl.ds(pl.multiple_of(column + half * right, 128), width)
            copy = pltpu.make_async_copy(buf.at[slot, pl.ds(0, rows)], outs[out].at[to_rows, to_columns], out_sem.at[slot])
            copy.start()
            stores.append(copy)
    if finish is not None:
        finish(full, own, more)
    for copy in stores[-slots:]:
        copy.wait()


def finish_small(begin, full, own, outs):
    gains, shifts, sbias, cbias, inner, outer = outs
    rows = slice(begin, begin + 16)
    low = full[own, rows].astype(F32)
    high = full[1 - own, rows].astype(F32)
    width = low.shape[1]
    for i, (g, s, value) in enumerate(((0, 1, low), (10, 11, low), (8, 9, high))):
        gains[i:i + 1] = value[g:g + 1]
        shifts[i:i + 1] = value[s:s + 1]
    for i, (a, b) in enumerate(((2, 9), (3, 13), (12, 8))):
        sbias[i:i + 1] = low[a:a + 1]
        cbias[i:i + 1] = low[b:b + 1]
    for j in range(inner.shape[0] // width):
        inner[j * width:(j + 1) * width] = high[j]
    outer[...] = high[10]


def unpack_call(where, parts, name, plan, micros, finish=None, more=()):
    shapes, moves = plan
    size, width = parts[0].shape
    most = max(move[1] for move in moves)
    slots = min(6, 2 * len(moves))
    scratch = [V((2, 2 * size, width), BF), V((slots, most, width), F32), sems(4), sems(slots)]
    outs = [(shape, F32) for shape in list(shapes) + list(more)]
    return call(functools.partial(unpack_kernel, moves, finish, len(shapes)), name, outs, [SM] + [ANY] * 4, scratch,
                (where, *parts), micros, [ANY] * len(shapes) + [VM] * len(more), room=24)


def ring(value, axis, shift):
    size = lax.axis_size(axis)
    return lax.ppermute(value, axis, [(i, (i + shift) % size) for i in range(size)])


def add(left, right):
    return (left.astype(F32) + right.astype(F32)).astype(BF)


def steps_of():
    rest = [("seq", 1 << b) for b in range(1, lax.axis_size("seq").bit_length() - 1)]
    dp = [("dp", 1 << b) for b in range(lax.axis_size("dp").bit_length() - 1)]
    near, far_off = dp[:2], dp[2:]
    halving = list(zip(near, near[::-1]))
    whole = [(step, step) for step in rest] + list(zip(far_off[::-1], far_off))
    return halving, whole


def flip(value, step):
    ways = lax.axis_size("seq")
    pairs = []
    for i in range(lax.axis_size("dp")):
        for s in range(ways):
            axis, bit = step[s % 2]
            to = (i ^ bit) * ways + s if axis == "dp" else i * ways + (s ^ bit)
            pairs.append((i * ways + s, to))
    return lax.ppermute(value, ("dp", "seq"), pairs)


def flip_core(value):
    return flip(value, (("seq", 1), ("seq", 1)))


def side_of(step):
    sides = [lax.axis_index(axis) // bit % 2 for axis, bit in step]
    return jnp.where(lax.axis_index("seq") % 2 == 0, sides[0], sides[1])


def scatter_step(mine, came, step):
    side = side_of(step)
    half = mine.shape[0] // 2

    def take(value, at):
        return lax.dynamic_index_in_dim(value.reshape(2, half, value.shape[1]), at, 0, keepdims=False)

    send = add(take(mine, 1 - side), take(came, 1 - side))
    return add(take(mine, side), take(came, side)), send, flip(send, step)


def scatter_quarters(mine, came, step):
    side = side_of(step)
    half = mine.shape[0] // 2

    def take(at):
        kept = lax.dynamic_index_in_dim(mine.reshape(2, half, mine.shape[1]), at, 0, keepdims=False)
        return add(kept, jnp.where(at == 0, jnp.concatenate(came[:2]), jnp.concatenate(came[2:4])))

    send = take(1 - side)
    return take(side), send, flip(send, step)


def scatter_pair(mine, came, step):
    side = side_of(step)

    def take(pair, at):
        return jnp.where(at == 0, pair[0], pair[1])

    send = add(take(mine, 1 - side), take(came, 1 - side))
    return add(take(mine, side), take(came, side)), send, flip(send, step)


def joined(mine, came, step):
    return jnp.where(side_of(step) == 0, jnp.concatenate([mine, came]), jnp.concatenate([came, mine]))


def places(step):
    parity = lax.axis_index("seq") % 2
    sides = [lax.axis_index(axis) // bit % 2 for axis, bit in step]
    own = jnp.where(parity == 0, sides[0], sides[1])
    other = jnp.where(parity == 0, sides[1], sides[0])
    return jnp.stack([parity, own, other]).astype(jnp.int32)


def tie(value, *others):
    return lax.optimization_barrier((value, *others))[0]


def local(
    layer_input, source_states, source_lengths, cotangent, norm_gain, norm_bias, self_in, self_bias, self_out,
    cross_query, cross_keyval, cross_bias, cross_out, feed_in, inner_bias, feed_out, outer_bias,
):
    ways = lax.axis_size("seq")
    x = layer_input[0]
    source = source_states[0]
    ct = cotangent[0]
    rows, width = x.shape
    srows = source.shape[0]
    xp = jnp.concatenate([ring(x, "seq", -b) for b in range(1, ways)])
    srcp = jnp.concatenate([ring(source, "seq", -b) for b in range(1, ways)])
    (gsend, acc, dn3, n3, n3t, gib, after, n1, n2, q, k, v, cq, ck, cv, p, cp, recip, crecip, mixed, cmixed, one) = forward_call(
        ways, source_lengths, x, xp, source, srcp, ct, norm_gain, norm_bias, self_bias, cross_bias,
        inner_bias, outer_bias,
        (self_in, self_out, cross_query, cross_keyval, cross_out, feed_in, feed_out),
    )
    halving, whole = steps_of()
    first, second = halving
    feed_came = flip_core(gsend)
    y, gkeep, two, small1 = feed_call(ct, norm_gain, inner_bias, n3, n3t, gib, acc, dn3, after, feed_in, feed_out)
    feed, feed_sent, feed_came = scatter_step(gkeep, tie(feed_came, two), first)
    cdq, cdk, cdv, btwo, bone, gm, oneg, small2 = cross_call(
        norm_gain, tie(two, feed_sent), cq, ck, cv, cp, crecip, cmixed, one, cross_query, cross_out, self_out)
    feed, feed_sent, feed_came = scatter_step(feed, tie(feed_came, gm), second)
    ckeep, *csend, sgrad = cross_weights_call(
        tie(cdq, feed_sent), cdk, cdv, btwo, bone, source, srcp, n2, cmixed, mixed, cross_keyval)
    cross_came = [flip_core(quarter) for quarter in csend]
    feed = add(feed, tie(feed_came, ckeep))
    feed_came = flip(feed, whole[0])
    cross, cross_sent, cross_came = scatter_quarters(ckeep, lax.optimization_barrier((*cross_came, feed)), first)
    part = 3 * HEADS // 8
    grads = self_call(0, part, "self_back_one", q, k, v, p, recip, mixed, tie(gm, feed, cross_sent))
    feed = add(feed, tie(feed_came, grads[0]))
    for step in whole[1:-1]:
        feed = add(feed, flip(feed, step))
    feed_came = flip(feed, whole[-1])
    cross, cross_sent, cross_came = scatter_step(cross, tie(cross_came, feed), second)
    more = self_call(part, HEADS // 2, "self_back_two", q, k, v, p, recip, mixed, tie(gm, feed, cross_sent))
    cross = add(cross, tie(cross_came, more[0]))
    cross_came = flip(cross, whole[0])
    *lasts, dn, dn_peer = self_weights_call(
        small1, small2, (*grads, tie(more[0], cross), *more[1:]), n1, x, xp, self_in)
    last_came = [flip_core(half) for half in lasts[2:]]
    dn_came = jnp.stack([ring(dn_peer[(b - 1) * rows:b * rows], "seq", b) for b in range(1, ways)])
    for b in range(1, ways):
        sgrad_came = ring(sgrad[b * srows:(b + 1) * srows], "seq", b).astype(F32)
        total = sgrad_came if b == 1 else total + sgrad_came
    sgrad = (sgrad[:srows].astype(F32) + total).astype(BF)
    cross = add(cross, tie(cross_came, dn))
    feed = add(feed, tie(feed_came, cross))
    feed_came = flip(feed, second)
    for step in whole[1:-1]:
        cross = add(cross, flip(cross, step))
    cross_came = flip(cross, whole[-1])
    last, last_sent, last_came = scatter_pair(lasts[:2], lax.optimization_barrier((*last_came, feed)), second)
    last, last_sent, last_came = scatter_step(last, last_came, first)
    feed = joined(feed, tie(feed_came, last_sent), second)
    feed_came = flip(feed, first)
    feed_other = flip_core(feed)
    last = add(last, tie(last_came, feed))
    last_came = flip(last, whole[0])
    cross = add(cross, tie(cross_came, last))
    cross_came = flip(cross, second)
    last = add(last, tie(last_came, cross))
    for step in whole[1:-1]:
        last = add(last, flip(last, step))
    last_came = flip(last, whole[-1])
    cross = joined(cross, tie(cross_came, last), second)
    cross_came = flip(cross, first)
    cross_other = flip_core(cross)
    last = add(last, tie(last_came, cross))
    last_came = flip(last, first)
    feed_came = tie(feed_came, last)
    feed_last = flip_core(feed_came)
    where = places(first)
    xgrad = last_call(x, norm_gain, dn, dn_came, oneg, (feed_came,))
    g_feed_in, g_feed_out = unpack_call(
        where, (feed, feed_came, feed_other, tie(feed_last, xgrad)), "feed_unpack", feed_plan(feed_in.shape[1], width), 5)
    last = joined(last, tie(last_came, g_feed_in), first)
    last_came = flip(last, second)
    last_other = flip_core(last)
    cross_came = tie(cross_came, last)
    cross_last = flip_core(cross_came)
    g_cross_out, g_cross_query, g_self_out, g_keyval = unpack_call(
        where, (cross, cross_came, cross_other, cross_last), "cross_unpack", cross_plan(width), 0.2)
    last_last = flip_core(tie(last_came, g_keyval))
    g_self_in, *small = unpack_call(
        places(second), (last, last_came, last_other, last_last), "last_unpack", last_plan(width), 0.2,
        functools.partial(finish_small, 3 * width // 2), [(3, width)] * 4 + [inner_bias.shape, outer_bias.shape])
    g_gain, g_shift, g_self_bias, g_cross_bias, g_inner, g_outer = small
    return (
        y[None], xgrad[None], sgrad[None], g_gain, g_shift, g_self_in, g_self_bias, g_self_out, g_cross_query, g_keyval, g_cross_bias,
        g_cross_out, g_feed_in, g_inner, g_feed_out, g_outer,
    )


def solution(mesh):
    split = P("dp", "seq", None)
    in_specs = (split, split, P("dp", None), split) + (P(),) * 13
    out_specs = (split,) * 3 + (P(),) * 13
    return jax.shard_map(local, mesh=mesh, in_specs=in_specs, out_specs=out_specs, check_vma=False)
```
